32 devices in a mesh: section: 4 (over y, x), dp: 8 (over z, core).
Axes of the slice: x: 2, y: 2, z: 4, core: 2. Of those that a mesh axis runs over, the one named last changes fastest.
Arguments:
- small_images: bfloat16 [2, 8, 196, 768], P(None, 'dp'), may hold values from -6 to 6
- large_images: bfloat16 [2, 8, 576, 768], P(None, 'dp'), may hold values from -6 to 6
- small_upstream: bfloat16 [2, 8, 196, 768], P(None, 'dp'), may hold values from -6 to 6
- large_upstream: bfloat16 [2, 8, 576, 768], P(None, 'dp'), may hold values from -6 to 6
- small_keep: int32 [4, 2, 8, 2], P('section', None, 'dp'), may hold values 0 or 1
- large_keep: int32 [4, 2, 8, 2], P('section', None, 'dp'), may hold values 0 or 1
- small_in: bfloat16 [4, 196, 384], P('section'), may hold values from -0.4375 to 0.4375
- small_bias: float32 [4, 384], P('section'), may hold values from -1.5 to 1.5
- small_out: bfloat16 [4, 384, 196], P('section'), may hold values from -0.3125 to 0.3125
- small_shift: float32 [4, 196], P('section'), may hold values from -1.5 to 1.5
- large_in: bfloat16 [4, 576, 384], P('section'), may hold values from -0.25 to 0.25
- large_bias: float32 [4, 384], P('section'), may hold values from -1.5 to 1.5
- large_out: bfloat16 [4, 384, 576], P('section'), may hold values from -0.3125 to 0.3125
- large_shift: float32 [4, 576], P('section'), may hold values from -1.5 to 1.5
- channel_in: bfloat16 [4, 768, 3072], P('section'), may hold values from -0.21875 to 0.21875
- channel_bias: float32 [4, 3072], P('section'), may hold values from -1.5 to 1.5
- channel_out: bfloat16 [4, 3072, 768], P('section'), may hold values from -0.109375 to 0.109375
- channel_shift: float32 [4, 768], P('section'), may hold values from -1.5 to 1.5
- norm_gain: float32 [4, 2, 768], P('section'), may hold values from 0.5 to 1.5
- norm_shift: float32 [4, 2, 768], P('section'), may hold values from -1.5 to 1.5
Outputs:
- small_outputs: bfloat16 [4, 2, 8, 196, 768], P('section', None, 'dp')
- large_outputs: bfloat16 [4, 2, 8, 576, 768], P('section', None, 'dp')
- small_backward: bfloat16 [4, 2, 8, 196, 768], P('section', None, 'dp')
- large_backward: bfloat16 [4, 2, 8, 576, 768], P('section', None, 'dp')
- small_in_grad: float32 [4, 196, 384], P('section', None, 'dp')
- small_bias_grad: float32 [4, 384], P('section')
- small_out_grad: float32 [4, 384, 196], P('section', 'dp')
- small_shift_grad: float32 [4, 196], P('section')
- large_in_grad: float32 [4, 576, 384], P('section', None, 'dp')
- large_bias_grad: float32 [4, 384], P('section')
- large_out_grad: float32 [4, 384, 576], P('section', 'dp')
- large_shift_grad: float32 [4, 576], P('section')
- channel_in_grad: float32 [4, 768, 3072], P('section', 'dp')
- channel_bias_grad: float32 [4, 3072], P('section')
- channel_out_grad: float32 [4, 3072, 768], P('section', None, 'dp')
- channel_shift_grad: float32 [4, 768], P('section')
- norm_gain_grad: float32 [4, 2, 768], P('section')
- norm_shift_grad: float32 [4, 2, 768], P('section')
The draws below stay inside these ranges and needn't reach their ends.
All inputs are finite; a program needn't handle non-finite values. No bound on the sum of `small_keep` or of `large_keep` on one device may be relied on, other than what follows from the above.
Results may differ from the reference program's by a relative error of at most 0.017.
Values may be sent and summed in bfloat16 or wider, within the bound.
A program may use at most 192 MiB of HBM per device.

```python
import jax
import jax.numpy as jnp
from jax import lax

D = 768
DS = 384
DC = 3072
PS = 196
PL = 576
MICRO = 2
LAYERS = 4
IMGS_S = 8
IMGS_L = 8


def touch_ends(entries, own_key, smallest, largest):
    place = [jax.random.randint(jax.random.fold_in(own_key, axis), (), 0, length) for axis, length in enumerate(entries.shape)]
    main_axis = entries.shape.index(max(entries.shape))
    next_to = place[:main_axis] + [(place[main_axis] + 1) % entries.shape[main_axis]] + place[main_axis + 1:]
    return entries.at[tuple(place)].set(smallest).at[tuple(next_to)].set(largest)


def strengthened(result, own_key, source, target, shards_of, factor):
    owner, partner = [(jnp.arange(result.shape[axis_at]) // (result.shape[axis_at] // shards_of)).reshape([-1 if axis == axis_at else 1 for axis in range(result.ndim)]) for axis_at in (source, target)]
    chosen = jax.random.permutation(own_key, shards_of)[partner]
    strong = (owner == chosen) | (owner == (partner + shards_of // 2) % shards_of)
    return jnp.where(strong, factor * result, result)


def level_of(stream_key, shape, shards, low, largest):
    level, own = 1.0, jax.random.fold_in(stream_key, 6)
    for axis_at, shards_of in shards:
        draws = jnp.exp(jax.random.uniform(jax.random.fold_in(own, axis_at), (shards_of,), jnp.float32, low / len(shards), largest / len(shards)))
        level = level * jnp.repeat(draws, shape[axis_at] // shards_of).reshape([-1 if axis == axis_at else 1 for axis in range(len(shape))])
    return level


def scatter_about(stream_key, shape, scale, most, cuts=(), dtype=jnp.bfloat16):
    result = jax.random.normal(stream_key, shape, jnp.float32) * scale
    if len(cuts) > 0:
        result = level_of(stream_key, shape, cuts, -0.22, 0.18) * result
    return jnp.clip(result, min=-most, max=most).astype(dtype)


def bell_draw_with(stream_key, extent, scale, most, split, heavy, held_as=jnp.bfloat16):
    result = scale * jax.random.normal(stream_key, extent, jnp.float32)
    if split:
        result = result * level_of(stream_key, extent, split, -0.22, 0.18)
    return jnp.clip(strengthened(result, jax.random.fold_in(stream_key, 3), *heavy), -most, most).astype(held_as)


def setup_inputs(seed: int = 0) -> dict:
    key_of = jax.random.split(jax.random.key(seed), 21)
    return {
        "small_images": scatter_about(key_of[0], (MICRO, IMGS_S, PS, D), 1.0, 6.0, ((1, 8),)),
        "large_images": scatter_about(key_of[1], (MICRO, IMGS_L, PL, D), 1.0, 6.0, ((1, 8),)),
        "small_upstream": bell_draw_with(key_of[2], (MICRO, IMGS_S, PS, D), 1.0, 6.0, ((1, 8),), (1, 3, 8, 2.0)),
        "large_upstream": bell_draw_with(key_of[3], (MICRO, IMGS_L, PL, D), 1.0, 6.0, ((1, 8),), (1, 3, 8, 2.0)),
        "small_keep": touch_ends((jax.random.randint(key_of[4], (LAYERS, MICRO, IMGS_S, 2), 0, 4) < 3).astype(jnp.int32), jax.random.fold_in(key_of[4], 1), 0, 1),
        "large_keep": touch_ends((jax.random.randint(key_of[5], (LAYERS, MICRO, IMGS_L, 2), 0, 4) < 3).astype(jnp.int32), jax.random.fold_in(key_of[5], 1), 0, 1),
        "small_in": scatter_about(key_of[6], (LAYERS, PS, DS), PS ** -0.5, 0.4375, ((0, 4),)),
        "small_bias": scatter_about(key_of[7], (LAYERS, DS), 0.3, 1.5, ((0, 4),), jnp.float32),
        "small_out": scatter_about(key_of[8], (LAYERS, DS, PS), DS ** -0.5, 0.3125, ((0, 4),)),
        "small_shift": scatter_about(key_of[9], (LAYERS, PS), 0.3, 1.5, ((0, 4),), jnp.float32),
        "large_in": scatter_about(key_of[10], (LAYERS, PL, DS), PL ** -0.5, 0.25, ((0, 4),)),
        "large_bias": scatter_about(key_of[11], (LAYERS, DS), 0.3, 1.5, ((0, 4),), jnp.float32),
        "large_out": scatter_about(key_of[12], (LAYERS, DS, PL), DS ** -0.5, 0.3125, ((0, 4),)),
        "large_shift": scatter_about(key_of[13], (LAYERS, PL), 0.3, 1.5, ((0, 4),), jnp.float32),
        "channel_in": scatter_about(key_of[14], (LAYERS, D, DC), D ** -0.5, 0.21875, ((0, 4),)),
        "channel_bias": scatter_about(key_of[15], (LAYERS, DC), 0.3, 1.5, ((0, 4),), jnp.float32),
        "channel_out": scatter_about(key_of[16], (LAYERS, DC, D), DC ** -0.5, 0.109375, ((0, 4),)),
        "channel_shift": scatter_about(key_of[17], (LAYERS, D), 0.3, 1.5, ((0, 4),), jnp.float32),
        "norm_gain": jnp.clip(1.0 + 0.1 * jax.random.normal(key_of[18], (LAYERS, 2, D), jnp.float32), 0.5, 1.5),
        "norm_shift": scatter_about(key_of[19], (LAYERS, 2, D), 0.3, 1.5, ((0, 4),), jnp.float32),
    }


@jax.custom_vjp
def low(v):
    return lax.optimization_barrier(v.astype(jnp.bfloat16)).astype(jnp.float32)

@jax.custom_vjp
def low_back(v):
    return v

def low_keep(v):
    return (low(v), None)

def low_pass(kept, grad):
    return (grad,)

def back_keep(v):
    return (v, None)

def back_low(kept, grad):
    return (low(grad),)
low.defvjp(low_keep, low_pass)
low_back.defvjp(back_keep, back_low)
EPSILON = 1e-06
HIGHEST = lax.Precision.HIGHEST

def norm_rows(value, gain, shift):
    center = lax.optimization_barrier(jnp.mean(value, axis=-1, keepdims=True))
    centred = value - center
    spread = lax.optimization_barrier(jnp.mean(centred * centred, axis=-1, keepdims=True))
    return centred * lax.rsqrt(spread + EPSILON) * gain + shift

def mixer_layer(value, keep, token_set, shared):
    tok_in, tok_bias, tok_out, tok_shift = token_set
    chan_in, chan_bias, chan_out, chan_shift, gains, shifts = shared
    normed = low(norm_rows(value, gains[0], shifts[0]))
    pre = jnp.einsum('sk,isd->ikd', tok_in, normed, precision=HIGHEST) + tok_bias[None, :, None]
    hidden = low(jax.nn.gelu(low_back(pre), approximate=False))
    branch = jnp.einsum('ks,ikd->isd', tok_out, hidden, precision=HIGHEST) + tok_shift[None, :, None]
    branch = low_back(branch)
    middle = value + keep[:, 0, None, None] * branch
    normed_two = low(norm_rows(middle, gains[1], shifts[1]))
    pre_two = jnp.einsum('isd,dc->isc', normed_two, chan_in, precision=HIGHEST) + chan_bias
    hidden_two = low(jax.nn.gelu(low_back(pre_two), approximate=False))
    branch_two = low_back(jnp.einsum('isc,cd->isd', hidden_two, chan_out, precision=HIGHEST) + chan_shift)
    return middle + keep[:, 1, None, None] * branch_two

def network(weights, small_value, large_value, small_mask, large_mask, small_taps, large_taps):
    small_now = small_value
    large_now = large_value
    small_made = []
    large_made = []
    for layer in range(LAYERS):
        small_now = low_back(small_now + small_taps[layer])
        large_now = low_back(large_now + large_taps[layer])
        shared = tuple((w[layer] for w in weights[8:]))
        small_set = tuple((w[layer] for w in weights[0:4]))
        large_set = tuple((w[layer] for w in weights[4:8]))
        small_now = low(mixer_layer(small_now, small_mask[layer], small_set, shared))
        large_now = low(mixer_layer(large_now, large_mask[layer], large_set, shared))
        small_made.append(small_now)
        large_made.append(large_now)
    return ((small_now, large_now), (jnp.stack(small_made), jnp.stack(large_made)))

def reference(small_images, large_images, small_upstream, large_upstream, small_keep, large_keep, small_in, small_bias, small_out, small_shift, large_in, large_bias, large_out, large_shift, channel_in, channel_bias, channel_out, channel_shift, norm_gain, norm_shift):
    weights = tuple((w.astype(jnp.float32) for w in (small_in, small_bias, small_out, small_shift, large_in, large_bias, large_out, large_shift, channel_in, channel_bias, channel_out, channel_shift, norm_gain, norm_shift)))
    small_masks = jnp.moveaxis(small_keep, 1, 0).astype(jnp.float32)
    large_masks = jnp.moveaxis(large_keep, 1, 0).astype(jnp.float32)

    def one_micro(totals, slices):
        small_value, large_value, small_grad, large_grad, small_mask, large_mask = slices
        small_value = small_value.astype(jnp.float32)
        large_value = large_value.astype(jnp.float32)
        small_taps = jnp.zeros((LAYERS,) + small_value.shape, jnp.float32)
        large_taps = jnp.zeros((LAYERS,) + large_value.shape, jnp.float32)

        def run(params, taps_small, taps_large):
            return network(params, small_value, large_value, small_mask, large_mask, taps_small, taps_large)
        finals, backward, made = jax.vjp(run, weights, small_taps, large_taps, has_aux=True)
        grads, small_back, large_back = backward((small_grad.astype(jnp.float32), large_grad.astype(jnp.float32)))
        totals = tuple((a + b for a, b in zip(totals, grads)))
        return (totals, (made[0], made[1], small_back, large_back))
    start = tuple((jnp.zeros_like(w) for w in weights))
    totals, stacked = lax.scan(one_micro, start, (small_images, large_images, small_upstream, large_upstream, small_masks, large_masks))
    small_made, large_made, small_back, large_back = (jnp.swapaxes(s, 0, 1).astype(jnp.bfloat16) for s in stacked)
    return (small_made, large_made, small_back, large_back, totals[0], totals[1], totals[2], totals[3], totals[4], totals[5], totals[6], totals[7], totals[8], totals[9], totals[10], totals[11], totals[12], totals[13])
```

```python
import functools

import jax
import jax.numpy as jnp
from jax import lax
from jax.experimental import pallas as pl
from jax.experimental.pallas import tpu as pltpu
from jax.sharding import PartitionSpec as P

MESH = pl.DeviceIdType.MESH
F32 = jnp.float32
BF16 = jnp.bfloat16
EPSILON = 1e-06
DENSITY = 0.3989422804014327
ROWS = 144
COLS = 256
WIDE = 512


def up_to(value, step):
    return -(-value // step) * step


def mm(a, b, ca, cb):
    return lax.dot_general(a, b, (((ca,), (cb,)), ((), ())), preferred_element_type=F32)


def gelu_pair(v):
    cdf = 0.5 + 0.5 * lax.erf(v * 0.7071067811865476)
    bell = jnp.exp2((v * v) * (-0.5 * 1.4426950408889634))
    return v * cdf, cdf + (v * DENSITY) * bell


def groups(x):
    return x.reshape(x.shape[0] // 8, 8, x.shape[1]).sum(0)


def kernel(
    dims,
    small_images,
    large_images,
    small_upstream,
    large_upstream,
    small_keep,
    large_keep,
    small_in,
    small_bias,
    small_out,
    small_shift,
    large_in,
    large_bias,
    large_out,
    large_shift,
    channel_in,
    channel_bias,
    channel_out,
    channel_shift,
    norm_gain,
    norm_shift,
    small_made,
    large_made,
    small_back,
    large_back,
    chan_a,
    chan_b,
    tok_l,
    tok_s,
    vec_out,
    win,
    wout,
    hid,
    slope,
    xin,
    up,
    n1,
    n2,
    u2,
    r2,
    gb1,
    stage,
    h1,
    sl1,
    lgin,
    lgin_t,
    lgout,
    lgout_t,
    sgin,
    sgin_t,
    sgout,
    sgout_t,
    turned,
    lbcol,
    lscol,
    sbcol,
    sscol,
    mid,
    acc,
    raw_a,
    raw_b,
    sums,
    wsem,
    isem,
    usem,
    ysem,
    gsem,
    fs,
    fr,
    bs,
    br,
    sibs,
    rights,
    lefts,
    outsem,
    vsem,
    ready,
    tl,
    ts,
    vecs,
):
    sections, n, ps, pl_, pp, d, ds_, dc, dp, fused = dims
    place = lax.axis_index("section")
    ahead = lax.rem(place + 1, sections)
    behind = lax.rem(place + sections - 1, sections)
    last = place // (sections - 1)
    first_rows = n * pl_
    half = pl_ // 2
    line = dp // 2 if fused else 1
    rank = lax.axis_index("dp")
    z = rank // 2
    core = rank % 2
    sibling = rank + 1 - 2 * core

    def weight_copies():
        pairs = (
            (large_in, lgin),
            (large_out, lgout_t),
            (small_in, raw_a.at[0, :, pl.ds(0, ds_)]),
            (small_out, raw_a.at[0, :, pl.ds(ds_, ds_)]),
            (channel_in, win),
            (channel_out, wout),
        )
        return [pltpu.make_async_copy(a, b, wsem.at[k]) for k, (a, b) in enumerate(pairs)]

    def large_copy(src, dst, sem, i):
        return pltpu.make_async_copy(src.at[i], dst.at[pl.ds(pl.multiple_of(i * pl_, 64), pl_)], sem.at[i])

    def small_copy(src, dst, sem, j):
        return pltpu.make_async_copy(src.at[j], dst.at[j], sem.at[n + j])

    copies = weight_copies()

    @pl.when(place == 0)
    def _():
        for i in range(n):
            large_copy(large_images, xin, isem, i).start()

    for c in copies:
        c.start()

    @pl.when(last == 1)
    def _():
        for i in range(n):
            large_copy(large_upstream, up, usem, i).start()
        for j in range(n):
            small_copy(small_upstream, raw_b, usem, j).start()

    barrier = pltpu.get_barrier_semaphore()

    @pl.when(place > 0)
    def _():
        pl.semaphore_signal(barrier, inc=1, device_id={"section": behind}, device_id_type=MESH)

    @pl.when(place < sections - 1)
    def _():
        pl.semaphore_signal(barrier, inc=1, device_id={"section": ahead}, device_id_type=MESH)

    peers = (place + sections - 2) // (sections - 1) + 1 - last
    if fused:
        pl.semaphore_signal(barrier, inc=1, device_id={"dp": sibling}, device_id_type=MESH)
        for k in range(1, line):
            pl.semaphore_signal(barrier, inc=1, device_id={"dp": (rank + 2 * k) % dp}, device_id_type=MESH)
        peers = peers + line
    pl.semaphore_wait(barrier, peers)

    def column(row, dst):
        width = up_to(dst.shape[0], 128)
        sums[0:1, 0:width] = jnp.zeros((1, width), F32)
        sums[0:1, 0 : row.shape[1]] = row
        dst[...] = jnp.transpose(jnp.broadcast_to(sums[0:1, 0:width], (128, width)))[0 : dst.shape[0]]

    column(large_bias[...], lbcol)
    column(large_shift[...], lscol)
    column(small_bias[...], sbcol)
    column(small_shift[...], sscol)
    sums[...] = jnp.zeros(sums.shape, F32)
    for c in copies[:4]:
        c.wait()
    for k, padded in enumerate((sgin, sgout_t)):
        padded[...] = jnp.zeros(padded.shape, BF16)
        padded[0:ps, :] = raw_a[0, :, k * ds_ : (k + 1) * ds_]

    @pl.when(place == 0)
    def _():
        for j in range(n):
            small_copy(small_images, raw_a, isem, j).start()

    lgin_t[...] = jnp.transpose(lgin[...])
    lgout[...] = jnp.transpose(lgout_t[...])
    sgin_t[...] = jnp.transpose(sgin[...])
    sgout[...] = jnp.transpose(sgout_t[...])

    gains = norm_gain[...]
    shifts = norm_shift[...]

    def ahead_copy(rows, size, k):
        return pltpu.make_async_remote_copy(
            src_ref=stage.at[pl.ds(rows, size)],
            dst_ref=xin.at[pl.ds(rows, size)],
            send_sem=fs.at[k],
            recv_sem=fr.at[k],
            device_id={"section": ahead},
            device_id_type=MESH,
        )

    def behind_copy(rows, size, k):
        return pltpu.make_async_remote_copy(
            src_ref=stage.at[pl.ds(rows, size)],
            dst_ref=up.at[pl.ds(rows, size)],
            send_sem=bs.at[k],
            recv_sem=br.at[k],
            device_id={"section": behind},
            device_id_type=MESH,
        )

    class Unit:
        def __init__(self, large, i):
            self.large = large
            self.i = i
            self.rows = pl_ if large else pp
            self.blocks = 2 if large else 1
            self.size = self.rows // self.blocks
            self.some = ROWS if large else pp
            self.base = pl.multiple_of(i * pl_, 64) if large else pl.multiple_of(first_rows + i * pp, 16)
            self.head = pl.multiple_of((i if large else n + i) * ds_, 128)
            self.heads = pl.ds(self.head, ds_)
            self.slot = i * 2 if large else 2 * n + i
            self.gin, self.gin_t = (lgin, lgin_t) if large else (sgin, sgin_t)
            self.gout, self.gout_t = (lgout, lgout_t) if large else (sgout, sgout_t)
            self.bcol, self.scol = (lbcol, lscol) if large else (sbcol, sscol)
            self.mask = large_keep if large else small_keep

        def at(self, offset, size):
            return pl.ds(pl.multiple_of(self.base + offset, 16), size)

        def keep(self, which):
            return self.mask[self.i, which].astype(F32)

        def out_copy(self, which, b):
            sem = (ysem, gsem)[which].at[self.slot + b]
            if self.large:
                dst = (large_made, large_back)[which]
                return pltpu.make_async_copy(
                    stage.at[self.at(b * half, half)], dst.at[self.i, pl.ds(b * half, half)], sem
                )
            src = (raw_a, raw_b)[which]
            dst = (small_made, small_back)[which]
            return pltpu.make_async_copy(src.at[self.i], dst.at[self.i], sem)

    units = 2 * n

    def unit_at(which):
        return (which + core) % 2, which // 2

    def forward(unit, step):
        @pl.when(place == 0)
        def _():
            if unit.large:
                large_copy(large_images, xin, isem, unit.i).wait()
            else:
                small_copy(small_images, raw_a, isem, unit.i).wait()
                xin[unit.at(0, pp)] = jnp.zeros((pp, d), BF16)
                xin[unit.at(0, ps)] = raw_a[unit.i]

        def norm_one(r):
            rows = unit.at(r * unit.some, unit.some)
            x = xin[rows].astype(F32)
            x = x - jnp.mean(x, axis=1, keepdims=True)
            s = lax.rsqrt(jnp.mean(x * x, axis=1, keepdims=True) + EPSILON)
            n1[rows] = (x * s * gains[0:1] + shifts[0:1]).astype(BF16)

        steps = unit.size // unit.some
        for b in range(unit.blocks):

            @pl.when(place > 0)
            def _(b=b):
                ahead_copy(unit.base + b * unit.size, unit.size, unit.slot + b).wait_recv()

            for r in range(b * steps, (b + 1) * steps):
                norm_one(r)
        rows = unit.at(0, unit.rows)
        keep_one = unit.keep(0)
        keep_two = unit.keep(1)
        for c in range(0, d, COLS):
            pre = mm(unit.gin_t[...], n1[rows, c : c + COLS], 1, 0) + unit.bcol[:, 0:1]
            act, slp = gelu_pair(pre)
            h1[unit.heads, c : c + COLS] = act.astype(BF16)
            sl1[unit.heads, c : c + COLS] = slp.astype(BF16)
        for c in range(0, d, COLS):
            branch = mm(unit.gout_t[...], h1[unit.heads, c : c + COLS], 1, 0) + unit.scol[:, 0:1]
            mid[0 : unit.rows, c : c + COLS] = xin[rows, c : c + COLS].astype(F32) + keep_one * branch

        def norm_two(r):
            rows = unit.at(r * unit.some, unit.some)
            x = mid[r * unit.some : (r + 1) * unit.some]
            x = x - jnp.mean(x, axis=1, keepdims=True)
            s = lax.rsqrt(jnp.mean(x * x, axis=1, keepdims=True) + EPSILON)
            x = x * s
            u2[rows] = x.astype(BF16)
            r2[rows] = jnp.broadcast_to(s, (unit.some, 128))
            n2[rows] = (x * gains[1:2] + shifts[1:2]).astype(BF16)

        for r in range(unit.rows // unit.some):
            norm_two(r)

        @pl.when(step == 0)
        def _():
            for c in copies[4:]:
                c.wait()

        for b in range(unit.blocks):
            size = unit.size
            rows = unit.at(b * size, size)
            here = slice(b * size, (b + 1) * size)
            total = channel_shift[...]
            parts = [slice(c, c + WIDE) for c in range(0, dc, WIDE)]
            ahead_of = mm(n2[rows], win[:, parts[0]], 1, 0)
            for c, cols in enumerate(parts):
                pre = ahead_of + channel_bias[:, cols]
                if c + 1 < len(parts):
                    ahead_of = mm(n2[rows], win[:, parts[c + 1]], 1, 0)
                act, slp = gelu_pair(pre)
                act = act.astype(BF16)
                hid[rows, cols] = act
                slope[rows, cols] = slp.astype(BF16)
                total = total + mm(act, wout[cols, :], 1, 0)
            y = (mid[here] + keep_two * total).astype(BF16)
            stage[rows] = y
            if not unit.large:
                raw_a[unit.i] = y[0:ps]

            @pl.when(place < sections - 1)
            def _(b=b, size=size):
                ahead_copy(unit.base + b * size, size, unit.slot + b).start()

            unit.out_copy(0, b).start()

    def backward(unit):
        @pl.when(last == 1)
        def _():
            if unit.large:
                large_copy(large_upstream, up, usem, unit.i).wait()
            else:
                small_copy(small_upstream, raw_b, usem, unit.i).wait()
                up[unit.at(0, pp)] = jnp.zeros((pp, d), BF16)
                up[unit.at(0, ps)] = raw_b[unit.i]

        keep_one = unit.keep(0)
        keep_two = unit.keep(1)
        size = unit.size
        for b in range(unit.blocks):
            rows = unit.at(b * size, size)
            here = slice(b * size, (b + 1) * size)

            @pl.when(place < sections - 1)
            def _(b=b):
                ahead_copy(unit.base + b * size, size, unit.slot + b).wait_send()

            unit.out_copy(0, b).wait()

            @pl.when(last == 0)
            def _(b=b):
                behind_copy(unit.base + b * size, size, unit.slot + b).wait_recv()

            stage[rows] = up[rows] * keep_two.astype(BF16)

            parts = [slice(c, c + WIDE) for c in range(0, dc, WIDE)]
            total = None
            ahead_of = mm(stage[rows], wout[parts[0], :], 1, 1)
            for c, cols in enumerate(parts):
                grad = ahead_of
                if c + 1 < len(parts):
                    ahead_of = mm(stage[rows], wout[parts[c + 1], :], 1, 1)
                grad = (grad * slope[rows, cols].astype(F32)).astype(BF16)
                slope[rows, cols] = grad
                term = mm(grad, win[:, cols], 1, 1)
                total = term if total is None else total + term
            acc[here] = total

        def norm_two(r):
            offset = r * unit.some
            rows = unit.at(offset, unit.some)
            local = slice(offset, offset + unit.some)
            h = acc[local]
            u = u2[rows].astype(F32)
            s = r2[rows][:, 0:1]
            g = up[rows].astype(F32)
            q = h * gains[1:2]
            first = jnp.mean(q, axis=1, keepdims=True)
            second = jnp.mean(q * u, axis=1, keepdims=True)
            g_mid = g + s * (q - first - u * second)
            mid[local] = g_mid
            gb1[rows] = (keep_one * g_mid).astype(BF16)
            up[rows] = (keep_two * g).astype(BF16)
            return groups(h * u), groups(h)

        parts = [norm_two(r) for r in range(unit.rows // unit.some)]
        sums[8:16, 0:d] += sum(p[0] for p in parts)
        sums[24:32, 0:d] += sum(p[1] for p in parts)
        rows = unit.at(0, unit.rows)
        for c in range(0, d, COLS):
            grad = mm(unit.gout[...], gb1[rows, c : c + COLS], 1, 0)
            grad = (grad * sl1[unit.heads, c : c + COLS].astype(F32)).astype(BF16)
            sl1[unit.heads, c : c + COLS] = grad
        for c in range(0, d, COLS):
            acc[0 : unit.rows, c : c + COLS] = mm(unit.gin[...], sl1[unit.heads, c : c + COLS], 1, 0)

        def norm_one(r):
            offset = r * unit.some
            rows = unit.at(offset, unit.some)
            local = slice(offset, offset + unit.some)
            x = xin[rows].astype(F32)
            x = x - jnp.mean(x, axis=1, keepdims=True)
            s = lax.rsqrt(jnp.mean(x * x, axis=1, keepdims=True) + EPSILON)
            u = x * s
            h = acc[local]
            q = h * gains[0:1]
            first = jnp.mean(q, axis=1, keepdims=True)
            second = jnp.mean(q * u, axis=1, keepdims=True)
            stage[rows] = (mid[local] + s * (q - first - u * second)).astype(BF16)
            return groups(h * u), groups(h)

        steps = size // unit.some
        for b in range(unit.blocks):
            parts = [norm_one(r) for r in range(b * steps, (b + 1) * steps)]
            sums[0:8, 0:d] += sum(p[0] for p in parts)
            sums[16:24, 0:d] += sum(p[1] for p in parts)
            if not unit.large:
                raw_b[unit.i] = stage[unit.at(0, ps)]

            @pl.when(place > 0)
            def _(b=b):
                behind_copy(unit.base + b * size, size, unit.slot + b).start()

            unit.out_copy(1, b).start()

    piece = d // dp
    tok_piece = ds_ // dp

    def turn(src):
        def some(rows, size):
            value = jnp.transpose(src[pl.ds(rows, size)])
            if not fused:
                turned[:, pl.ds(rows, size)] = value
                return
            for b in range(dp):
                at = ((b % 2) * line + b // 2) * piece
                turned[at : at + piece, pl.ds(rows, size)] = value[b * piece : (b + 1) * piece]

        def full(r, carry):
            some(pl.multiple_of(r * 128, 128), 128)
            return carry

        whole = src.shape[0] // 128
        lax.fori_loop(0, whole, full, 0)
        if src.shape[0] % 128:
            some(whole * 128, src.shape[0] % 128)


    def step(t, carry):
        back = (1 - last) * (t // units) + last * (t % 2)
        which = (1 - last) * (t % units) + last * (t // 2)
        small, i = unit_at(which)

        @pl.when(t == 2 * units - 1)
        def _():
            turn(n2)

        @pl.when((back == 0) & (small == 0))
        def _():
            forward(Unit(True, i), t)

        @pl.when((back == 0) & (small == 1))
        def _():
            forward(Unit(False, i), t)

        @pl.when((back == 1) & (small == 0))
        def _():
            backward(Unit(True, i))

        @pl.when((back == 1) & (small == 1))
        def _():
            backward(Unit(False, i))

        return carry

    lax.fori_loop(0, 2 * units, step, 0)

    total = hid.shape[0]
    chunks = dc // d
    kinds = (chunks, chunks, 1, 1)
    first_of = (0, chunks, 2 * chunks, 2 * chunks + 1)
    count = sum(kinds)
    large_width, small_width = up_to(pl_, 128), up_to(pp, 128)
    widths = (d, d, large_width, small_width)
    own = line
    across = line + 1

    def columns(kind, k):
        if kind < 2:
            return pl.ds(pl.multiple_of(k * d, 128), d)
        return pl.ds(0, widths[kind])

    def own_rows(kind):
        return ((slope, 0), (hid, 0), (up, 0), (up, d))[kind]

    def weight_product(kind, k):
        src = (slope, hid)[kind]

        def part(j, carry):
            cols = pl.ds(pl.multiple_of(k * d + j * COLS, COLS), COLS)
            if kind == 0:
                bias = mm(jnp.ones((8, total), BF16), src[:, cols], 1, 0)[0:1]
                vecs[own, pl.ds(k, 1), pl.ds(pl.multiple_of(j * COLS, COLS), COLS)] = bias
            src[0:d, cols] = mm(turned[...], src[:, cols], 1, 0).astype(BF16)
            return carry

        lax.fori_loop(0, d // COLS, part, 0)

    def token_product(large):
        unit_rows = pl_ if large else pp
        ones_d = jnp.ones((8, d), BF16)
        out_grad = in_grad = bias = shift = None
        for k in range(n):
            base = k * pl_ if large else first_rows + k * pp
            head = k * ds_ if large else (n + k) * ds_
            g = gb1[base : base + unit_rows]
            x = n1[base : base + unit_rows]
            h = h1[head : head + ds_]
            p = sl1[head : head + ds_]
            terms = (mm(p, x, 1, 1), mm(h, g, 1, 1), mm(ones_d, p, 1, 1), mm(ones_d, g, 1, 1))
            if k == 0:
                in_grad, out_grad, bias, shift = terms
            else:
                in_grad, out_grad, bias, shift = in_grad + terms[0], out_grad + terms[1], bias + terms[2], shift + terms[3]
        src, base = own_rows(2 if large else 3)
        for at, value in ((0, in_grad), (1, out_grad)):
            value = value.astype(BF16)
            if not fused:
                src[base + at * ds_ : base + (at + 1) * ds_, 0:unit_rows] = value
                continue
            for b in range(dp):
                to = base + ((b % 2) * line + b // 2) * piece + at * tok_piece
                src[to : to + tok_piece, 0:unit_rows] = value[b * tok_piece : (b + 1) * tok_piece]
        row = chunks + 5 + (0 if large else 2)
        vecs[own, row : row + 1, 0:ds_] = bias[0:1]
        vecs[own, row + 1 : row + 2, 0:unit_rows] = shift[0:1]

    def product(kind, k):
        if kind < 2:
            if kind == 1:

                @pl.when(k == 0)
                def _():
                    turn(up)
                    vecs[own, chunks : chunks + 1] = mm(jnp.ones((8, total), BF16), up[...], 1, 0)[0:1]
                    for j in range(4):
                        vecs[own, chunks + 1 + j : chunks + 2 + j] = jnp.sum(sums[8 * j : 8 * j + 8], axis=0, keepdims=True)

            weight_product(kind, k)
        else:
            token_product(kind == 2)

    def ways(step_of):
        def at(c, valid=True):
            for kind in range(4):
                low, high = first_of[kind], first_of[kind] + kinds[kind]

                @pl.when((c >= low) & (c < high) & valid)
                def _(kind=kind, low=low):
                    step_of(kind, c - low)

        return at

    vecs[own] = jnp.zeros(vecs.shape[1:], F32)
    if not fused:

        def whole_copies(kind, k):
            src, base = own_rows(kind)
            if kind < 2:
                cols = columns(kind, k)
                dst = (chan_a, chan_b)[kind]
                return [pltpu.make_async_copy(src.at[pl.ds(0, d), cols], dst.at[:, cols], outsem.at[first_of[kind] + k])]
            cols = pl.ds(0, widths[kind])
            dst = (tok_l, tok_s)[kind - 2]
            return [pltpu.make_async_copy(src.at[pl.ds(base, d), cols], dst, outsem.at[first_of[kind]])]

        def one(kind, k):
            product(kind, k)
            for c in whole_copies(kind, k):
                c.start()

        def finish(kind, k):
            for c in whole_copies(kind, k):
                c.wait()

        def run(c, carry):
            ways(one)(c)
            return carry

        def end(c, carry):
            ways(finish)(c)
            return carry

        lax.fori_loop(0, count, run, 0)
        lax.fori_loop(0, count, end, 0)
        vec_out[...] = vecs[own]
    else:
        rightward, leftward = (rank + 2) % dp, (rank + dp - 2) % dp

        def mine(kind, k, to, core_of=core):
            src, base = own_rows(kind)
            return src.at[pl.ds(pl.multiple_of(base + (core_of * line + to) * piece, 16), piece), columns(kind, k)]

        def crossing(kind, k, rows, size):
            ref, base = ((win, 0), (win, d // 2), (wout, 3 * d), (wout, 3 * d + d // 2))[kind]
            return ref.at[pl.ds(pl.multiple_of(base + rows, 16), size), columns(kind, k)]

        def from_left(kind, k, to):
            ref, base = ((wout, 0), (wout, chunks * (line - 1)), (n2, 0), (n2, line - 1))[kind]
            rows = (base + k * (line - 1) + to - 1) * piece
            return ref.at[pl.ds(pl.multiple_of(rows, 16), piece), pl.ds(0, widths[kind])]

        def from_right(kind, k, to):
            ref, base = ((xin, 0), (u2, 0), (n2, 2 * (line - 1)), (n2, 3 * (line - 1)))[kind]
            rows = (base + k * (line - 1) + to) * piece
            return ref.at[pl.ds(pl.multiple_of(rows, 16), piece), pl.ds(0, widths[kind])]

        def sem_of(kind, k, to):
            return (first_of[kind] + k) * line + to

        def cross_copy(kind, k):
            src, base = own_rows(kind)
            rows = pl.ds(pl.multiple_of(base + (1 - core) * line * piece, 16), line * piece)
            c = first_of[kind] + k
            return pltpu.make_async_remote_copy(
                src_ref=src.at[rows, columns(kind, k)],
                dst_ref=crossing(kind, k, 0, line * piece),
                send_sem=sibs.at[0, c],
                recv_sem=sibs.at[1, c],
                device_id={"dp": sibling},
                device_id_type=MESH,
            )

        def right_copy(kind, k, to):
            return pltpu.make_async_remote_copy(
                src_ref=mine(kind, k, to),
                dst_ref=from_left(kind, k, to),
                send_sem=rights.at[0, sem_of(kind, k, to)],
                recv_sem=rights.at[1, sem_of(kind, k, to)],
                device_id={"dp": rightward},
                device_id_type=MESH,
            )

        def left_copy(kind, k, to):
            return pltpu.make_async_remote_copy(
                src_ref=mine(kind, k, to),
                dst_ref=from_right(kind, k, to),
                send_sem=lefts.at[0, sem_of(kind, k, to)],
                recv_sem=lefts.at[1, sem_of(kind, k, to)],
                device_id={"dp": leftward},
                device_id_type=MESH,
            )

        def chip_sum(kind, k, to):
            return mine(kind, k, to)[...].astype(F32) + crossing(kind, k, to * piece, piece)[...].astype(F32)

        def flow_right(kind, k):
            def one(j, carry):
                to = line - 1 - j

                @pl.when(z == 0)
                def _():
                    mine(kind, k, to)[...] = chip_sum(kind, k, to).astype(BF16)

                @pl.when(z > 0)
                def _():
                    right_copy(kind, k, to).wait_recv()
                    value = chip_sum(kind, k, to) + from_left(kind, k, to)[...].astype(F32)
                    mine(kind, k, to)[...] = value.astype(BF16)

                right_copy(kind, k, to).start()
                return carry

            lax.fori_loop(0, line - 1 - z, one, 0)

        def flow_left(kind, k):
            def one(to, carry):
                @pl.when(z == line - 1)
                def _():
                    mine(kind, k, to)[...] = chip_sum(kind, k, to).astype(BF16)

                @pl.when(z < line - 1)
                def _():
                    left_copy(kind, k, to).wait_recv()
                    value = chip_sum(kind, k, to) + from_right(kind, k, to)[...].astype(F32)
                    mine(kind, k, to)[...] = value.astype(BF16)

                left_copy(kind, k, to).start()
                return carry

            lax.fori_loop(0, z, one, 0)

        def out_stage(kind, k):
            if kind == 0:
                return mid.at[pl.ds(pl.multiple_of(k * piece, 16), piece)]
            if kind == 1:
                return acc.at[pl.ds(pl.multiple_of(k * piece, 16), piece)]
            return (tl, ts)[kind - 2]

        def out_copies(kind, k):
            c = first_of[kind] + k
            if kind < 2:
                dst = (chan_a, chan_b)[kind].at[:, columns(kind, k)]
            else:
                dst = (tok_l, tok_s)[kind - 2]
            return pltpu.make_async_copy(out_stage(kind, k), dst, outsem.at[c])

        def gather(kind, k):
            width = (d, d, pl_, ps)[kind]
            dst = out_stage(kind, k)
            dst[...] = chip_sum(kind, k, z)[:, 0:width]

            @pl.when(z > 0)
            def _():
                right_copy(kind, k, z).wait_recv()
                dst[...] += from_left(kind, k, z)[...].astype(F32)[:, 0:width]

            @pl.when(z < line - 1)
            def _():
                left_copy(kind, k, z).wait_recv()
                dst[...] += from_right(kind, k, z)[...].astype(F32)[:, 0:width]

            out_copies(kind, k).start()

        def vec_cross():
            return pltpu.make_async_remote_copy(
                src_ref=vecs.at[own],
                dst_ref=vecs.at[across],
                send_sem=vsem.at[0, 0],
                recv_sem=vsem.at[1, 0],
                device_id={"dp": sibling},
                device_id_type=MESH,
            )

        def vec_copy(k):
            return pltpu.make_async_remote_copy(
                src_ref=vecs.at[z],
                dst_ref=vecs.at[z],
                send_sem=vsem.at[0, k],
                recv_sem=vsem.at[1, k],
                device_id={"dp": (rank + 2 * k) % dp},
                device_id_type=MESH,
            )

        def first(kind, k):
            product(kind, k)
            if kind == 0:

                @pl.when(k == 0)
                def _():
                    pl.semaphore_wait(ready.at[0], 1)

                    @pl.when(z < line - 1)
                    def _():
                        pl.semaphore_wait(ready.at[1], 1)

                    @pl.when(z > 0)
                    def _():
                        pl.semaphore_wait(ready.at[2], 1)

            cross_copy(kind, k).start()

        def crossed(kind, k):
            cross_copy(kind, k).wait_recv()

        def finish(kind, k):
            cross_copy(kind, k).wait_send()
            out_copies(kind, k).wait()

            def right(j, carry):
                right_copy(kind, k, line - 1 - j).wait_send()
                return carry

            def left(to, carry):
                left_copy(kind, k, to).wait_send()
                return carry

            lax.fori_loop(0, line - 1 - z, right, 0)
            lax.fori_loop(0, z, left, 0)

        pl.semaphore_signal(ready.at[0], inc=1, device_id={"dp": sibling}, device_id_type=MESH)

        @pl.when(z > 0)
        def _():
            pl.semaphore_signal(ready.at[1], inc=1, device_id={"dp": leftward}, device_id_type=MESH)

        @pl.when(z < line - 1)
        def _():
            pl.semaphore_signal(ready.at[2], inc=1, device_id={"dp": rightward}, device_id_type=MESH)

        def run(c, carry):

            ways(crossed)(c - 1)
            ways(flow_right)(c - 1 - z, z < line - 1)
            ways(flow_left)(c - line + z, z > 0)
            ways(first)(c)

            @pl.when(c == count)
            def _():
                vec_cross().start()

            @pl.when(c == count + 1)
            def _():
                vec_cross().wait()
                vecs[z] = vecs[own] + vecs[across]
                for k in range(1, line):
                    vec_copy(k).start()

            ways(gather)(c - line - 1)
            return carry

        lax.fori_loop(0, count + line + 1, run, 0)

        def end(c, carry):
            ways(finish)(c)
            return carry

        lax.fori_loop(0, count, end, 0)
        for k in range(1, line):
            vec_copy(k).wait()
        value = vecs[0]
        for k in range(1, line):
            value = value + vecs[k]
        vec_out[...] = value

    for i in range(2 * n):
        unit = Unit(i < n, i % n)
        for b in range(unit.blocks):
            unit.out_copy(1, b).wait()

            @pl.when(place > 0)
            def _(b=b, unit=unit):
                behind_copy(unit.base + b * unit.size, unit.size, unit.slot + b).wait_send()


def finish_kernel(tok_piece, d, chunks, tok_l, tok_s, vec, *outs):
    for k, src in enumerate((tok_l, tok_s)):
        outs[2 * k][...] = src[0:tok_piece]
        outs[2 * k + 1][...] = src[tok_piece:]
    for k in range(chunks):
        outs[4][:, k * d : (k + 1) * d] = vec[k : k + 1]
    at = chunks
    for out in outs[5:]:
        rows, width = out.shape
        out[...] = vec[at : at + rows, 0:width]
        at += rows


def local(
    small_images,
    large_images,
    small_upstream,
    large_upstream,
    small_keep,
    large_keep,
    small_in,
    small_bias,
    small_out,
    small_shift,
    large_in,
    large_bias,
    large_out,
    large_shift,
    channel_in,
    channel_bias,
    channel_out,
    channel_shift,
    norm_gain,
    norm_shift,
):
    sections = lax.axis_size("section")
    micro, imgs, ps, d = small_images.shape
    pl_ = large_images.shape[2]
    n = micro * imgs
    ds_ = small_in.shape[2]
    dc = channel_in.shape[2]
    pp = up_to(ps, 16)
    rows = n * (pl_ + pp)
    small_width, large_width = up_to(pp, 128), up_to(pl_, 128)
    dp = lax.axis_size("dp")
    piece, tok_piece = d // dp, ds_ // dp
    fused = d % (16 * dp) == 0 and ds_ % (16 * dp) == 0 and dc == 4 * d and d == 2 * ds_ and 2 * dp * piece <= rows
    dims = (sections, n, ps, pl_, pp, d, ds_, dc, dp, fused)
    chunks = dc // d
    line = dp // 2 if fused else 1
    count = 2 * chunks + 2
    vec_rows = up_to(chunks + 9, 8)
    any_ = pl.BlockSpec(memory_space=pl.ANY)
    vmem = pl.BlockSpec(memory_space=pltpu.VMEM)
    smem = pl.BlockSpec(memory_space=pltpu.SMEM)
    block = max(pl_, n * pp)
    blocks = 2 * n + n
    scratch = [
        pltpu.VMEM((d, dc), BF16),
        pltpu.VMEM((dc, d), BF16),
        pltpu.VMEM((rows, dc), BF16),
        pltpu.VMEM((rows, dc), BF16),
        pltpu.VMEM((rows, d), BF16),
        pltpu.VMEM((rows, d), BF16),
        pltpu.VMEM((rows, d), BF16),
        pltpu.VMEM((rows, d), BF16),
        pltpu.VMEM((rows, d), BF16),
        pltpu.VMEM((rows, 128), F32),
        pltpu.VMEM((rows, d), BF16),
        pltpu.VMEM((rows, d), BF16),
        pltpu.VMEM((2 * n * ds_, d), BF16),
        pltpu.VMEM((2 * n * ds_, d), BF16),
        pltpu.VMEM((pl_, ds_), BF16),
        pltpu.VMEM((ds_, pl_), BF16),
        pltpu.VMEM((ds_, pl_), BF16),
        pltpu.VMEM((pl_, ds_), BF16),
        pltpu.VMEM((pp, ds_), BF16),
        pltpu.VMEM((ds_, pp), BF16),
        pltpu.VMEM((ds_, pp), BF16),
        pltpu.VMEM((pp, ds_), BF16),
        pltpu.VMEM((d, rows), BF16),
        pltpu.VMEM((ds_, 128), F32),
        pltpu.VMEM((pl_, 128), F32),
        pltpu.VMEM((ds_, 128), F32),
        pltpu.VMEM((pp, 128), F32),
        pltpu.VMEM((block, d), F32),
        pltpu.VMEM((block, d), F32),
        pltpu.VMEM((n, ps, d), BF16),
        pltpu.VMEM((n, ps, d), BF16),
        pltpu.VMEM((32, d), F32),
        pltpu.SemaphoreType.DMA((6,)),
        pltpu.SemaphoreType.DMA((2 * n,)),
        pltpu.SemaphoreType.DMA((2 * n,)),
        pltpu.SemaphoreType.DMA((blocks,)),
        pltpu.SemaphoreType.DMA((blocks,)),
        pltpu.SemaphoreType.DMA((blocks,)),
        pltpu.SemaphoreType.DMA((blocks,)),
        pltpu.SemaphoreType.DMA((blocks,)),
        pltpu.SemaphoreType.DMA((blocks,)),
        pltpu.SemaphoreType.DMA((2, count)),
        pltpu.SemaphoreType.DMA((2, count * line)),
        pltpu.SemaphoreType.DMA((2, count * line)),
        pltpu.SemaphoreType.DMA((count,)),
        pltpu.SemaphoreType.DMA((2, line)),
        pltpu.SemaphoreType.REGULAR((3,)),
        pltpu.VMEM((2 * tok_piece, pl_), F32),
        pltpu.VMEM((2 * tok_piece, ps), F32),
        pltpu.VMEM((line + 2, vec_rows, d), F32),
    ]
    if fused:
        reduced = (
            jax.ShapeDtypeStruct((piece, dc), F32),
            jax.ShapeDtypeStruct((piece, dc), F32),
            jax.ShapeDtypeStruct((2 * tok_piece, pl_), F32),
            jax.ShapeDtypeStruct((2 * tok_piece, ps), F32),
        )
    else:
        reduced = (
            jax.ShapeDtypeStruct((d, dc), BF16),
            jax.ShapeDtypeStruct((d, dc), BF16),
            jax.ShapeDtypeStruct((d, large_width), BF16),
            jax.ShapeDtypeStruct((d, small_width), BF16),
        )
    outs = (
        jax.ShapeDtypeStruct((n, ps, d), BF16),
        jax.ShapeDtypeStruct((n, pl_, d), BF16),
        jax.ShapeDtypeStruct((n, ps, d), BF16),
        jax.ShapeDtypeStruct((n, pl_, d), BF16),
        *reduced,
        jax.ShapeDtypeStruct((vec_rows, d), F32),
    )
    made_s, made_l, back_s, back_l, chan_a, chan_b, tok_l, tok_s, vec = pl.pallas_call(
        functools.partial(kernel, dims),
        out_shape=outs,
        in_specs=[any_] * 4
        + [smem] * 2
        + [any_, vmem, any_, vmem] * 2
        + [any_, vmem, any_, vmem]
        + [vmem, vmem],
        out_specs=(any_,) * 8 + (vmem,),
        scratch_shapes=scratch,
        compiler_params=pltpu.CompilerParams(
            collective_id=0, has_side_effects=True, vmem_limit_bytes=65400 * 1024
        ),
        cost_estimate=pl.CostEstimate(flops=50 * 10**9, bytes_accessed=40 * 10**6, transcendentals=10**7),
    )(
        small_images.reshape(n, ps, d),
        large_images.reshape(n, pl_, d),
        small_upstream.reshape(n, ps, d),
        large_upstream.reshape(n, pl_, d),
        small_keep.reshape(n, 2),
        large_keep.reshape(n, 2),
        small_in[0],
        small_bias,
        small_out[0].T,
        small_shift,
        large_in[0],
        large_bias,
        large_out[0].T,
        large_shift,
        channel_in[0],
        channel_bias,
        channel_out[0],
        channel_shift,
        norm_gain[0],
        norm_shift[0],
    )
    if fused:
        final = [jax.ShapeDtypeStruct((tok_piece, width), F32) for width in (pl_, pl_, ps, ps)]
        final += [
            jax.ShapeDtypeStruct(shape, F32)
            for shape in ((1, dc), (1, d), (2, d), (2, d), (1, ds_), (1, pl_), (1, ds_), (1, ps))
        ]
        lin, lout, sin, sout, cbias, cshift, gain, shift, lbias, lshift, sbias, sshift = pl.pallas_call(
            functools.partial(finish_kernel, tok_piece, d, chunks),
            out_shape=final,
            in_specs=[vmem] * 3,
            out_specs=[vmem] * 12,
        )(tok_l, tok_s, vec)
    else:
        chan_a, chan_b = (lax.psum_scatter(x, "dp", scatter_dimension=0, tiled=True).astype(F32) for x in (chan_a, chan_b))
        tok = jnp.concatenate([tok_l, tok_s], axis=1).reshape(2, ds_, large_width + small_width)
        tok = lax.psum_scatter(tok, "dp", scatter_dimension=1, tiled=True).astype(F32)
        lin, lout, sin, sout = tok[0, :, 0:pl_], tok[1, :, 0:pl_], tok[0, :, large_width:], tok[1, :, large_width:]
        sin, sout = sin[:, 0:ps], sout[:, 0:ps]
        vec = lax.psum(vec, "dp")
        at = chunks
        cbias, cshift = vec[0:at].reshape(1, dc), vec[at : at + 1]
        gain, shift = vec[at + 1 : at + 3], vec[at + 3 : at + 5]
        lbias, lshift = vec[at + 5 : at + 6, 0:ds_], vec[at + 6 : at + 7, 0:pl_]
        sbias, sshift = vec[at + 7 : at + 8, 0:ds_], vec[at + 8 : at + 9, 0:ps]
    return (
        made_s.reshape(1, micro, imgs, ps, d),
        made_l.reshape(1, micro, imgs, pl_, d),
        back_s.reshape(1, micro, imgs, ps, d),
        back_l.reshape(1, micro, imgs, pl_, d),
        sin.T[None],
        sbias,
        sout[None],
        sshift,
        lin.T[None],
        lbias,
        lout[None],
        lshift,
        chan_a[None],
        cbias,
        chan_b.T[None],
        cshift,
        gain[None],
        shift[None],
    )


def solution(mesh):
    placed = (
        (P(None, "dp", None, None),) * 4
        + (P("section", None, "dp", None),) * 2
        + (P("section", None, None), P("section", None)) * 6
        + (P("section", None, None),) * 2
    )
    outs = (
        (P("section", None, "dp", None, None),) * 4
        + (P("section", None, "dp"), P("section", None), P("section", "dp", None), P("section", None)) * 2
        + (P("section", "dp", None), P("section", None), P("section", None, "dp"), P("section", None))
        + (P("section", None, None),) * 2
    )
    return jax.shard_map(local, mesh=mesh, in_specs=placed, out_specs=outs, check_vma=False)
```

```python
import functools

import jax
import jax.numpy as jnp
from jax import lax
from jax.experimental import pallas as pl
from jax.experimental.pallas import tpu as pltpu
from jax.sharding import PartitionSpec as P

MESH = pl.DeviceIdType.MESH
F32 = jnp.float32
BF16 = jnp.bfloat16
EPSILON = 1e-06
DENSITY = 0.3989422804014327
ROWS = 144
COLS = 256
WIDE = 512


def up_to(value, step):
    return -(-value // step) * step


def mm(a, b, ca, cb):
    return lax.dot_general(a, b, (((ca,), (cb,)), ((), ())), preferred_element_type=F32)


def gelu_pair(v):
    cdf = 0.5 + 0.5 * lax.erf(v * 0.7071067811865476)
    bell = jnp.exp2((v * v) * (-0.5 * 1.4426950408889634))
    return v * cdf, cdf + (v * DENSITY) * bell


def groups(x):
    return x.reshape(x.shape[0] // 8, 8, x.shape[1]).sum(0)


def kernel(
    dims,
    small_images,
    large_images,
    small_upstream,
    large_upstream,
    small_keep,
    large_keep,
    small_in,
    small_bias,
    small_out,
    small_shift,
    large_in,
    large_bias,
    large_out,
    large_shift,
    channel_in,
    channel_bias,
    channel_out,
    channel_shift,
    norm_gain,
    norm_shift,
    small_made,
    large_made,
    small_back,
    large_back,
    chan_a,
    chan_b,
    tok_l,
    tok_s,
    vec_out,
    win,
    wout,
    hid,
    slope,
    xin,
    up,
    n1,
    n2,
    u2,
    r2,
    gb1,
    stage,
    h1,
    sl1,
    lgin,
    lgin_t,
    lgout,
    lgout_t,
    sgin,
    sgin_t,
    sgout,
    sgout_t,
    turned,
    lbcol,
    lscol,
    sbcol,
    sscol,
    mid,
    acc,
    raw_a,
    raw_b,
    sums,
    wsem,
    isem,
    usem,
    ysem,
    gsem,
    fs,
    fr,
    bs,
    br,
    sibs,
    rights,
    lefts,
    outsem,
    vsem,
    ready,
    lent,
    tl,
    ts,
    vecs,
    paired,
    pairs,
):
    sections, n, ps, pl_, pp, d, ds_, dc, dp, fused, shared = dims
    place = lax.axis_index("section")
    ahead = lax.rem(place + 1, sections)
    behind = lax.rem(place + sections - 1, sections)
    last = place // (sections - 1)
    first_rows = n * pl_
    half = pl_ // 2
    line = dp // 2 if fused else 1
    rank = lax.axis_index("dp")
    z = rank // 2
    core = rank % 2
    sibling = rank + 1 - 2 * core
    partner = (place + sections // 2) % sections
    giver = place < sections // 2
    taker = place >= sections // 2

    def weight_copies():
        pairs = (
            (large_in, lgin),
            (large_out, lgout_t),
            (small_in, raw_a.at[0, :, pl.ds(0, ds_)]),
            (small_out, raw_a.at[0, :, pl.ds(ds_, ds_)]),
            (channel_in, win),
            (channel_out, wout),
        )
        return [pltpu.make_async_copy(a, b, wsem.at[k]) for k, (a, b) in enumerate(pairs)]

    def large_copy(src, dst, sem, i):
        return pltpu.make_async_copy(src.at[i], dst.at[pl.ds(pl.multiple_of(i * pl_, 64), pl_)], sem.at[i])

    def small_copy(src, dst, sem, j):
        return pltpu.make_async_copy(src.at[j], dst.at[j], sem.at[n + j])

    copies = weight_copies()

    @pl.when(place == 0)
    def _():
        for i in range(n):
            large_copy(large_images, xin, isem, i).start()

    for c in copies:
        c.start()

    @pl.when(last == 1)
    def _():
        for i in range(n):
            large_copy(large_upstream, up, usem, i).start()
        for j in range(n):
            small_copy(small_upstream, raw_b, usem, j).start()

    barrier = pltpu.get_barrier_semaphore()

    @pl.when(place > 0)
    def _():
        pl.semaphore_signal(barrier, inc=1, device_id={"section": behind}, device_id_type=MESH)

    @pl.when(place < sections - 1)
    def _():
        pl.semaphore_signal(barrier, inc=1, device_id={"section": ahead}, device_id_type=MESH)

    peers = (place + sections - 2) // (sections - 1) + 1 - last
    if fused:
        pl.semaphore_signal(barrier, inc=1, device_id={"dp": sibling}, device_id_type=MESH)
        for k in range(1, line):
            pl.semaphore_signal(barrier, inc=1, device_id={"dp": (rank + 2 * k) % dp}, device_id_type=MESH)
        pl.semaphore_signal(barrier, inc=1, device_id={"section": partner}, device_id_type=MESH)
        peers = peers + line + 1
    pl.semaphore_wait(barrier, peers)

    def column(row, dst):
        width = up_to(dst.shape[0], 128)
        sums[0:1, 0:width] = jnp.zeros((1, width), F32)
        sums[0:1, 0 : row.shape[1]] = row
        dst[...] = jnp.transpose(jnp.broadcast_to(sums[0:1, 0:width], (128, width)))[0 : dst.shape[0]]

    column(large_bias[...], lbcol)
    column(large_shift[...], lscol)
    column(small_bias[...], sbcol)
    column(small_shift[...], sscol)
    sums[...] = jnp.zeros(sums.shape, F32)
    for c in copies[:4]:
        c.wait()
    for k, padded in enumerate((sgin, sgout_t)):
        padded[...] = jnp.zeros(padded.shape, BF16)
        padded[0:ps, :] = raw_a[0, :, k * ds_ : (k + 1) * ds_]

    @pl.when(place == 0)
    def _():
        for j in range(n):
            small_copy(small_images, raw_a, isem, j).start()

    lgin_t[...] = jnp.transpose(lgin[...])
    lgout[...] = jnp.transpose(lgout_t[...])
    sgin_t[...] = jnp.transpose(sgin[...])
    sgout[...] = jnp.transpose(sgout_t[...])

    gains = norm_gain[...]
    shifts = norm_shift[...]

    def ahead_copy(rows, size, k):
        return pltpu.make_async_remote_copy(
            src_ref=stage.at[pl.ds(rows, size)],
            dst_ref=xin.at[pl.ds(rows, size)],
            send_sem=fs.at[k],
            recv_sem=fr.at[k],
            device_id={"section": ahead},
            device_id_type=MESH,
        )

    def behind_copy(rows, size, k):
        return pltpu.make_async_remote_copy(
            src_ref=stage.at[pl.ds(rows, size)],
            dst_ref=up.at[pl.ds(rows, size)],
            send_sem=bs.at[k],
            recv_sem=br.at[k],
            device_id={"section": behind},
            device_id_type=MESH,
        )

    class Unit:
        def __init__(self, large, i):
            self.large = large
            self.i = i
            self.rows = pl_ if large else pp
            self.blocks = 2 if large else 1
            self.size = self.rows // self.blocks
            self.some = ROWS if large else pp
            self.base = pl.multiple_of(i * pl_, 64) if large else pl.multiple_of(first_rows + i * pp, 16)
            self.head = pl.multiple_of((i if large else n + i) * ds_, 128)
            self.heads = pl.ds(self.head, ds_)
            self.slot = i * 2 if large else 2 * n + i
            self.gin, self.gin_t = (lgin, lgin_t) if large else (sgin, sgin_t)
            self.gout, self.gout_t = (lgout, lgout_t) if large else (sgout, sgout_t)
            self.bcol, self.scol = (lbcol, lscol) if large else (sbcol, sscol)
            self.mask = large_keep if large else small_keep

        def at(self, offset, size):
            return pl.ds(pl.multiple_of(self.base + offset, 16), size)

        def keep(self, which):
            return self.mask[self.i, which].astype(F32)

        def out_copy(self, which, b):
            sem = (ysem, gsem)[which].at[self.slot + b]
            if self.large:
                dst = (large_made, large_back)[which]
                return pltpu.make_async_copy(
                    stage.at[self.at(b * half, half)], dst.at[self.i, pl.ds(b * half, half)], sem
                )
            src = (raw_a, raw_b)[which]
            dst = (small_made, small_back)[which]
            return pltpu.make_async_copy(src.at[self.i], dst.at[self.i], sem)

    units = 2 * n

    def unit_at(which):
        return (which + core) % 2, which // 2

    def forward(unit, step):
        @pl.when(place == 0)
        def _():
            if unit.large:
                large_copy(large_images, xin, isem, unit.i).wait()
            else:
                small_copy(small_images, raw_a, isem, unit.i).wait()
                xin[unit.at(0, pp)] = jnp.zeros((pp, d), BF16)
                xin[unit.at(0, ps)] = raw_a[unit.i]

        def norm_one(r):
            rows = unit.at(r * unit.some, unit.some)
            x = xin[rows].astype(F32)
            x = x - jnp.mean(x, axis=1, keepdims=True)
            s = lax.rsqrt(jnp.mean(x * x, axis=1, keepdims=True) + EPSILON)
            n1[rows] = (x * s * gains[0:1] + shifts[0:1]).astype(BF16)

        steps = unit.size // unit.some
        for b in range(unit.blocks):

            @pl.when(place > 0)
            def _(b=b):
                ahead_copy(unit.base + b * unit.size, unit.size, unit.slot + b).wait_recv()

            for r in range(b * steps, (b + 1) * steps):
                norm_one(r)
        rows = unit.at(0, unit.rows)
        keep_one = unit.keep(0)
        keep_two = unit.keep(1)
        for c in range(0, d, COLS):
            pre = mm(unit.gin_t[...], n1[rows, c : c + COLS], 1, 0) + unit.bcol[:, 0:1]
            act, slp = gelu_pair(pre)
            h1[unit.heads, c : c + COLS] = act.astype(BF16)
            sl1[unit.heads, c : c + COLS] = slp.astype(BF16)
        for c in range(0, d, COLS):
            branch = mm(unit.gout_t[...], h1[unit.heads, c : c + COLS], 1, 0) + unit.scol[:, 0:1]
            mid[0 : unit.rows, c : c + COLS] = xin[rows, c : c + COLS].astype(F32) + keep_one * branch

        def norm_two(r):
            rows = unit.at(r * unit.some, unit.some)
            x = mid[r * unit.some : (r + 1) * unit.some]
            x = x - jnp.mean(x, axis=1, keepdims=True)
            s = lax.rsqrt(jnp.mean(x * x, axis=1, keepdims=True) + EPSILON)
            x = x * s
            u2[rows] = x.astype(BF16)
            r2[rows] = jnp.broadcast_to(s, (unit.some, 128))
            n2[rows] = (x * gains[1:2] + shifts[1:2]).astype(BF16)

        for r in range(unit.rows // unit.some):
            norm_two(r)

        @pl.when(step == 0)
        def _():
            for c in copies[4:]:
                c.wait()

        for b in range(unit.blocks):
            size = unit.size
            rows = unit.at(b * size, size)
            here = slice(b * size, (b + 1) * size)
            total = channel_shift[...]
            parts = [slice(c, c + WIDE) for c in range(0, dc, WIDE)]
            ahead_of = mm(n2[rows], win[:, parts[0]], 1, 0)
            for c, cols in enumerate(parts):
                pre = ahead_of + channel_bias[:, cols]
                if c + 1 < len(parts):
                    ahead_of = mm(n2[rows], win[:, parts[c + 1]], 1, 0)
                act, slp = gelu_pair(pre)
                act = act.astype(BF16)
                hid[rows, cols] = act
                slope[rows, cols] = slp.astype(BF16)
                total = total + mm(act, wout[cols, :], 1, 0)
            y = (mid[here] + keep_two * total).astype(BF16)
            stage[rows] = y
            if not unit.large:
                raw_a[unit.i] = y[0:ps]

            @pl.when(place < sections - 1)
            def _(b=b, size=size):
                ahead_copy(unit.base + b * size, size, unit.slot + b).start()

            if unit.large or not fused:
                unit.out_copy(0, b).start()

    def backward(unit):
        @pl.when(last == 1)
        def _():
            if unit.large:
                large_copy(large_upstream, up, usem, unit.i).wait()
            else:
                small_copy(small_upstream, raw_b, usem, unit.i).wait()
                up[unit.at(0, pp)] = jnp.zeros((pp, d), BF16)
                up[unit.at(0, ps)] = raw_b[unit.i]

        keep_one = unit.keep(0)
        keep_two = unit.keep(1)
        size = unit.size
        for b in range(unit.blocks):
            rows = unit.at(b * size, size)
            here = slice(b * size, (b + 1) * size)

            @pl.when(place < sections - 1)
            def _(b=b):
                ahead_copy(unit.base + b * size, size, unit.slot + b).wait_send()

            if unit.large or not fused:
                unit.out_copy(0, b).wait()

            @pl.when(last == 0)
            def _(b=b):
                behind_copy(unit.base + b * size, size, unit.slot + b).wait_recv()

            stage[rows] = up[rows] * keep_two.astype(BF16)

            parts = [slice(c, c + WIDE) for c in range(0, dc, WIDE)]
            total = None
            ahead_of = mm(stage[rows], wout[parts[0], :], 1, 1)
            for c, cols in enumerate(parts):
                grad = ahead_of
                if c + 1 < len(parts):
                    ahead_of = mm(stage[rows], wout[parts[c + 1], :], 1, 1)
                grad = (grad * slope[rows, cols].astype(F32)).astype(BF16)
                slope[rows, cols] = grad
                term = mm(grad, win[:, cols], 1, 1)
                total = term if total is None else total + term
            acc[here] = total

        def norm_two(r):
            offset = r * unit.some
            rows = unit.at(offset, unit.some)
            local = slice(offset, offset + unit.some)
            h = acc[local]
            u = u2[rows].astype(F32)
            s = r2[rows][:, 0:1]
            g = up[rows].astype(F32)
            q = h * gains[1:2]
            first = jnp.mean(q, axis=1, keepdims=True)
            second = jnp.mean(q * u, axis=1, keepdims=True)
            g_mid = g + s * (q - first - u * second)
            mid[local] = g_mid
            gb1[rows] = (keep_one * g_mid).astype(BF16)
            up[rows] = (keep_two * g).astype(BF16)
            return groups(h * u), groups(h)

        parts = [norm_two(r) for r in range(unit.rows // unit.some)]
        sums[8:16, 0:d] += sum(p[0] for p in parts)
        sums[24:32, 0:d] += sum(p[1] for p in parts)
        rows = unit.at(0, unit.rows)
        for c in range(0, d, COLS):
            grad = mm(unit.gout[...], gb1[rows, c : c + COLS], 1, 0)
            grad = (grad * sl1[unit.heads, c : c + COLS].astype(F32)).astype(BF16)
            sl1[unit.heads, c : c + COLS] = grad
        for c in range(0, d, COLS):
            acc[0 : unit.rows, c : c + COLS] = mm(unit.gin[...], sl1[unit.heads, c : c + COLS], 1, 0)

        def norm_one(r):
            offset = r * unit.some
            rows = unit.at(offset, unit.some)
            local = slice(offset, offset + unit.some)
            x = xin[rows].astype(F32)
            x = x - jnp.mean(x, axis=1, keepdims=True)
            s = lax.rsqrt(jnp.mean(x * x, axis=1, keepdims=True) + EPSILON)
            u = x * s
            h = acc[local]
            q = h * gains[0:1]
            first = jnp.mean(q, axis=1, keepdims=True)
            second = jnp.mean(q * u, axis=1, keepdims=True)
            stage[rows] = (mid[local] + s * (q - first - u * second)).astype(BF16)
            return groups(h * u), groups(h)

        steps = size // unit.some
        for b in range(unit.blocks):
            parts = [norm_one(r) for r in range(b * steps, (b + 1) * steps)]
            sums[0:8, 0:d] += sum(p[0] for p in parts)
            sums[16:24, 0:d] += sum(p[1] for p in parts)
            if not unit.large:
                raw_b[unit.i] = stage[unit.at(0, ps)]

            @pl.when(place > 0)
            def _(b=b):
                behind_copy(unit.base + b * size, size, unit.slot + b).start()

            if unit.large or not fused:
                unit.out_copy(1, b).start()

    piece = d // dp
    tok_piece = ds_ // dp

    def turn(src):
        def some(rows, size):
            value = jnp.transpose(src[pl.ds(rows, size)])
            if not fused:
                turned[:, pl.ds(rows, size)] = value
                return
            for b in range(dp):
                at = ((b % 2) * line + b // 2) * piece
                turned[at : at + piece, pl.ds(rows, size)] = value[b * piece : (b + 1) * piece]

        def full(r, carry):
            some(pl.multiple_of(r * 128, 128), 128)
            return carry

        whole = src.shape[0] // 128
        lax.fori_loop(0, whole, full, 0)
        if src.shape[0] % 128:
            some(whole * 128, src.shape[0] % 128)


    def step(t, carry):
        back = (1 - last) * (t // units) + last * (t % 2)
        which = (1 - last) * (t % units) + last * (t // 2)
        small, i = unit_at(which)

        @pl.when(t == 2 * units - 1)
        def _():
            turn(n2)

        @pl.when((back == 0) & (small == 0))
        def _():
            forward(Unit(True, i), t)

        @pl.when((back == 0) & (small == 1))
        def _():
            forward(Unit(False, i), t)

        @pl.when((back == 1) & (small == 0))
        def _():
            backward(Unit(True, i))

        @pl.when((back == 1) & (small == 1))
        def _():
            backward(Unit(False, i))

        return carry

    lax.fori_loop(0, 2 * units, step, 0)

    total = hid.shape[0]
    chunks = dc // d
    count = 2 * chunks + 2
    kinds = (chunks, chunks, 1, 1, shared)
    first_of = (0, chunks + 2, chunks, chunks + 1, count + 1)
    large_width, small_width = up_to(pl_, 128), up_to(pp, 128)
    widths = (d, d, large_width, small_width, d)
    own = line
    across = line + 1

    def columns(kind, k):
        if kind < 2:
            return pl.ds(pl.multiple_of(k * d, 128), d)
        return pl.ds(0, widths[kind])

    def own_rows(kind):
        return ((slope, 0), (hid, 0), (up, 0), (up, d))[kind]

    def weight_product(kind, k):
        src = (slope, hid)[kind]

        def part(j, carry):
            cols = pl.ds(pl.multiple_of(k * d + j * COLS, COLS), COLS)
            if kind == 0:
                bias = mm(jnp.ones((8, total), BF16), src[:, cols], 1, 0)[0:1]
                vecs[own, pl.ds(k, 1), pl.ds(pl.multiple_of(j * COLS, COLS), COLS)] = bias
            src[0:d, cols] = mm(turned[...], src[:, cols], 1, 0).astype(BF16)
            return carry

        lax.fori_loop(0, d // COLS, part, 0)

    def token_product(large):
        unit_rows = pl_ if large else pp
        ones_d = jnp.ones((8, d), BF16)
        out_grad = in_grad = bias = shift = None
        for k in range(n):
            base = k * pl_ if large else first_rows + k * pp
            head = k * ds_ if large else (n + k) * ds_
            g = gb1[base : base + unit_rows]
            x = n1[base : base + unit_rows]
            h = h1[head : head + ds_]
            p = sl1[head : head + ds_]
            terms = (mm(p, x, 1, 1), mm(h, g, 1, 1), mm(ones_d, p, 1, 1), mm(ones_d, g, 1, 1))
            if k == 0:
                in_grad, out_grad, bias, shift = terms
            else:
                in_grad, out_grad, bias, shift = in_grad + terms[0], out_grad + terms[1], bias + terms[2], shift + terms[3]
        src, base = own_rows(2 if large else 3)
        for at, value in ((0, in_grad), (1, out_grad)):
            value = value.astype(BF16)
            if not fused:
                src[base + at * ds_ : base + (at + 1) * ds_, 0:unit_rows] = value
                continue
            for b in range(dp):
                to = base + ((b % 2) * line + b // 2) * piece + at * tok_piece
                src[to : to + tok_piece, 0:unit_rows] = value[b * tok_piece : (b + 1) * tok_piece]
        row = chunks + 5 + (0 if large else 2)
        vecs[own, row : row + 1, 0:ds_] = bias[0:1]
        vecs[own, row + 1 : row + 2, 0:unit_rows] = shift[0:1]

    def product(kind, k):
        if kind == 2:
            turn(up)
            vecs[own, chunks : chunks + 1] = mm(jnp.ones((8, total), BF16), up[...], 1, 0)[0:1]
            for j in range(4):
                vecs[own, chunks + 1 + j : chunks + 2 + j] = jnp.sum(sums[8 * j : 8 * j + 8], axis=0, keepdims=True)
        if kind < 2:
            weight_product(kind, k)
        else:
            token_product(kind == 2)

    def ways(step_of, kept=False):
        def at(c, valid=True):
            for kind in range(5 if fused else 4):
                low, high = first_of[kind], first_of[kind] + kinds[kind]
                here = (c >= low) & (c < high) & valid
                if kind == 4:
                    here = here & taker
                if kind == 0 and kept:
                    here = here & (taker | (c < 1) | (c > shared))

                @pl.when(here)
                def _(kind=kind, low=low):
                    step_of(kind, c - low)

        return at

    vecs[own] = jnp.zeros(vecs.shape[1:], F32)
    if not fused:

        def whole_copies(kind, k):
            src, base = own_rows(kind)
            if kind < 2:
                cols = columns(kind, k)
                dst = (chan_a, chan_b)[kind]
                return [pltpu.make_async_copy(src.at[pl.ds(0, d), cols], dst.at[:, cols], outsem.at[first_of[kind] + k])]
            cols = pl.ds(0, widths[kind])
            dst = (tok_l, tok_s)[kind - 2]
            return [pltpu.make_async_copy(src.at[pl.ds(base, d), cols], dst, outsem.at[first_of[kind]])]

        def one(kind, k):
            product(kind, k)
            for c in whole_copies(kind, k):
                c.start()

        def finish(kind, k):
            for c in whole_copies(kind, k):
                c.wait()

        def run(c, carry):
            ways(one)(c)
            return carry

        def end(c, carry):
            ways(finish)(c)
            return carry

        lax.fori_loop(0, count, run, 0)
        lax.fori_loop(0, count, end, 0)
        vec_out[...] = vecs[own]
    else:
        rightward, leftward = (rank + 2) % dp, (rank + dp - 2) % dp

        def mine(kind, k, to):
            if kind == 4:
                return h1.at[pl.ds(pl.multiple_of((k * line + to) * piece, 16), piece)]
            src, base = own_rows(kind)
            return src.at[pl.ds(pl.multiple_of(base + (core * line + to) * piece, 16), piece), columns(kind, k)]

        def crossing(kind, k, rows, size):
            ref, base = ((win, 0), (win, d // 2), (wout, 3 * d), (wout, 3 * d + d // 2))[kind]
            return ref.at[pl.ds(pl.multiple_of(base + rows, 16), size), columns(kind, k)]

        def from_left(kind, k, to):
            ref, base = ((wout, 0), (wout, chunks * (line - 1)), (n2, 0), (n2, line - 1), (sl1, 0))[kind]
            rows = (base + k * (line - 1) + to - 1) * piece
            return ref.at[pl.ds(pl.multiple_of(rows, 16), piece), pl.ds(0, widths[kind])]

        def from_right(kind, k, to):
            ref, base = ((xin, 0), (u2, 0), (n2, 2 * (line - 1)), (n2, 3 * (line - 1)), (sl1, shared * (line - 1)))[kind]
            rows = (base + k * (line - 1) + to) * piece
            return ref.at[pl.ds(pl.multiple_of(rows, 16), piece), pl.ds(0, widths[kind])]

        def sem_of(kind, k, to):
            return ((count if kind == 4 else first_of[kind]) + k) * line + to

        def cross_copy(kind, k):
            src, base = own_rows(kind)
            rows = pl.ds(pl.multiple_of(base + (1 - core) * line * piece, 16), line * piece)
            c = first_of[kind] + k
            return pltpu.make_async_remote_copy(
                src_ref=src.at[rows, columns(kind, k)],
                dst_ref=crossing(kind, k, 0, line * piece),
                send_sem=sibs.at[0, c],
                recv_sem=sibs.at[1, c],
                device_id={"dp": sibling},
                device_id_type=MESH,
            )

        def right_copy(kind, k, to):
            return pltpu.make_async_remote_copy(
                src_ref=mine(kind, k, to),
                dst_ref=from_left(kind, k, to),
                send_sem=rights.at[0, sem_of(kind, k, to)],
                recv_sem=rights.at[1, sem_of(kind, k, to)],
                device_id={"dp": rightward},
                device_id_type=MESH,
            )

        def left_copy(kind, k, to):
            return pltpu.make_async_remote_copy(
                src_ref=mine(kind, k, to),
                dst_ref=from_right(kind, k, to),
                send_sem=lefts.at[0, sem_of(kind, k, to)],
                recv_sem=lefts.at[1, sem_of(kind, k, to)],
                device_id={"dp": leftward},
                device_id_type=MESH,
            )

        def chip_sum(kind, k, to):
            if kind == 4:
                return mine(kind, k, to)[...].astype(F32)
            return mine(kind, k, to)[...].astype(F32) + crossing(kind, k, to * piece, piece)[...].astype(F32)

        def flow_right(kind, k):
            def one(j, carry):
                to = line - 1 - j

                @pl.when(z == 0)
                def _():
                    mine(kind, k, to)[...] = chip_sum(kind, k, to).astype(BF16)

                @pl.when(z > 0)
                def _():
                    right_copy(kind, k, to).wait_recv()
                    value = chip_sum(kind, k, to) + from_left(kind, k, to)[...].astype(F32)
                    mine(kind, k, to)[...] = value.astype(BF16)

                right_copy(kind, k, to).start()
                return carry

            lax.fori_loop(0, line - 1 - z, one, 0)

        def flow_left(kind, k):
            def one(to, carry):
                @pl.when(z == line - 1)
                def _():
                    mine(kind, k, to)[...] = chip_sum(kind, k, to).astype(BF16)

                @pl.when(z < line - 1)
                def _():
                    left_copy(kind, k, to).wait_recv()
                    value = chip_sum(kind, k, to) + from_right(kind, k, to)[...].astype(F32)
                    mine(kind, k, to)[...] = value.astype(BF16)

                left_copy(kind, k, to).start()
                return carry

            lax.fori_loop(0, z, one, 0)

        def out_stage(kind, k):
            if kind == 0:
                return mid.at[pl.ds(pl.multiple_of(k * piece, 16), piece)]
            if kind in (1, 4):
                at = k + (chunks if kind == 4 else 0)
                return acc.at[pl.ds(pl.multiple_of(at * piece, 16), piece)]
            return (tl, ts)[kind - 2]

        def out_copies(kind, k):
            c = first_of[kind] + k
            if kind < 2:
                dst = (chan_a, chan_b)[kind].at[:, columns(kind, k)]
            else:
                dst = (tok_l, tok_s)[kind - 2]
            return pltpu.make_async_copy(out_stage(kind, k), dst, outsem.at[c])

        def gather(kind, k):
            width = (d, d, pl_, ps, d)[kind]
            dst = out_stage(kind, k)
            dst[...] = chip_sum(kind, k, z)[:, 0:width]

            @pl.when(z > 0)
            def _():
                right_copy(kind, k, z).wait_recv()
                dst[...] += from_left(kind, k, z)[...].astype(F32)[:, 0:width]

            @pl.when(z < line - 1)
            def _():
                left_copy(kind, k, z).wait_recv()
                dst[...] += from_right(kind, k, z)[...].astype(F32)[:, 0:width]

            if kind == 4:
                return_copy(k).start()
            else:
                out_copies(kind, k).start()

        def lend_copy(k):
            rows = pl.ds(pl.multiple_of(core * line * piece, 16), line * piece)
            return pltpu.make_async_remote_copy(
                src_ref=slope.at[rows, columns(0, k + 1)],
                dst_ref=h1.at[pl.ds(pl.multiple_of(k * line * piece, 16), line * piece)],
                send_sem=lent.at[0, k],
                recv_sem=lent.at[1, k],
                device_id={"section": partner},
                device_id_type=MESH,
            )

        def return_copy(k):
            return pltpu.make_async_remote_copy(
                src_ref=out_stage(4, k),
                dst_ref=out_stage(0, k + 1),
                send_sem=lent.at[2, k],
                recv_sem=lent.at[3, k],
                device_id={"section": partner},
                device_id_type=MESH,
            )

        def lend(c):
            @pl.when(giver & (c >= 1) & (c <= shared))
            def _():
                @pl.when(c == 1)
                def _():
                    pl.semaphore_wait(ready.at[3], 1)

                def one(to, carry):
                    mine(0, c, to)[...] = chip_sum(0, c, to).astype(BF16)
                    return carry

                lax.fori_loop(0, line, one, 0)
                lend_copy(c - 1).start()

        def pair_copy(which):
            return pltpu.make_async_copy(paired, (small_made, small_back)[which], pairs.at[which])

        def pair(which):
            if which:
                pair_copy(0).wait()
            src = (raw_a, raw_b)[which]
            for r in range(0, ps, 32):
                rows = slice(r, min(r + 32, ps))
                images = [src[j, rows].astype(F32)[:, None, :] for j in range(n)]
                paired[rows] = jnp.concatenate(images, axis=1).astype(BF16)
            pair_copy(which).start()

        def vec_cross():
            return pltpu.make_async_remote_copy(
                src_ref=vecs.at[own],
                dst_ref=vecs.at[across],
                send_sem=vsem.at[0, 0],
                recv_sem=vsem.at[1, 0],
                device_id={"dp": sibling},
                device_id_type=MESH,
            )

        def vec_copy(k):
            return pltpu.make_async_remote_copy(
                src_ref=vecs.at[z],
                dst_ref=vecs.at[z],
                send_sem=vsem.at[0, k],
                recv_sem=vsem.at[1, k],
                device_id={"dp": (rank + 2 * k) % dp},
                device_id_type=MESH,
            )

        def first(kind, k):
            if kind == 4:

                @pl.when(k == 0)
                def _():
                    @pl.when(z < line - 1)
                    def _():
                        pl.semaphore_wait(ready.at[4], 1)

                    @pl.when(z > 0)
                    def _():
                        pl.semaphore_wait(ready.at[5], 1)

                lend_copy(k).wait_recv()
                return
            product(kind, k)
            if kind == 3:

                @pl.when(taker)
                def _():
                    pl.semaphore_signal(ready.at[3], inc=1, device_id={"section": partner}, device_id_type=MESH)

                    @pl.when(z > 0)
                    def _():
                        pl.semaphore_signal(ready.at[4], inc=1, device_id={"dp": leftward}, device_id_type=MESH)

                    @pl.when(z < line - 1)
                    def _():
                        pl.semaphore_signal(ready.at[5], inc=1, device_id={"dp": rightward}, device_id_type=MESH)

            if kind == 0:

                @pl.when(k == 0)
                def _():
                    pl.semaphore_wait(ready.at[0], 1)

                    @pl.when(z < line - 1)
                    def _():
                        pl.semaphore_wait(ready.at[1], 1)

                    @pl.when(z > 0)
                    def _():
                        pl.semaphore_wait(ready.at[2], 1)

            cross_copy(kind, k).start()

        def crossed(kind, k):
            if kind < 4:
                cross_copy(kind, k).wait_recv()

        def finish(kind, k):
            if kind == 4:
                return_copy(k).wait_send()
            else:
                cross_copy(kind, k).wait_send()
                out_copies(kind, k).wait()

            def right(j, carry):
                right_copy(kind, k, line - 1 - j).wait_send()
                return carry

            def left(to, carry):
                left_copy(kind, k, to).wait_send()
                return carry

            sent = line - 1 - z, z
            if kind == 0:
                away = giver & (k >= 1) & (k <= shared)
                own_line = 1 - away.astype(jnp.int32)
                sent = sent[0] * own_line, sent[1] * own_line
            lax.fori_loop(0, sent[0], right, 0)
            lax.fori_loop(0, sent[1], left, 0)

        pl.semaphore_signal(ready.at[0], inc=1, device_id={"dp": sibling}, device_id_type=MESH)

        @pl.when(z > 0)
        def _():
            pl.semaphore_signal(ready.at[1], inc=1, device_id={"dp": leftward}, device_id_type=MESH)

        @pl.when(z < line - 1)
        def _():
            pl.semaphore_signal(ready.at[2], inc=1, device_id={"dp": rightward}, device_id_type=MESH)

        def run(c, carry):
            ways(crossed)(c - 1)
            lend(c - 1)
            ways(flow_right, True)(c - 1 - z, z < line - 1)
            ways(flow_left, True)(c - line + z, z > 0)
            ways(first)(c)

            @pl.when(c == count)
            def _():
                vec_cross().start()

            @pl.when(c == count + 1)
            def _():
                vec_cross().wait()
                vecs[z] = vecs[own] + vecs[across]
                for k in range(1, line):
                    vec_copy(k).start()

            for which in range(2):

                @pl.when(c == count - 2 + which)
                def _(which=which):
                    pair(which)

            ways(gather, True)(c - line - 1)
            return carry

        steps = count + 1 + shared
        lax.fori_loop(0, steps + line + 1, run, 0)

        @pl.when(giver)
        def _():
            for k in range(shared):
                lend_copy(k).wait_send()
                return_copy(k).wait_recv()
                out_copies(0, k + 1).start()

        def end(c, carry):
            ways(finish)(c)
            return carry

        lax.fori_loop(0, steps, end, 0)
        pair_copy(1).wait()
        for k in range(1, line):
            vec_copy(k).wait()
        value = vecs[0]
        for k in range(1, line):
            value = value + vecs[k]
        vec_out[...] = value

    for i in range(2 * n):
        unit = Unit(i < n, i % n)
        for b in range(unit.blocks):
            if unit.large or not fused:
                unit.out_copy(1, b).wait()

            @pl.when(place > 0)
            def _(b=b, unit=unit):
                behind_copy(unit.base + b * unit.size, unit.size, unit.slot + b).wait_send()


def finish_kernel(tok_piece, d, chunks, tok_l, tok_s, vec, *outs):
    for k, src in enumerate((tok_l, tok_s)):
        outs[2 * k][...] = src[0:tok_piece]
        outs[2 * k + 1][...] = src[tok_piece:]
    for k in range(chunks):
        outs[4][:, k * d : (k + 1) * d] = vec[k : k + 1]
    at = chunks
    for out in outs[5:]:
        rows, width = out.shape
        out[...] = vec[at : at + rows, 0:width]
        at += rows


def local(
    small_images,
    large_images,
    small_upstream,
    large_upstream,
    small_keep,
    large_keep,
    small_in,
    small_bias,
    small_out,
    small_shift,
    large_in,
    large_bias,
    large_out,
    large_shift,
    channel_in,
    channel_bias,
    channel_out,
    channel_shift,
    norm_gain,
    norm_shift,
):
    sections = lax.axis_size("section")
    micro, imgs, ps, d = small_images.shape
    pl_ = large_images.shape[2]
    n = micro * imgs
    ds_ = small_in.shape[2]
    dc = channel_in.shape[2]
    pp = up_to(ps, 16)
    rows = n * (pl_ + pp)
    small_width, large_width = up_to(pp, 128), up_to(pl_, 128)
    dp = lax.axis_size("dp")
    piece, tok_piece = d // dp, ds_ // dp
    fused = d % (16 * dp) == 0 and ds_ % (16 * dp) == 0 and dc == 4 * d and d == 2 * ds_ and 2 * dp * piece <= rows
    fused = fused and sections % 2 == 0 and sections > 2
    shared = 2
    dims = (sections, n, ps, pl_, pp, d, ds_, dc, dp, fused, shared)
    chunks = dc // d
    line = dp // 2 if fused else 1
    count = 2 * chunks + 2
    vec_rows = up_to(chunks + 9, 8)
    any_ = pl.BlockSpec(memory_space=pl.ANY)
    vmem = pl.BlockSpec(memory_space=pltpu.VMEM)
    smem = pl.BlockSpec(memory_space=pltpu.SMEM)
    block = max(pl_, n * pp)
    blocks = 2 * n + n
    scratch = [
        pltpu.VMEM((d, dc), BF16),
        pltpu.VMEM((dc, d), BF16),
        pltpu.VMEM((rows, dc), BF16),
        pltpu.VMEM((rows, dc), BF16),
        pltpu.VMEM((rows, d), BF16),
        pltpu.VMEM((rows, d), BF16),
        pltpu.VMEM((rows, d), BF16),
        pltpu.VMEM((rows, d), BF16),
        pltpu.VMEM((rows, d), BF16),
        pltpu.VMEM((rows, 128), F32),
        pltpu.VMEM((rows, d), BF16),
        pltpu.VMEM((rows, d), BF16),
        pltpu.VMEM((2 * n * ds_, d), BF16),
        pltpu.VMEM((2 * n * ds_, d), BF16),
        pltpu.VMEM((pl_, ds_), BF16),
        pltpu.VMEM((ds_, pl_), BF16),
        pltpu.VMEM((ds_, pl_), BF16),
        pltpu.VMEM((pl_, ds_), BF16),
        pltpu.VMEM((pp, ds_), BF16),
        pltpu.VMEM((ds_, pp), BF16),
        pltpu.VMEM((ds_, pp), BF16),
        pltpu.VMEM((pp, ds_), BF16),
        pltpu.VMEM((d, rows), BF16),
        pltpu.VMEM((ds_, 128), F32),
        pltpu.VMEM((pl_, 128), F32),
        pltpu.VMEM((ds_, 128), F32),
        pltpu.VMEM((pp, 128), F32),
        pltpu.VMEM((block, d), F32),
        pltpu.VMEM((block, d), F32),
        pltpu.VMEM((n, ps, d), BF16),
        pltpu.VMEM((n, ps, d), BF16),
        pltpu.VMEM((32, d), F32),
        pltpu.SemaphoreType.DMA((6,)),
        pltpu.SemaphoreType.DMA((2 * n,)),
        pltpu.SemaphoreType.DMA((2 * n,)),
        pltpu.SemaphoreType.DMA((blocks,)),
        pltpu.SemaphoreType.DMA((blocks,)),
        pltpu.SemaphoreType.DMA((blocks,)),
        pltpu.SemaphoreType.DMA((blocks,)),
        pltpu.SemaphoreType.DMA((blocks,)),
        pltpu.SemaphoreType.DMA((blocks,)),
        pltpu.SemaphoreType.DMA((2, count)),
        pltpu.SemaphoreType.DMA((2, (count + shared) * line)),
        pltpu.SemaphoreType.DMA((2, (count + shared) * line)),
        pltpu.SemaphoreType.DMA((count,)),
        pltpu.SemaphoreType.DMA((2, line)),
        pltpu.SemaphoreType.REGULAR((6,)),
        pltpu.SemaphoreType.DMA((4, shared)),
        pltpu.VMEM((2 * tok_piece, pl_), F32),
        pltpu.VMEM((2 * tok_piece, ps), F32),
        pltpu.VMEM((line + 2, vec_rows, d), F32),
        pltpu.VMEM((ps, n, d) if fused else (8, 128), BF16),
        pltpu.SemaphoreType.DMA((2,)),
    ]
    if fused:
        reduced = (
            jax.ShapeDtypeStruct((piece, dc), F32),
            jax.ShapeDtypeStruct((piece, dc), F32),
            jax.ShapeDtypeStruct((2 * tok_piece, pl_), F32),
            jax.ShapeDtypeStruct((2 * tok_piece, ps), F32),
        )
    else:
        reduced = (
            jax.ShapeDtypeStruct((d, dc), BF16),
            jax.ShapeDtypeStruct((d, dc), BF16),
            jax.ShapeDtypeStruct((d, large_width), BF16),
            jax.ShapeDtypeStruct((d, small_width), BF16),
        )
    small_shape = (ps, n, d) if fused else (n, ps, d)
    outs = (
        jax.ShapeDtypeStruct(small_shape, BF16),
        jax.ShapeDtypeStruct((n, pl_, d), BF16),
        jax.ShapeDtypeStruct(small_shape, BF16),
        jax.ShapeDtypeStruct((n, pl_, d), BF16),
        *reduced,
        jax.ShapeDtypeStruct((vec_rows, d), F32),
    )
    made_s, made_l, back_s, back_l, chan_a, chan_b, tok_l, tok_s, vec = pl.pallas_call(
        functools.partial(kernel, dims),
        out_shape=outs,
        in_specs=[any_] * 4
        + [smem] * 2
        + [any_, vmem, any_, vmem] * 2
        + [any_, vmem, any_, vmem]
        + [vmem, vmem],
        out_specs=(any_,) * 8 + (vmem,),
        scratch_shapes=scratch,
        compiler_params=pltpu.CompilerParams(
            collective_id=0, has_side_effects=True, vmem_limit_bytes=65400 * 1024
        ),
        cost_estimate=pl.CostEstimate(flops=50 * 10**9, bytes_accessed=40 * 10**6, transcendentals=10**7),
    )(
        small_images.reshape(n, ps, d),
        large_images.reshape(n, pl_, d),
        small_upstream.reshape(n, ps, d),
        large_upstream.reshape(n, pl_, d),
        small_keep.reshape(n, 2),
        large_keep.reshape(n, 2),
        small_in[0],
        small_bias,
        small_out[0].T,
        small_shift,
        large_in[0],
        large_bias,
        large_out[0].T,
        large_shift,
        channel_in[0],
        channel_bias,
        channel_out[0],
        channel_shift,
        norm_gain[0],
        norm_shift[0],
    )
    if fused:
        final = [jax.ShapeDtypeStruct((tok_piece, width), F32) for width in (pl_, pl_, ps, ps)]
        final += [
            jax.ShapeDtypeStruct(shape, F32)
            for shape in ((1, dc), (1, d), (2, d), (2, d), (1, ds_), (1, pl_), (1, ds_), (1, ps))
        ]
        lin, lout, sin, sout, cbias, cshift, gain, shift, lbias, lshift, sbias, sshift = pl.pallas_call(
            functools.partial(finish_kernel, tok_piece, d, chunks),
            out_shape=final,
            in_specs=[vmem] * 3,
            out_specs=[vmem] * 12,
        )(tok_l, tok_s, vec)
        made_s, back_s = (x.transpose(1, 0, 2) for x in (made_s, back_s))
    else:
        chan_a, chan_b = (lax.psum_scatter(x, "dp", scatter_dimension=0, tiled=True).astype(F32) for x in (chan_a, chan_b))
        tok = jnp.concatenate([tok_l, tok_s], axis=1).reshape(2, ds_, large_width + small_width)
        tok = lax.psum_scatter(tok, "dp", scatter_dimension=1, tiled=True).astype(F32)
        lin, lout, sin, sout = tok[0, :, 0:pl_], tok[1, :, 0:pl_], tok[0, :, large_width:], tok[1, :, large_width:]
        sin, sout = sin[:, 0:ps], sout[:, 0:ps]
        vec = lax.psum(vec, "dp")
        at = chunks
        cbias, cshift = vec[0:at].reshape(1, dc), vec[at : at + 1]
        gain, shift = vec[at + 1 : at + 3], vec[at + 3 : at + 5]
        lbias, lshift = vec[at + 5 : at + 6, 0:ds_], vec[at + 6 : at + 7, 0:pl_]
        sbias, sshift = vec[at + 7 : at + 8, 0:ds_], vec[at + 8 : at + 9, 0:ps]
    return (
        made_s.reshape(1, micro, imgs, ps, d),
        made_l.reshape(1, micro, imgs, pl_, d),
        back_s.reshape(1, micro, imgs, ps, d),
        back_l.reshape(1, micro, imgs, pl_, d),
        sin.T[None],
        sbias,
        sout[None],
        sshift,
        lin.T[None],
        lbias,
        lout[None],
        lshift,
        chan_a[None],
        cbias,
        chan_b.T[None],
        cshift,
        gain[None],
        shift[None],
    )


def solution(mesh):
    placed = (
        (P(None, "dp", None, None),) * 4
        + (P("section", None, "dp", None),) * 2
        + (P("section", None, None), P("section", None)) * 6
        + (P("section", None, None),) * 2
    )
    outs = (
        (P("section", None, "dp", None, None),) * 4
        + (P("section", None, "dp"), P("section", None), P("section", "dp", None), P("section", None)) * 2
        + (P("section", "dp", None), P("section", None), P("section", None, "dp"), P("section", None))
        + (P("section", None, None),) * 2
    )
    return jax.shard_map(local, mesh=mesh, in_specs=placed, out_specs=outs, check_vma=False)
```

```python
import functools

import jax
import jax.numpy as jnp
from jax import lax
from jax.experimental import pallas as pl
from jax.experimental.pallas import tpu as pltpu
from jax.sharding import PartitionSpec as P

MESH = pl.DeviceIdType.MESH
F32 = jnp.float32
BF16 = jnp.bfloat16
EPSILON = 1e-06
DENSITY = 0.3989422804014327
ROWS = 144
COLS = 256
WIDE = 512


def up_to(value, step):
    return -(-value // step) * step


def mm(a, b, ca, cb):
    return lax.dot_general(a, b, (((ca,), (cb,)), ((), ())), preferred_element_type=F32)


def gelu_pair(v):
    cdf = 0.5 + 0.5 * lax.erf(v * 0.7071067811865476)
    bell = jnp.exp2((v * v) * (-0.5 * 1.4426950408889634))
    return v * cdf, cdf + (v * DENSITY) * bell


def groups(x):
    return x.reshape(x.shape[0] // 8, 8, x.shape[1]).sum(0)


def kernel(
    dims,
    small_images,
    large_images,
    small_upstream,
    large_upstream,
    small_keep,
    large_keep,
    small_in,
    small_bias,
    small_out,
    small_shift,
    large_in,
    large_bias,
    large_out,
    large_shift,
    channel_in,
    channel_bias,
    channel_out,
    channel_shift,
    norm_gain,
    norm_shift,
    small_made,
    large_made,
    small_back,
    large_back,
    chan_a,
    chan_b,
    tok_l,
    tok_s,
    vec_out,
    win,
    wout,
    hid,
    slope,
    xin,
    up,
    n1,
    n2,
    u2,
    r2,
    gb1,
    stage,
    h1,
    sl1,
    lgin,
    lgin_t,
    lgout,
    lgout_t,
    sgin,
    sgin_t,
    sgout,
    sgout_t,
    turned,
    lbcol,
    lscol,
    sbcol,
    sscol,
    mid,
    acc,
    raw_a,
    raw_b,
    sums,
    wsem,
    isem,
    usem,
    ysem,
    gsem,
    fs,
    fr,
    bs,
    br,
    sibs,
    rights,
    lefts,
    outsem,
    vsem,
    ready,
    lent,
    tl,
    ts,
    vecs,
    paired,
    pairs,
):
    sections, n, ps, pl_, pp, d, ds_, dc, dp, fused, shared = dims
    place = lax.axis_index("section")
    ahead = lax.rem(place + 1, sections)
    behind = lax.rem(place + sections - 1, sections)
    last = place // (sections - 1)
    first_rows = n * pl_
    half = pl_ // 2
    line = dp // 2 if fused else 1
    rank = lax.axis_index("dp")
    z = rank // 2
    core = rank % 2
    sibling = rank + 1 - 2 * core
    partner = (place + sections // 2) % sections
    giver = place < sections // 2
    taker = place > 0
    owner = (place + sections - 1) // 2 % 2
    foreign = 1 + last

    def weight_copies():
        pairs = (
            (large_in, lgin),
            (large_out, lgout_t),
            (small_in, raw_a.at[0, :, pl.ds(0, ds_)]),
            (small_out, raw_a.at[0, :, pl.ds(ds_, ds_)]),
            (channel_in, win),
            (channel_out, wout),
        )
        return [pltpu.make_async_copy(a, b, wsem.at[k]) for k, (a, b) in enumerate(pairs)]

    def large_copy(src, dst, sem, i):
        return pltpu.make_async_copy(src.at[i], dst.at[pl.ds(pl.multiple_of(i * pl_, 64), pl_)], sem.at[i])

    def small_copy(src, dst, sem, j):
        return pltpu.make_async_copy(src.at[j], dst.at[j], sem.at[n + j])

    copies = weight_copies()

    @pl.when(place == 0)
    def _():
        for i in range(n):
            large_copy(large_images, xin, isem, i).start()

    for c in copies:
        c.start()

    @pl.when(last == 1)
    def _():
        for i in range(n):
            large_copy(large_upstream, up, usem, i).start()
        for j in range(n):
            small_copy(small_upstream, raw_b, usem, j).start()

    barrier = pltpu.get_barrier_semaphore()

    @pl.when(place > 0)
    def _():
        pl.semaphore_signal(barrier, inc=1, device_id={"section": behind}, device_id_type=MESH)

    @pl.when(place < sections - 1)
    def _():
        pl.semaphore_signal(barrier, inc=1, device_id={"section": ahead}, device_id_type=MESH)

    peers = (place + sections - 2) // (sections - 1) + 1 - last
    if fused:
        pl.semaphore_signal(barrier, inc=1, device_id={"dp": sibling}, device_id_type=MESH)
        for k in range(1, line):
            pl.semaphore_signal(barrier, inc=1, device_id={"dp": (rank + 2 * k) % dp}, device_id_type=MESH)
        pl.semaphore_signal(barrier, inc=1, device_id={"section": partner}, device_id_type=MESH)
        peers = peers + line + 1
    pl.semaphore_wait(barrier, peers)

    def column(row, dst):
        width = up_to(dst.shape[0], 128)
        sums[0:1, 0:width] = jnp.zeros((1, width), F32)
        sums[0:1, 0 : row.shape[1]] = row
        dst[...] = jnp.transpose(jnp.broadcast_to(sums[0:1, 0:width], (128, width)))[0 : dst.shape[0]]

    column(large_bias[...], lbcol)
    column(large_shift[...], lscol)
    column(small_bias[...], sbcol)
    column(small_shift[...], sscol)
    sums[...] = jnp.zeros(sums.shape, F32)
    for c in copies[:4]:
        c.wait()
    for k, padded in enumerate((sgin, sgout_t)):
        padded[...] = jnp.zeros(padded.shape, BF16)
        padded[0:ps, :] = raw_a[0, :, k * ds_ : (k + 1) * ds_]

    @pl.when(place == 0)
    def _():
        for j in range(n):
            small_copy(small_images, raw_a, isem, j).start()

    lgin_t[...] = jnp.transpose(lgin[...])
    lgout[...] = jnp.transpose(lgout_t[...])
    sgin_t[...] = jnp.transpose(sgin[...])
    sgout[...] = jnp.transpose(sgout_t[...])

    gains = norm_gain[...]
    shifts = norm_shift[...]

    def ahead_copy(rows, size, k):
        return pltpu.make_async_remote_copy(
            src_ref=stage.at[pl.ds(rows, size)],
            dst_ref=xin.at[pl.ds(rows, size)],
            send_sem=fs.at[k],
            recv_sem=fr.at[k],
            device_id={"section": ahead},
            device_id_type=MESH,
        )

    def behind_copy(rows, size, k):
        return pltpu.make_async_remote_copy(
            src_ref=stage.at[pl.ds(rows, size)],
            dst_ref=up.at[pl.ds(rows, size)],
            send_sem=bs.at[k],
            recv_sem=br.at[k],
            device_id={"section": behind},
            device_id_type=MESH,
        )

    class Unit:
        def __init__(self, large, i):
            self.large = large
            self.i = i
            self.rows = pl_ if large else pp
            self.blocks = 2 if large else 1
            self.size = self.rows // self.blocks
            self.some = ROWS if large else pp
            self.base = pl.multiple_of(i * pl_, 64) if large else pl.multiple_of(first_rows + i * pp, 16)
            self.head = pl.multiple_of((i if large else n + i) * ds_, 128)
            self.heads = pl.ds(self.head, ds_)
            self.slot = i * 2 if large else 2 * n + i
            self.gin, self.gin_t = (lgin, lgin_t) if large else (sgin, sgin_t)
            self.gout, self.gout_t = (lgout, lgout_t) if large else (sgout, sgout_t)
            self.bcol, self.scol = (lbcol, lscol) if large else (sbcol, sscol)
            self.mask = large_keep if large else small_keep

        def at(self, offset, size):
            return pl.ds(pl.multiple_of(self.base + offset, 16), size)

        def keep(self, which):
            return self.mask[self.i, which].astype(F32)

        def out_copy(self, which, b):
            sem = (ysem, gsem)[which].at[self.slot + b]
            if self.large:
                dst = (large_made, large_back)[which]
                return pltpu.make_async_copy(
                    stage.at[self.at(b * half, half)], dst.at[self.i, pl.ds(b * half, half)], sem
                )
            src = (raw_a, raw_b)[which]
            dst = (small_made, small_back)[which]
            return pltpu.make_async_copy(src.at[self.i], dst.at[self.i], sem)

    units = 2 * n

    def unit_at(which):
        return (which + core) % 2, which // 2

    def forward(unit, step):
        @pl.when(place == 0)
        def _():
            if unit.large:
                large_copy(large_images, xin, isem, unit.i).wait()
            else:
                small_copy(small_images, raw_a, isem, unit.i).wait()
                xin[unit.at(0, pp)] = jnp.zeros((pp, d), BF16)
                xin[unit.at(0, ps)] = raw_a[unit.i]

        def norm_one(r):
            rows = unit.at(r * unit.some, unit.some)
            x = xin[rows].astype(F32)
            x = x - jnp.mean(x, axis=1, keepdims=True)
            s = lax.rsqrt(jnp.mean(x * x, axis=1, keepdims=True) + EPSILON)
            n1[rows] = (x * s * gains[0:1] + shifts[0:1]).astype(BF16)

        steps = unit.size // unit.some
        for b in range(unit.blocks):

            @pl.when(place > 0)
            def _(b=b):
                ahead_copy(unit.base + b * unit.size, unit.size, unit.slot + b).wait_recv()

            for r in range(b * steps, (b + 1) * steps):
                norm_one(r)
        rows = unit.at(0, unit.rows)
        keep_one = unit.keep(0)
        keep_two = unit.keep(1)
        for c in range(0, d, COLS):
            pre = mm(unit.gin_t[...], n1[rows, c : c + COLS], 1, 0) + unit.bcol[:, 0:1]
            act, slp = gelu_pair(pre)
            h1[unit.heads, c : c + COLS] = act.astype(BF16)
            sl1[unit.heads, c : c + COLS] = slp.astype(BF16)
        for c in range(0, d, COLS):
            branch = mm(unit.gout_t[...], h1[unit.heads, c : c + COLS], 1, 0) + unit.scol[:, 0:1]
            mid[0 : unit.rows, c : c + COLS] = xin[rows, c : c + COLS].astype(F32) + keep_one * branch

        def norm_two(r):
            rows = unit.at(r * unit.some, unit.some)
            x = mid[r * unit.some : (r + 1) * unit.some]
            x = x - jnp.mean(x, axis=1, keepdims=True)
            s = lax.rsqrt(jnp.mean(x * x, axis=1, keepdims=True) + EPSILON)
            x = x * s
            u2[rows] = x.astype(BF16)
            r2[rows] = jnp.broadcast_to(s, (unit.some, 128))
            n2[rows] = (x * gains[1:2] + shifts[1:2]).astype(BF16)

        for r in range(unit.rows // unit.some):
            norm_two(r)

        @pl.when(step == 0)
        def _():
            for c in copies[4:]:
                c.wait()

        for b in range(unit.blocks):
            size = unit.size
            rows = unit.at(b * size, size)
            here = slice(b * size, (b + 1) * size)
            total = channel_shift[...]
            parts = [slice(c, c + WIDE) for c in range(0, dc, WIDE)]
            ahead_of = mm(n2[rows], win[:, parts[0]], 1, 0)
            for c, cols in enumerate(parts):
                pre = ahead_of + channel_bias[:, cols]
                if c + 1 < len(parts):
                    ahead_of = mm(n2[rows], win[:, parts[c + 1]], 1, 0)
                act, slp = gelu_pair(pre)
                act = act.astype(BF16)
                hid[rows, cols] = act
                slope[rows, cols] = slp.astype(BF16)
                total = total + mm(act, wout[cols, :], 1, 0)
            y = (mid[here] + keep_two * total).astype(BF16)
            stage[rows] = y
            if not unit.large:
                raw_a[unit.i] = y[0:ps]

            @pl.when(place < sections - 1)
            def _(b=b, size=size):
                ahead_copy(unit.base + b * size, size, unit.slot + b).start()

            if unit.large or not fused:
                unit.out_copy(0, b).start()

    def backward(unit):
        @pl.when(last == 1)
        def _():
            if unit.large:
                large_copy(large_upstream, up, usem, unit.i).wait()
            else:
                small_copy(small_upstream, raw_b, usem, unit.i).wait()
                up[unit.at(0, pp)] = jnp.zeros((pp, d), BF16)
                up[unit.at(0, ps)] = raw_b[unit.i]

        keep_one = unit.keep(0)
        keep_two = unit.keep(1)
        size = unit.size
        for b in range(unit.blocks):
            rows = unit.at(b * size, size)
            here = slice(b * size, (b + 1) * size)

            @pl.when(place < sections - 1)
            def _(b=b):
                ahead_copy(unit.base + b * size, size, unit.slot + b).wait_send()

            if unit.large or not fused:
                unit.out_copy(0, b).wait()

            @pl.when(last == 0)
            def _(b=b):
                behind_copy(unit.base + b * size, size, unit.slot + b).wait_recv()

            stage[rows] = up[rows] * keep_two.astype(BF16)

            parts = [slice(c, c + WIDE) for c in range(0, dc, WIDE)]
            total = None
            ahead_of = mm(stage[rows], wout[parts[0], :], 1, 1)
            for c, cols in enumerate(parts):
                grad = ahead_of
                if c + 1 < len(parts):
                    ahead_of = mm(stage[rows], wout[parts[c + 1], :], 1, 1)
                grad = (grad * slope[rows, cols].astype(F32)).astype(BF16)
                slope[rows, cols] = grad
                term = mm(grad, win[:, cols], 1, 1)
                total = term if total is None else total + term
            acc[here] = total

        def norm_two(r):
            offset = r * unit.some
            rows = unit.at(offset, unit.some)
            local = slice(offset, offset + unit.some)
            h = acc[local]
            u = u2[rows].astype(F32)
            s = r2[rows][:, 0:1]
            g = up[rows].astype(F32)
            q = h * gains[1:2]
            first = jnp.mean(q, axis=1, keepdims=True)
            second = jnp.mean(q * u, axis=1, keepdims=True)
            g_mid = g + s * (q - first - u * second)
            mid[local] = g_mid
            gb1[rows] = (keep_one * g_mid).astype(BF16)
            up[rows] = (keep_two * g).astype(BF16)
            return groups(h * u), groups(h)

        parts = [norm_two(r) for r in range(unit.rows // unit.some)]
        sums[8:16, 0:d] += sum(p[0] for p in parts)
        sums[24:32, 0:d] += sum(p[1] for p in parts)
        rows = unit.at(0, unit.rows)
        for c in range(0, d, COLS):
            grad = mm(unit.gout[...], gb1[rows, c : c + COLS], 1, 0)
            grad = (grad * sl1[unit.heads, c : c + COLS].astype(F32)).astype(BF16)
            sl1[unit.heads, c : c + COLS] = grad
        for c in range(0, d, COLS):
            acc[0 : unit.rows, c : c + COLS] = mm(unit.gin[...], sl1[unit.heads, c : c + COLS], 1, 0)

        def norm_one(r):
            offset = r * unit.some
            rows = unit.at(offset, unit.some)
            local = slice(offset, offset + unit.some)
            x = xin[rows].astype(F32)
            x = x - jnp.mean(x, axis=1, keepdims=True)
            s = lax.rsqrt(jnp.mean(x * x, axis=1, keepdims=True) + EPSILON)
            u = x * s
            h = acc[local]
            q = h * gains[0:1]
            first = jnp.mean(q, axis=1, keepdims=True)
            second = jnp.mean(q * u, axis=1, keepdims=True)
            stage[rows] = (mid[local] + s * (q - first - u * second)).astype(BF16)
            return groups(h * u), groups(h)

        steps = size // unit.some
        for b in range(unit.blocks):
            parts = [norm_one(r) for r in range(b * steps, (b + 1) * steps)]
            sums[0:8, 0:d] += sum(p[0] for p in parts)
            sums[16:24, 0:d] += sum(p[1] for p in parts)
            if not unit.large:
                raw_b[unit.i] = stage[unit.at(0, ps)]

            @pl.when(place > 0)
            def _(b=b):
                behind_copy(unit.base + b * size, size, unit.slot + b).start()

            if unit.large or not fused:
                unit.out_copy(1, b).start()

    piece = d // dp
    tok_piece = ds_ // dp

    def turn(src):
        def some(rows, size):
            value = jnp.transpose(src[pl.ds(rows, size)])
            if not fused:
                turned[:, pl.ds(rows, size)] = value
                return
            for b in range(dp):
                at = ((b % 2) * line + b // 2) * piece
                turned[at : at + piece, pl.ds(rows, size)] = value[b * piece : (b + 1) * piece]

        def full(r, carry):
            some(pl.multiple_of(r * 128, 128), 128)
            return carry

        whole = src.shape[0] // 128
        lax.fori_loop(0, whole, full, 0)
        if src.shape[0] % 128:
            some(whole * 128, src.shape[0] % 128)


    def step(t, carry):
        back = (1 - last) * (t // units) + last * (t % 2)
        which = (1 - last) * (t % units) + last * (t // 2)
        small, i = unit_at(which)

        @pl.when(t == 2 * units - 1)
        def _():
            turn(n2)

        @pl.when((back == 0) & (small == 0))
        def _():
            forward(Unit(True, i), t)

        @pl.when((back == 0) & (small == 1))
        def _():
            forward(Unit(False, i), t)

        @pl.when((back == 1) & (small == 0))
        def _():
            backward(Unit(True, i))

        @pl.when((back == 1) & (small == 1))
        def _():
            backward(Unit(False, i))

        return carry

    lax.fori_loop(0, 2 * units, step, 0)

    total = hid.shape[0]
    chunks = dc // d
    count = 2 * chunks + 2
    kinds = (chunks, chunks, 1, 1, shared)
    first_of = (0, chunks + 2, chunks, chunks + 1, count + 1)
    large_width, small_width = up_to(pl_, 128), up_to(pp, 128)
    widths = (d, d, large_width, small_width, d)
    own = line
    across = line + 1

    def columns(kind, k):
        if kind < 2:
            return pl.ds(pl.multiple_of(k * d, 128), d)
        return pl.ds(0, widths[kind])

    def own_rows(kind):
        return ((slope, 0), (hid, 0), (up, 0), (up, d))[kind]

    def weight_product(kind, k):
        src = (slope, hid)[kind]

        def part(j, carry):
            cols = pl.ds(pl.multiple_of(k * d + j * COLS, COLS), COLS)
            if kind == 0:
                bias = mm(jnp.ones((8, total), BF16), src[:, cols], 1, 0)[0:1]
                vecs[own, pl.ds(k, 1), pl.ds(pl.multiple_of(j * COLS, COLS), COLS)] = bias
            src[0:d, cols] = mm(turned[...], src[:, cols], 1, 0).astype(BF16)
            return carry

        lax.fori_loop(0, d // COLS, part, 0)

    def token_product(large):
        unit_rows = pl_ if large else pp
        ones_d = jnp.ones((8, d), BF16)
        out_grad = in_grad = bias = shift = None
        for k in range(n):
            base = k * pl_ if large else first_rows + k * pp
            head = k * ds_ if large else (n + k) * ds_
            g = gb1[base : base + unit_rows]
            x = n1[base : base + unit_rows]
            h = h1[head : head + ds_]
            p = sl1[head : head + ds_]
            terms = (mm(p, x, 1, 1), mm(h, g, 1, 1), mm(ones_d, p, 1, 1), mm(ones_d, g, 1, 1))
            if k == 0:
                in_grad, out_grad, bias, shift = terms
            else:
                in_grad, out_grad, bias, shift = in_grad + terms[0], out_grad + terms[1], bias + terms[2], shift + terms[3]
        src, base = own_rows(2 if large else 3)
        for at, value in ((0, in_grad), (1, out_grad)):
            value = value.astype(BF16)
            if not fused:
                src[base + at * ds_ : base + (at + 1) * ds_, 0:unit_rows] = value
                continue
            for b in range(dp):
                to = base + ((b % 2) * line + b // 2) * piece + at * tok_piece
                src[to : to + tok_piece, 0:unit_rows] = value[b * tok_piece : (b + 1) * tok_piece]
        row = chunks + 5 + (0 if large else 2)
        vecs[own, row : row + 1, 0:ds_] = bias[0:1]
        vecs[own, row + 1 : row + 2, 0:unit_rows] = shift[0:1]

    def product(kind, k):
        if kind == 2:
            turn(up)
            vecs[own, chunks : chunks + 1] = mm(jnp.ones((8, total), BF16), up[...], 1, 0)[0:1]
            for j in range(4):
                vecs[own, chunks + 1 + j : chunks + 2 + j] = jnp.sum(sums[8 * j : 8 * j + 8], axis=0, keepdims=True)
        if kind < 2:
            weight_product(kind, k)
        else:
            token_product(kind == 2)

    def ways(step_of, kept=False):
        def at(c, valid=True):
            for kind in range(5 if fused else 4):
                low, high = first_of[kind], first_of[kind] + kinds[kind]
                here = (c >= low) & (c < high) & valid
                if kind == 4:
                    here = here & taker & (c < low + foreign)
                if kind == 0 and kept:
                    here = here & ((place >= sections // 2) | (c < 1) | (c > shared))

                @pl.when(here)
                def _(kind=kind, low=low):
                    step_of(kind, c - low)

        return at

    vecs[own] = jnp.zeros(vecs.shape[1:], F32)
    if not fused:

        def whole_copies(kind, k):
            src, base = own_rows(kind)
            if kind < 2:
                cols = columns(kind, k)
                dst = (chan_a, chan_b)[kind]
                return [pltpu.make_async_copy(src.at[pl.ds(0, d), cols], dst.at[:, cols], outsem.at[first_of[kind] + k])]
            cols = pl.ds(0, widths[kind])
            dst = (tok_l, tok_s)[kind - 2]
            return [pltpu.make_async_copy(src.at[pl.ds(base, d), cols], dst, outsem.at[first_of[kind]])]

        def one(kind, k):
            product(kind, k)
            for c in whole_copies(kind, k):
                c.start()

        def finish(kind, k):
            for c in whole_copies(kind, k):
                c.wait()

        def run(c, carry):
            ways(one)(c)
            return carry

        def end(c, carry):
            ways(finish)(c)
            return carry

        lax.fori_loop(0, count, run, 0)
        lax.fori_loop(0, count, end, 0)
        vec_out[...] = vecs[own]
    else:
        rightward, leftward = (rank + 2) % dp, (rank + dp - 2) % dp

        def mine(kind, k, to):
            if kind == 4:
                return h1.at[pl.ds(pl.multiple_of((k * line + to) * piece, 16), piece)]
            src, base = own_rows(kind)
            return src.at[pl.ds(pl.multiple_of(base + (core * line + to) * piece, 16), piece), columns(kind, k)]

        def crossing(kind, k, rows, size):
            ref, base = ((win, 0), (win, d // 2), (wout, 3 * d), (wout, 3 * d + d // 2))[kind]
            return ref.at[pl.ds(pl.multiple_of(base + rows, 16), size), columns(kind, k)]

        def from_left(kind, k, to):
            ref, base = ((wout, 0), (wout, chunks * (line - 1)), (n2, 0), (n2, line - 1), (sl1, 0))[kind]
            rows = (base + k * (line - 1) + to - 1) * piece
            return ref.at[pl.ds(pl.multiple_of(rows, 16), piece), pl.ds(0, widths[kind])]

        def from_right(kind, k, to):
            ref, base = ((xin, 0), (u2, 0), (n2, 2 * (line - 1)), (n2, 3 * (line - 1)), (sl1, shared * (line - 1)))[kind]
            rows = (base + k * (line - 1) + to) * piece
            return ref.at[pl.ds(pl.multiple_of(rows, 16), piece), pl.ds(0, widths[kind])]

        def sem_of(kind, k, to):
            return ((count if kind == 4 else first_of[kind]) + k) * line + to

        def cross_copy(kind, k):
            src, base = own_rows(kind)
            rows = pl.ds(pl.multiple_of(base + (1 - core) * line * piece, 16), line * piece)
            c = first_of[kind] + k
            return pltpu.make_async_remote_copy(
                src_ref=src.at[rows, columns(kind, k)],
                dst_ref=crossing(kind, k, 0, line * piece),
                send_sem=sibs.at[0, c],
                recv_sem=sibs.at[1, c],
                device_id={"dp": sibling},
                device_id_type=MESH,
            )

        def right_copy(kind, k, to):
            return pltpu.make_async_remote_copy(
                src_ref=mine(kind, k, to),
                dst_ref=from_left(kind, k, to),
                send_sem=rights.at[0, sem_of(kind, k, to)],
                recv_sem=rights.at[1, sem_of(kind, k, to)],
                device_id={"dp": rightward},
                device_id_type=MESH,
            )

        def left_copy(kind, k, to):
            return pltpu.make_async_remote_copy(
                src_ref=mine(kind, k, to),
                dst_ref=from_right(kind, k, to),
                send_sem=lefts.at[0, sem_of(kind, k, to)],
                recv_sem=lefts.at[1, sem_of(kind, k, to)],
                device_id={"dp": leftward},
                device_id_type=MESH,
            )

        def chip_sum(kind, k, to):
            if kind == 4:
                return mine(kind, k, to)[...].astype(F32)
            return mine(kind, k, to)[...].astype(F32) + crossing(kind, k, to * piece, piece)[...].astype(F32)

        def flow_right(kind, k):
            def one(j, carry):
                to = line - 1 - j

                @pl.when(z == 0)
                def _():
                    mine(kind, k, to)[...] = chip_sum(kind, k, to).astype(BF16)

                @pl.when(z > 0)
                def _():
                    right_copy(kind, k, to).wait_recv()
                    value = chip_sum(kind, k, to) + from_left(kind, k, to)[...].astype(F32)
                    mine(kind, k, to)[...] = value.astype(BF16)

                right_copy(kind, k, to).start()
                return carry

            lax.fori_loop(0, line - 1 - z, one, 0)

        def flow_left(kind, k):
            def one(to, carry):
                @pl.when(z == line - 1)
                def _():
                    mine(kind, k, to)[...] = chip_sum(kind, k, to).astype(BF16)

                @pl.when(z < line - 1)
                def _():
                    left_copy(kind, k, to).wait_recv()
                    value = chip_sum(kind, k, to) + from_right(kind, k, to)[...].astype(F32)
                    mine(kind, k, to)[...] = value.astype(BF16)

                left_copy(kind, k, to).start()
                return carry

            lax.fori_loop(0, z, one, 0)

        def out_stage(kind, k):
            if kind == 0:
                return mid.at[pl.ds(pl.multiple_of(k * piece, 16), piece)]
            if kind in (1, 4):
                at = k + (chunks if kind == 4 else 0)
                return acc.at[pl.ds(pl.multiple_of(at * piece, 16), piece)]
            return (tl, ts)[kind - 2]

        def out_copies(kind, k):
            c = first_of[kind] + k
            if kind < 2:
                dst = (chan_a, chan_b)[kind].at[:, columns(kind, k)]
            else:
                dst = (tok_l, tok_s)[kind - 2]
            return pltpu.make_async_copy(out_stage(kind, k), dst, outsem.at[c])

        def gather(kind, k):
            width = (d, d, pl_, ps, d)[kind]
            dst = out_stage(kind, k)
            dst[...] = chip_sum(kind, k, z)[:, 0:width]

            @pl.when(z > 0)
            def _():
                right_copy(kind, k, z).wait_recv()
                dst[...] += from_left(kind, k, z)[...].astype(F32)[:, 0:width]

            @pl.when(z < line - 1)
            def _():
                left_copy(kind, k, z).wait_recv()
                dst[...] += from_right(kind, k, z)[...].astype(F32)[:, 0:width]

            if kind == 4:
                give_back(k).start()
            else:
                out_copies(kind, k).start()

        def lend_copy(j, f, to):
            rows = pl.ds(pl.multiple_of(core * line * piece, 16), line * piece)
            return pltpu.make_async_remote_copy(
                src_ref=slope.at[rows, columns(0, j + 1)],
                dst_ref=h1.at[pl.ds(pl.multiple_of(f * line * piece, 16), line * piece)],
                send_sem=lent.at[0, j],
                recv_sem=lent.at[1, f],
                device_id={"section": to},
                device_id_type=MESH,
            )

        def return_copy(f, j, to):
            return pltpu.make_async_remote_copy(
                src_ref=out_stage(4, f),
                dst_ref=out_stage(0, j + 1),
                send_sem=lent.at[2, f],
                recv_sem=lent.at[3, j],
                device_id={"section": to},
                device_id_type=MESH,
            )

        def lend_away(j):
            return lend_copy(j, place * j, (1 - place) * (2 - j) + place * 3)

        def give_back(f):
            return return_copy(f, f + (2 - place) * (1 - last), owner)

        def lend(c):
            @pl.when(giver & (c >= 1) & (c <= shared))
            def _():
                @pl.when(c == 1)
                def _():
                    pl.semaphore_wait(ready.at[3], 1)

                @pl.when((c == 2) & (place == 0))
                def _():
                    pl.semaphore_wait(ready.at[6], 1)

                def one(to, carry):
                    mine(0, c, to)[...] = chip_sum(0, c, to).astype(BF16)
                    return carry

                lax.fori_loop(0, line, one, 0)
                lend_away(c - 1).start()

        def pair_copy(which):
            return pltpu.make_async_copy(paired, (small_made, small_back)[which], pairs.at[which])

        def pair(which):
            if which:
                pair_copy(0).wait()
            src = (raw_a, raw_b)[which]
            for r in range(0, ps, 32):
                rows = slice(r, min(r + 32, ps))
                images = [src[j, rows].astype(F32)[:, None, :] for j in range(n)]
                paired[rows] = jnp.concatenate(images, axis=1).astype(BF16)
            pair_copy(which).start()

        def vec_cross():
            return pltpu.make_async_remote_copy(
                src_ref=vecs.at[own],
                dst_ref=vecs.at[across],
                send_sem=vsem.at[0, 0],
                recv_sem=vsem.at[1, 0],
                device_id={"dp": sibling},
                device_id_type=MESH,
            )

        def vec_copy(k):
            return pltpu.make_async_remote_copy(
                src_ref=vecs.at[z],
                dst_ref=vecs.at[z],
                send_sem=vsem.at[0, k],
                recv_sem=vsem.at[1, k],
                device_id={"dp": (rank + 2 * k) % dp},
                device_id_type=MESH,
            )

        def first(kind, k):
            if kind == 4:

                @pl.when(k == 0)
                def _():
                    @pl.when(z < line - 1)
                    def _():
                        pl.semaphore_wait(ready.at[4], 1)

                    @pl.when(z > 0)
                    def _():
                        pl.semaphore_wait(ready.at[5], 1)

                lend_copy(0, k, owner).wait_recv()
                return
            product(kind, k)
            if kind == 3:

                @pl.when(taker)
                def _():
                    for at, here in ((6, place == 1), (3, place > 1)):

                        @pl.when(here)
                        def _(at=at):
                            pl.semaphore_signal(ready.at[at], inc=1, device_id={"section": owner}, device_id_type=MESH)

                    @pl.when(z > 0)
                    def _():
                        pl.semaphore_signal(ready.at[4], inc=1, device_id={"dp": leftward}, device_id_type=MESH)

                    @pl.when(z < line - 1)
                    def _():
                        pl.semaphore_signal(ready.at[5], inc=1, device_id={"dp": rightward}, device_id_type=MESH)

            if kind == 0:

                @pl.when(k == 0)
                def _():
                    pl.semaphore_wait(ready.at[0], 1)

                    @pl.when(z < line - 1)
                    def _():
                        pl.semaphore_wait(ready.at[1], 1)

                    @pl.when(z > 0)
                    def _():
                        pl.semaphore_wait(ready.at[2], 1)

            cross_copy(kind, k).start()

        def crossed(kind, k):
            if kind < 4:
                cross_copy(kind, k).wait_recv()

        def finish(kind, k):
            if kind == 4:
                give_back(k).wait_send()
            else:
                cross_copy(kind, k).wait_send()
                out_copies(kind, k).wait()

            def right(j, carry):
                right_copy(kind, k, line - 1 - j).wait_send()
                return carry

            def left(to, carry):
                left_copy(kind, k, to).wait_send()
                return carry

            sent = line - 1 - z, z
            if kind == 0:
                away = giver & (k >= 1) & (k <= shared)
                own_line = 1 - away.astype(jnp.int32)
                sent = sent[0] * own_line, sent[1] * own_line
            lax.fori_loop(0, sent[0], right, 0)
            lax.fori_loop(0, sent[1], left, 0)

        pl.semaphore_signal(ready.at[0], inc=1, device_id={"dp": sibling}, device_id_type=MESH)

        @pl.when(z > 0)
        def _():
            pl.semaphore_signal(ready.at[1], inc=1, device_id={"dp": leftward}, device_id_type=MESH)

        @pl.when(z < line - 1)
        def _():
            pl.semaphore_signal(ready.at[2], inc=1, device_id={"dp": rightward}, device_id_type=MESH)

        def run(c, carry):
            ways(crossed)(c - 1)
            lend(c - 1)
            ways(flow_right, True)(c - 1 - z, z < line - 1)
            ways(flow_left, True)(c - line + z, z > 0)
            ways(first)(c)

            @pl.when(c == count)
            def _():
                vec_cross().start()

            @pl.when(c == count + 1)
            def _():
                vec_cross().wait()
                vecs[z] = vecs[own] + vecs[across]
                for k in range(1, line):
                    vec_copy(k).start()

            for which in range(2):

                @pl.when(c == count - 2 + which)
                def _(which=which):
                    pair(which)

            ways(gather, True)(c - line - 1)
            return carry

        steps = count + 1 + shared
        lax.fori_loop(0, steps + line + 1, run, 0)

        @pl.when(giver)
        def _():
            for k in range(shared):
                lend_away(k).wait_send()
                return_copy(0, k, owner).wait_recv()
                out_copies(0, k + 1).start()

        def end(c, carry):
            ways(finish)(c)
            return carry

        lax.fori_loop(0, steps, end, 0)
        pair_copy(1).wait()
        for k in range(1, line):
            vec_copy(k).wait()
        value = vecs[0]
        for k in range(1, line):
            value = value + vecs[k]
        vec_out[...] = value

    for i in range(2 * n):
        unit = Unit(i < n, i % n)
        for b in range(unit.blocks):
            if unit.large or not fused:
                unit.out_copy(1, b).wait()

            @pl.when(place > 0)
            def _(b=b, unit=unit):
                behind_copy(unit.base + b * unit.size, unit.size, unit.slot + b).wait_send()


def finish_kernel(tok_piece, d, chunks, moved, *refs):
    sources, (tok_l, tok_s, vec), rest = refs[:moved], refs[moved : moved + 3], refs[moved + 3 :]
    outs, vias, sem = rest[: -moved - 1], rest[-moved - 1 : -1], rest[-1]
    bring = [pltpu.make_async_copy(a, b, sem.at[0, k]) for k, (a, b) in enumerate(zip(sources, vias))]
    take = [pltpu.make_async_copy(a, b, sem.at[1, k]) for k, (a, b) in enumerate(zip(vias, outs[:moved]))]
    for c in bring:
        c.start()
    outs = outs[moved:]
    for k, src in enumerate((tok_l, tok_s)):
        outs[2 * k][...] = src[0:tok_piece]
        outs[2 * k + 1][...] = src[tok_piece:]
    for k in range(chunks):
        outs[4][:, k * d : (k + 1) * d] = vec[k : k + 1]
    at = chunks
    for out in outs[5:]:
        rows, width = out.shape
        out[...] = vec[at : at + rows, 0:width]
        at += rows
    for a, b in zip(bring, take):
        a.wait()
        b.start()
    for c in take:
        c.wait()


def local(
    small_images,
    large_images,
    small_upstream,
    large_upstream,
    small_keep,
    large_keep,
    small_in,
    small_bias,
    small_out,
    small_shift,
    large_in,
    large_bias,
    large_out,
    large_shift,
    channel_in,
    channel_bias,
    channel_out,
    channel_shift,
    norm_gain,
    norm_shift,
):
    sections = lax.axis_size("section")
    micro, imgs, ps, d = small_images.shape
    pl_ = large_images.shape[2]
    n = micro * imgs
    ds_ = small_in.shape[2]
    dc = channel_in.shape[2]
    pp = up_to(ps, 16)
    rows = n * (pl_ + pp)
    small_width, large_width = up_to(pp, 128), up_to(pl_, 128)
    dp = lax.axis_size("dp")
    piece, tok_piece = d // dp, ds_ // dp
    fused = d % (16 * dp) == 0 and ds_ % (16 * dp) == 0 and dc == 4 * d and d == 2 * ds_ and 2 * dp * piece <= rows
    fused = fused and sections == 4
    shared = 2
    dims = (sections, n, ps, pl_, pp, d, ds_, dc, dp, fused, shared)
    chunks = dc // d
    line = dp // 2 if fused else 1
    count = 2 * chunks + 2
    vec_rows = up_to(chunks + 9, 8)
    any_ = pl.BlockSpec(memory_space=pl.ANY)
    vmem = pl.BlockSpec(memory_space=pltpu.VMEM)
    smem = pl.BlockSpec(memory_space=pltpu.SMEM)
    block = max(pl_, n * pp)
    blocks = 2 * n + n
    scratch = [
        pltpu.VMEM((d, dc), BF16),
        pltpu.VMEM((dc, d), BF16),
        pltpu.VMEM((rows, dc), BF16),
        pltpu.VMEM((rows, dc), BF16),
        pltpu.VMEM((rows, d), BF16),
        pltpu.VMEM((rows, d), BF16),
        pltpu.VMEM((rows, d), BF16),
        pltpu.VMEM((rows, d), BF16),
        pltpu.VMEM((rows, d), BF16),
        pltpu.VMEM((rows, 128), F32),
        pltpu.VMEM((rows, d), BF16),
        pltpu.VMEM((rows, d), BF16),
        pltpu.VMEM((2 * n * ds_, d), BF16),
        pltpu.VMEM((2 * n * ds_, d), BF16),
        pltpu.VMEM((pl_, ds_), BF16),
        pltpu.VMEM((ds_, pl_), BF16),
        pltpu.VMEM((ds_, pl_), BF16),
        pltpu.VMEM((pl_, ds_), BF16),
        pltpu.VMEM((pp, ds_), BF16),
        pltpu.VMEM((ds_, pp), BF16),
        pltpu.VMEM((ds_, pp), BF16),
        pltpu.VMEM((pp, ds_), BF16),
        pltpu.VMEM((d, rows), BF16),
        pltpu.VMEM((ds_, 128), F32),
        pltpu.VMEM((pl_, 128), F32),
        pltpu.VMEM((ds_, 128), F32),
        pltpu.VMEM((pp, 128), F32),
        pltpu.VMEM((block, d), F32),
        pltpu.VMEM((block, d), F32),
        pltpu.VMEM((n, ps, d), BF16),
        pltpu.VMEM((n, ps, d), BF16),
        pltpu.VMEM((32, d), F32),
        pltpu.SemaphoreType.DMA((6,)),
        pltpu.SemaphoreType.DMA((2 * n,)),
        pltpu.SemaphoreType.DMA((2 * n,)),
        pltpu.SemaphoreType.DMA((blocks,)),
        pltpu.SemaphoreType.DMA((blocks,)),
        pltpu.SemaphoreType.DMA((blocks,)),
        pltpu.SemaphoreType.DMA((blocks,)),
        pltpu.SemaphoreType.DMA((blocks,)),
        pltpu.SemaphoreType.DMA((blocks,)),
        pltpu.SemaphoreType.DMA((2, count)),
        pltpu.SemaphoreType.DMA((2, (count + shared) * line)),
        pltpu.SemaphoreType.DMA((2, (count + shared) * line)),
        pltpu.SemaphoreType.DMA((count,)),
        pltpu.SemaphoreType.DMA((2, line)),
        pltpu.SemaphoreType.REGULAR((7,)),
        pltpu.SemaphoreType.DMA((4, shared)),
        pltpu.VMEM((2 * tok_piece, pl_), F32),
        pltpu.VMEM((2 * tok_piece, ps), F32),
        pltpu.VMEM((line + 2, vec_rows, d), F32),
        pltpu.VMEM((ps, n, d) if fused else (8, 128), BF16),
        pltpu.SemaphoreType.DMA((2,)),
    ]
    if fused:
        reduced = (
            jax.ShapeDtypeStruct((piece, dc), F32),
            jax.ShapeDtypeStruct((piece, dc), F32),
            jax.ShapeDtypeStruct((2 * tok_piece, pl_), F32),
            jax.ShapeDtypeStruct((2 * tok_piece, ps), F32),
        )
    else:
        reduced = (
            jax.ShapeDtypeStruct((d, dc), BF16),
            jax.ShapeDtypeStruct((d, dc), BF16),
            jax.ShapeDtypeStruct((d, large_width), BF16),
            jax.ShapeDtypeStruct((d, small_width), BF16),
        )
    small_shape = (ps, n, d) if fused else (n, ps, d)
    outs = (
        jax.ShapeDtypeStruct(small_shape, BF16),
        jax.ShapeDtypeStruct((n, pl_, d), BF16),
        jax.ShapeDtypeStruct(small_shape, BF16),
        jax.ShapeDtypeStruct((n, pl_, d), BF16),
        *reduced,
        jax.ShapeDtypeStruct((vec_rows, d), F32),
    )
    made_s, made_l, back_s, back_l, chan_a, chan_b, tok_l, tok_s, vec = pl.pallas_call(
        functools.partial(kernel, dims),
        out_shape=outs,
        in_specs=[any_] * 4
        + [smem] * 2
        + [any_, vmem, any_, vmem] * 2
        + [any_, vmem, any_, vmem]
        + [vmem, vmem],
        out_specs=(any_,) * 8 + (vmem,),
        scratch_shapes=scratch,
        compiler_params=pltpu.CompilerParams(
            collective_id=0, has_side_effects=True, vmem_limit_bytes=65400 * 1024
        ),
        cost_estimate=pl.CostEstimate(flops=50 * 10**9, bytes_accessed=40 * 10**6, transcendentals=10**7),
    )(
        small_images.reshape(n, ps, d),
        large_images.reshape(n, pl_, d),
        small_upstream.reshape(n, ps, d),
        large_upstream.reshape(n, pl_, d),
        small_keep.reshape(n, 2),
        large_keep.reshape(n, 2),
        small_in[0],
        small_bias,
        small_out[0].T,
        small_shift,
        large_in[0],
        large_bias,
        large_out[0].T,
        large_shift,
        channel_in[0],
        channel_bias,
        channel_out[0],
        channel_shift,
        norm_gain[0],
        norm_shift[0],
    )
    if fused:
        large = (made_l, back_l, chan_a, chan_b, made_s, back_s)
        final = [jax.ShapeDtypeStruct(x.shape, x.dtype) for x in large]
        final += [jax.ShapeDtypeStruct((tok_piece, width), F32) for width in (pl_, pl_, ps, ps)]
        final += [
            jax.ShapeDtypeStruct(shape, F32)
            for shape in ((1, dc), (1, d), (2, d), (2, d), (1, ds_), (1, pl_), (1, ds_), (1, ps))
        ]
        made_l, back_l, chan_a, chan_b, made_s, back_s, lin, lout, sin, sout, *vecs = pl.pallas_call(
            functools.partial(finish_kernel, tok_piece, d, chunks, len(large)),
            out_shape=final,
            in_specs=[any_] * len(large) + [vmem] * 3,
            out_specs=[any_] * len(large) + [vmem] * 12,
            scratch_shapes=[pltpu.VMEM(x.shape, x.dtype) for x in large] + [pltpu.SemaphoreType.DMA((2, len(large)))],
            compiler_params=pltpu.CompilerParams(vmem_limit_bytes=65400 * 1024),
        )(*large, tok_l, tok_s, vec)
        cbias, cshift, gain, shift, lbias, lshift, sbias, sshift = vecs
        made_s, back_s = (x.transpose(1, 0, 2) for x in (made_s, back_s))
    else:
        chan_a, chan_b = (lax.psum_scatter(x, "dp", scatter_dimension=0, tiled=True).astype(F32) for x in (chan_a, chan_b))
        tok = jnp.concatenate([tok_l, tok_s], axis=1).reshape(2, ds_, large_width + small_width)
        tok = lax.psum_scatter(tok, "dp", scatter_dimension=1, tiled=True).astype(F32)
        lin, lout, sin, sout = tok[0, :, 0:pl_], tok[1, :, 0:pl_], tok[0, :, large_width:], tok[1, :, large_width:]
        sin, sout = sin[:, 0:ps], sout[:, 0:ps]
        vec = lax.psum(vec, "dp")
        at = chunks
        cbias, cshift = vec[0:at].reshape(1, dc), vec[at : at + 1]
        gain, shift = vec[at + 1 : at + 3], vec[at + 3 : at + 5]
        lbias, lshift = vec[at + 5 : at + 6, 0:ds_], vec[at + 6 : at + 7, 0:pl_]
        sbias, sshift = vec[at + 7 : at + 8, 0:ds_], vec[at + 8 : at + 9, 0:ps]
    return (
        made_s.reshape(1, micro, imgs, ps, d),
        made_l.reshape(1, micro, imgs, pl_, d),
        back_s.reshape(1, micro, imgs, ps, d),
        back_l.reshape(1, micro, imgs, pl_, d),
        sin.T[None],
        sbias,
        sout[None],
        sshift,
        lin.T[None],
        lbias,
        lout[None],
        lshift,
        chan_a[None],
        cbias,
        chan_b.T[None],
        cshift,
        gain[None],
        shift[None],
    )


def solution(mesh):
    placed = (
        (P(None, "dp", None, None),) * 4
        + (P("section", None, "dp", None),) * 2
        + (P("section", None, None), P("section", None)) * 6
        + (P("section", None, None),) * 2
    )
    outs = (
        (P("section", None, "dp", None, None),) * 4
        + (P("section", None, "dp"), P("section", None), P("section", "dp", None), P("section", None)) * 2
        + (P("section", "dp", None), P("section", None), P("section", None, "dp"), P("section", None))
        + (P("section", None, None),) * 2
    )
    return jax.shard_map(local, mesh=mesh, in_specs=placed, out_specs=outs, check_vma=False)
```

```python
import functools

import jax
import jax.numpy as jnp
from jax import lax
from jax.experimental import pallas as pl
from jax.experimental.pallas import tpu as pltpu
from jax.sharding import PartitionSpec as P

MESH = pl.DeviceIdType.MESH
F32 = jnp.float32
BF16 = jnp.bfloat16
EPSILON = 1e-06
DENSITY = 0.3989422804014327
ROWS = 144
COLS = 256
WIDE = 512


def up_to(value, step):
    return -(-value // step) * step


def mm(a, b, ca, cb):
    return lax.dot_general(a, b, (((ca,), (cb,)), ((), ())), preferred_element_type=F32)


def gelu_pair(v):
    cdf = 0.5 + 0.5 * lax.erf(v * 0.7071067811865476)
    bell = jnp.exp2((v * v) * (-0.5 * 1.4426950408889634))
    return v * cdf, cdf + (v * DENSITY) * bell


def groups(x):
    return x.reshape(x.shape[0] // 8, 8, x.shape[1]).sum(0)


def kernel(
    dims,
    small_images,
    large_images,
    small_upstream,
    large_upstream,
    small_keep,
    large_keep,
    small_in,
    small_bias,
    small_out,
    small_shift,
    large_in,
    large_bias,
    large_out,
    large_shift,
    channel_in,
    channel_bias,
    channel_out,
    channel_shift,
    norm_gain,
    norm_shift,
    small_made,
    large_made,
    small_back,
    large_back,
    chan_a,
    chan_b,
    tok_l,
    tok_s,
    vec_out,
    win,
    wout,
    hid,
    slope,
    xin,
    up,
    n1,
    n2,
    u2,
    r2,
    gb1,
    stage,
    h1,
    sl1,
    lgin,
    lgin_t,
    lgout,
    lgout_t,
    sgin,
    sgin_t,
    sgout,
    sgout_t,
    turned,
    lbcol,
    lscol,
    sbcol,
    sscol,
    mid,
    acc,
    raw_a,
    raw_b,
    sums,
    wsem,
    isem,
    usem,
    ysem,
    gsem,
    fs,
    fr,
    bs,
    br,
    sibs,
    rights,
    lefts,
    outsem,
    vsem,
    ready,
    lent,
    tl,
    ts,
    vecs,
    paired,
    pairs,
):
    sections, n, ps, pl_, pp, d, ds_, dc, dp, fused, shared = dims
    place = lax.axis_index("section")
    ahead = lax.rem(place + 1, sections)
    behind = lax.rem(place + sections - 1, sections)
    last = place // (sections - 1)
    first_rows = n * pl_
    half = pl_ // 2
    line = dp // 2 if fused else 1
    rank = lax.axis_index("dp")
    z = rank // 2
    core = rank % 2
    sibling = rank + 1 - 2 * core
    partner = (place + sections // 2) % sections
    giver = place < sections // 2
    taker = place > 0
    owner = (place + sections - 1) // 2 % 2
    foreign = 1 + last

    def weight_copies():
        pairs = (
            (large_in, lgin),
            (large_out, lgout_t),
            (small_in, raw_a.at[0, :, pl.ds(0, ds_)]),
            (small_out, raw_a.at[0, :, pl.ds(ds_, ds_)]),
            (channel_in, win),
            (channel_out, wout),
        )
        return [pltpu.make_async_copy(a, b, wsem.at[k]) for k, (a, b) in enumerate(pairs)]

    def large_copy(src, dst, sem, i):
        return pltpu.make_async_copy(src.at[i], dst.at[pl.ds(pl.multiple_of(i * pl_, 64), pl_)], sem.at[i])

    def small_copy(src, dst, sem, j):
        return pltpu.make_async_copy(src.at[j], dst.at[j], sem.at[n + j])

    copies = weight_copies()

    @pl.when(place == 0)
    def _():
        for i in range(n):
            large_copy(large_images, xin, isem, i).start()

    for c in copies:
        c.start()

    @pl.when(last == 1)
    def _():
        for i in range(n):
            large_copy(large_upstream, up, usem, i).start()
        for j in range(n):
            small_copy(small_upstream, raw_b, usem, j).start()

    barrier = pltpu.get_barrier_semaphore()

    @pl.when(place > 0)
    def _():
        pl.semaphore_signal(barrier, inc=1, device_id={"section": behind}, device_id_type=MESH)

    @pl.when(place < sections - 1)
    def _():
        pl.semaphore_signal(barrier, inc=1, device_id={"section": ahead}, device_id_type=MESH)

    peers = (place + sections - 2) // (sections - 1) + 1 - last
    if fused:
        pl.semaphore_signal(barrier, inc=1, device_id={"dp": sibling}, device_id_type=MESH)
        for k in range(1, line):
            pl.semaphore_signal(barrier, inc=1, device_id={"dp": (rank + 2 * k) % dp}, device_id_type=MESH)
        pl.semaphore_signal(barrier, inc=1, device_id={"section": partner}, device_id_type=MESH)
        peers = peers + line + 1

    def column(row, dst):
        width = up_to(dst.shape[0], 128)
        sums[0:1, 0:width] = jnp.zeros((1, width), F32)
        sums[0:1, 0 : row.shape[1]] = row
        dst[...] = jnp.transpose(jnp.broadcast_to(sums[0:1, 0:width], (128, width)))[0 : dst.shape[0]]

    column(large_bias[...], lbcol)
    column(large_shift[...], lscol)
    column(small_bias[...], sbcol)
    column(small_shift[...], sscol)
    sums[...] = jnp.zeros(sums.shape, F32)
    for c in copies[:4]:
        c.wait()
    for k, padded in enumerate((sgin, sgout_t)):
        padded[...] = jnp.zeros(padded.shape, BF16)
        padded[0:ps, :] = raw_a[0, :, k * ds_ : (k + 1) * ds_]

    @pl.when(place == 0)
    def _():
        for j in range(n):
            small_copy(small_images, raw_a, isem, j).start()

    lgin_t[...] = jnp.transpose(lgin[...])
    sgin_t[...] = jnp.transpose(sgin[...])

    def prepare_backward():
        lgout[...] = jnp.transpose(lgout_t[...])
        sgout[...] = jnp.transpose(sgout_t[...])

    @pl.when(last == 1)
    def _():
        prepare_backward()


    gains = norm_gain[...]
    shifts = norm_shift[...]

    def ahead_copy(rows, size, k):
        return pltpu.make_async_remote_copy(
            src_ref=stage.at[pl.ds(rows, size)],
            dst_ref=xin.at[pl.ds(rows, size)],
            send_sem=fs.at[k],
            recv_sem=fr.at[k],
            device_id={"section": ahead},
            device_id_type=MESH,
        )

    def behind_copy(rows, size, k):
        return pltpu.make_async_remote_copy(
            src_ref=stage.at[pl.ds(rows, size)],
            dst_ref=up.at[pl.ds(rows, size)],
            send_sem=bs.at[k],
            recv_sem=br.at[k],
            device_id={"section": behind},
            device_id_type=MESH,
        )

    class Unit:
        def __init__(self, large, i):
            self.large = large
            self.i = i
            self.rows = pl_ if large else pp
            self.blocks = 2 if large else 1
            self.size = self.rows // self.blocks
            self.some = ROWS if large else pp
            self.base = pl.multiple_of(i * pl_, 64) if large else pl.multiple_of(first_rows + i * pp, 16)
            self.head = pl.multiple_of((i if large else n + i) * ds_, 128)
            self.heads = pl.ds(self.head, ds_)
            self.slot = i * 2 if large else 2 * n + i
            self.gin, self.gin_t = (lgin, lgin_t) if large else (sgin, sgin_t)
            self.gout, self.gout_t = (lgout, lgout_t) if large else (sgout, sgout_t)
            self.bcol, self.scol = (lbcol, lscol) if large else (sbcol, sscol)
            self.mask = large_keep if large else small_keep

        def at(self, offset, size):
            return pl.ds(pl.multiple_of(self.base + offset, 16), size)

        def keep(self, which):
            return self.mask[self.i, which].astype(F32)

        def out_copy(self, which, b):
            sem = (ysem, gsem)[which].at[self.slot + b]
            if self.large:
                dst = (large_made, large_back)[which]
                return pltpu.make_async_copy(
                    stage.at[self.at(b * half, half)], dst.at[self.i, pl.ds(b * half, half)], sem
                )
            src = (raw_a, raw_b)[which]
            dst = (small_made, small_back)[which]
            return pltpu.make_async_copy(src.at[self.i], dst.at[self.i], sem)

    units = 2 * n

    def unit_at(which):
        return (which + core) % 2, which // 2

    def forward(unit, step):
        @pl.when(place == 0)
        def _():
            if unit.large:
                large_copy(large_images, xin, isem, unit.i).wait()
            else:
                small_copy(small_images, raw_a, isem, unit.i).wait()
                xin[unit.at(0, pp)] = jnp.zeros((pp, d), BF16)
                xin[unit.at(0, ps)] = raw_a[unit.i]

        def norm_one(r):
            rows = unit.at(r * unit.some, unit.some)
            x = xin[rows].astype(F32)
            x = x - jnp.mean(x, axis=1, keepdims=True)
            s = lax.rsqrt(jnp.mean(x * x, axis=1, keepdims=True) + EPSILON)
            n1[rows] = (x * s * gains[0:1] + shifts[0:1]).astype(BF16)

        steps = unit.size // unit.some
        for b in range(unit.blocks):

            @pl.when(place > 0)
            def _(b=b):
                ahead_copy(unit.base + b * unit.size, unit.size, unit.slot + b).wait_recv()

            for r in range(b * steps, (b + 1) * steps):
                norm_one(r)
        rows = unit.at(0, unit.rows)
        keep_one = unit.keep(0)
        keep_two = unit.keep(1)
        for c in range(0, d, COLS):
            pre = mm(unit.gin_t[...], n1[rows, c : c + COLS], 1, 0) + unit.bcol[:, 0:1]
            act, slp = gelu_pair(pre)
            h1[unit.heads, c : c + COLS] = act.astype(BF16)
            sl1[unit.heads, c : c + COLS] = slp.astype(BF16)
        for c in range(0, d, COLS):
            branch = mm(unit.gout_t[...], h1[unit.heads, c : c + COLS], 1, 0) + unit.scol[:, 0:1]
            mid[0 : unit.rows, c : c + COLS] = xin[rows, c : c + COLS].astype(F32) + keep_one * branch

        def norm_two(r):
            rows = unit.at(r * unit.some, unit.some)
            x = mid[r * unit.some : (r + 1) * unit.some]
            x = x - jnp.mean(x, axis=1, keepdims=True)
            s = lax.rsqrt(jnp.mean(x * x, axis=1, keepdims=True) + EPSILON)
            x = x * s
            u2[rows] = x.astype(BF16)
            r2[rows] = jnp.broadcast_to(s, (unit.some, 128))
            n2[rows] = (x * gains[1:2] + shifts[1:2]).astype(BF16)

        for r in range(unit.rows // unit.some):
            norm_two(r)

        @pl.when(step == 0)
        def _():
            for c in copies[4:]:
                c.wait()

        for b in range(unit.blocks):
            size = unit.size
            rows = unit.at(b * size, size)
            here = slice(b * size, (b + 1) * size)
            total = channel_shift[...]
            parts = [slice(c, c + COLS) for c in range(0, dc, COLS)]
            ahead_of = mm(n2[rows], win[:, parts[0]], 1, 0)
            acts = []
            for c, cols in enumerate(parts):
                pre = ahead_of + channel_bias[:, cols]
                if c + 1 < len(parts):
                    ahead_of = mm(n2[rows], win[:, parts[c + 1]], 1, 0)
                act, slp = gelu_pair(pre)
                acts.append(act.astype(BF16))
                hid[rows, cols] = acts[-1]
                slope[rows, cols] = slp.astype(BF16)
                if cols.stop % WIDE == 0:
                    total = total + mm(jnp.concatenate(acts, axis=1), wout[cols.stop - WIDE : cols.stop, :], 1, 0)
                    acts = []
            y = (mid[here] + keep_two * total).astype(BF16)
            stage[rows] = y
            if not unit.large:
                raw_a[unit.i] = y[0:ps]

            if b == 0:

                @pl.when(step == 0)
                def _():
                    pl.semaphore_wait(barrier, peers)

            @pl.when(place < sections - 1)
            def _(b=b, size=size):
                ahead_copy(unit.base + b * size, size, unit.slot + b).start()

            if unit.large or not fused:
                unit.out_copy(0, b).start()

    def backward(unit):
        @pl.when(last == 1)
        def _():
            if unit.large:
                large_copy(large_upstream, up, usem, unit.i).wait()
            else:
                small_copy(small_upstream, raw_b, usem, unit.i).wait()
                up[unit.at(0, pp)] = jnp.zeros((pp, d), BF16)
                up[unit.at(0, ps)] = raw_b[unit.i]

        keep_one = unit.keep(0)
        keep_two = unit.keep(1)
        size = unit.size
        for b in range(unit.blocks):
            rows = unit.at(b * size, size)
            here = slice(b * size, (b + 1) * size)

            @pl.when(place < sections - 1)
            def _(b=b):
                ahead_copy(unit.base + b * size, size, unit.slot + b).wait_send()

            if unit.large or not fused:
                unit.out_copy(0, b).wait()

            @pl.when(last == 0)
            def _(b=b):
                behind_copy(unit.base + b * size, size, unit.slot + b).wait_recv()

            stage[rows] = up[rows] * keep_two.astype(BF16)

            parts = [slice(c, c + COLS) for c in range(0, dc, COLS)]
            total = None
            ahead_of = mm(stage[rows], wout[parts[0], :], 1, 1)
            grads = []
            for c, cols in enumerate(parts):
                grad = ahead_of
                if c + 1 < len(parts):
                    ahead_of = mm(stage[rows], wout[parts[c + 1], :], 1, 1)
                grads.append((grad * slope[rows, cols].astype(F32)).astype(BF16))
                slope[rows, cols] = grads[-1]
                if cols.stop % WIDE == 0:
                    term = mm(jnp.concatenate(grads, axis=1), win[:, cols.stop - WIDE : cols.stop], 1, 1)
                    total = term if total is None else total + term
                    grads = []
            acc[here] = total

        def norm_two(r):
            offset = r * unit.some
            rows = unit.at(offset, unit.some)
            local = slice(offset, offset + unit.some)
            h = acc[local]
            u = u2[rows].astype(F32)
            s = r2[rows][:, 0:1]
            g = up[rows].astype(F32)
            q = h * gains[1:2]
            first = jnp.mean(q, axis=1, keepdims=True)
            second = jnp.mean(q * u, axis=1, keepdims=True)
            g_mid = g + s * (q - first - u * second)
            mid[local] = g_mid
            gb1[rows] = (keep_one * g_mid).astype(BF16)
            up[rows] = (keep_two * g).astype(BF16)
            return groups(h * u), groups(h)

        parts = [norm_two(r) for r in range(unit.rows // unit.some)]
        sums[8:16, 0:d] += sum(p[0] for p in parts)
        sums[24:32, 0:d] += sum(p[1] for p in parts)
        rows = unit.at(0, unit.rows)
        for c in range(0, d, COLS):
            grad = mm(unit.gout[...], gb1[rows, c : c + COLS], 1, 0)
            grad = (grad * sl1[unit.heads, c : c + COLS].astype(F32)).astype(BF16)
            sl1[unit.heads, c : c + COLS] = grad
        for c in range(0, d, COLS):
            acc[0 : unit.rows, c : c + COLS] = mm(unit.gin[...], sl1[unit.heads, c : c + COLS], 1, 0)

        def norm_one(r):
            offset = r * unit.some
            rows = unit.at(offset, unit.some)
            local = slice(offset, offset + unit.some)
            x = xin[rows].astype(F32)
            x = x - jnp.mean(x, axis=1, keepdims=True)
            s = lax.rsqrt(jnp.mean(x * x, axis=1, keepdims=True) + EPSILON)
            u = x * s
            h = acc[local]
            q = h * gains[0:1]
            first = jnp.mean(q, axis=1, keepdims=True)
            second = jnp.mean(q * u, axis=1, keepdims=True)
            stage[rows] = (mid[local] + s * (q - first - u * second)).astype(BF16)
            return groups(h * u), groups(h)

        steps = size // unit.some
        for b in range(unit.blocks):
            parts = [norm_one(r) for r in range(b * steps, (b + 1) * steps)]
            sums[0:8, 0:d] += sum(p[0] for p in parts)
            sums[16:24, 0:d] += sum(p[1] for p in parts)
            if not unit.large:
                raw_b[unit.i] = stage[unit.at(0, ps)]

            @pl.when(place > 0)
            def _(b=b):
                behind_copy(unit.base + b * size, size, unit.slot + b).start()

            if unit.large or not fused:
                unit.out_copy(1, b).start()

    piece = d // dp
    tok_piece = ds_ // dp

    def turn(src):
        def some(rows, size):
            value = jnp.transpose(src[pl.ds(rows, size)])
            if not fused:
                turned[:, pl.ds(rows, size)] = value
                return
            for b in range(dp):
                at = ((b % 2) * line + b // 2) * piece
                turned[at : at + piece, pl.ds(rows, size)] = value[b * piece : (b + 1) * piece]

        def full(r, carry):
            some(pl.multiple_of(r * 128, 128), 128)
            return carry

        whole = src.shape[0] // 128
        lax.fori_loop(0, whole, full, 0)
        if src.shape[0] % 128:
            some(whole * 128, src.shape[0] % 128)


    def step(t, carry):
        back = (1 - last) * (t // units) + last * (t % 2)
        which = (1 - last) * (t % units) + last * (t // 2)
        small, i = unit_at(which)

        @pl.when((t == units) & (last == 0))
        def _():
            prepare_backward()

        @pl.when(t == 2 * units - 1)
        def _():
            turn(n2)

        @pl.when((back == 0) & (small == 0))
        def _():
            forward(Unit(True, i), t)

        @pl.when((back == 0) & (small == 1))
        def _():
            forward(Unit(False, i), t)

        @pl.when((back == 1) & (small == 0))
        def _():
            backward(Unit(True, i))

        @pl.when((back == 1) & (small == 1))
        def _():
            backward(Unit(False, i))

        return carry

    lax.fori_loop(0, 2 * units, step, 0)

    total = hid.shape[0]
    chunks = dc // d
    count = 2 * chunks + 2
    kinds = (chunks, chunks, 1, 1, shared)
    first_of = (0, chunks + 2, chunks, chunks + 1, count + 1)
    large_width, small_width = up_to(pl_, 128), up_to(pp, 128)
    widths = (d, d, large_width, small_width, d)
    own = line
    across = line + 1

    def columns(kind, k):
        if kind < 2:
            return pl.ds(pl.multiple_of(k * d, 128), d)
        return pl.ds(0, widths[kind])

    def own_rows(kind):
        return ((slope, 0), (hid, 0), (up, 0), (up, d))[kind]

    def weight_product(kind, k):
        src = (slope, hid)[kind]

        def part(j, carry):
            cols = pl.ds(pl.multiple_of(k * d + j * COLS, COLS), COLS)
            if kind == 0:
                bias = mm(jnp.ones((8, total), BF16), src[:, cols], 1, 0)[0:1]
                vecs[own, pl.ds(k, 1), pl.ds(pl.multiple_of(j * COLS, COLS), COLS)] = bias
            src[0:d, cols] = mm(turned[...], src[:, cols], 1, 0).astype(BF16)
            return carry

        lax.fori_loop(0, d // COLS, part, 0)

    def token_product(large):
        unit_rows = pl_ if large else pp
        ones_d = jnp.ones((8, d), BF16)
        out_grad = in_grad = bias = shift = None
        for k in range(n):
            base = k * pl_ if large else first_rows + k * pp
            head = k * ds_ if large else (n + k) * ds_
            g = gb1[base : base + unit_rows]
            x = n1[base : base + unit_rows]
            h = h1[head : head + ds_]
            p = sl1[head : head + ds_]
            terms = (mm(p, x, 1, 1), mm(h, g, 1, 1), mm(ones_d, p, 1, 1), mm(ones_d, g, 1, 1))
            if k == 0:
                in_grad, out_grad, bias, shift = terms
            else:
                in_grad, out_grad, bias, shift = in_grad + terms[0], out_grad + terms[1], bias + terms[2], shift + terms[3]
        src, base = own_rows(2 if large else 3)
        for at, value in ((0, in_grad), (1, out_grad)):
            value = value.astype(BF16)
            if not fused:
                src[base + at * ds_ : base + (at + 1) * ds_, 0:unit_rows] = value
                continue
            for b in range(dp):
                to = base + ((b % 2) * line + b // 2) * piece + at * tok_piece
                src[to : to + tok_piece, 0:unit_rows] = value[b * tok_piece : (b + 1) * tok_piece]
        row = chunks + 5 + (0 if large else 2)
        vecs[own, row : row + 1, 0:ds_] = bias[0:1]
        vecs[own, row + 1 : row + 2, 0:unit_rows] = shift[0:1]

    def product(kind, k):
        if kind == 2:
            turn(up)
            vecs[own, chunks : chunks + 1] = mm(jnp.ones((8, total), BF16), up[...], 1, 0)[0:1]
            for j in range(4):
                vecs[own, chunks + 1 + j : chunks + 2 + j] = jnp.sum(sums[8 * j : 8 * j + 8], axis=0, keepdims=True)
        if kind < 2:
            weight_product(kind, k)
        else:
            token_product(kind == 2)

    def ways(step_of, kept=False):
        def at(c, valid=True):
            for kind in range(5 if fused else 4):
                low, high = first_of[kind], first_of[kind] + kinds[kind]
                here = (c >= low) & (c < high) & valid
                if kind == 4:
                    here = here & taker & (c < low + foreign)
                if kind == 0 and kept:
                    here = here & ((place >= sections // 2) | (c < 1) | (c > shared))

                @pl.when(here)
                def _(kind=kind, low=low):
                    step_of(kind, c - low)

        return at

    vecs[own] = jnp.zeros(vecs.shape[1:], F32)
    if not fused:

        def whole_copies(kind, k):
            src, base = own_rows(kind)
            if kind < 2:
                cols = columns(kind, k)
                dst = (chan_a, chan_b)[kind]
                return [pltpu.make_async_copy(src.at[pl.ds(0, d), cols], dst.at[:, cols], outsem.at[first_of[kind] + k])]
            cols = pl.ds(0, widths[kind])
            dst = (tok_l, tok_s)[kind - 2]
            return [pltpu.make_async_copy(src.at[pl.ds(base, d), cols], dst, outsem.at[first_of[kind]])]

        def one(kind, k):
            product(kind, k)
            for c in whole_copies(kind, k):
                c.start()

        def finish(kind, k):
            for c in whole_copies(kind, k):
                c.wait()

        def run(c, carry):
            ways(one)(c)
            return carry

        def end(c, carry):
            ways(finish)(c)
            return carry

        lax.fori_loop(0, count, run, 0)
        lax.fori_loop(0, count, end, 0)
        vec_out[...] = vecs[own]
    else:
        rightward, leftward = (rank + 2) % dp, (rank + dp - 2) % dp

        def mine(kind, k, to):
            if kind == 4:
                return h1.at[pl.ds(pl.multiple_of((k * line + to) * piece, 16), piece)]
            src, base = own_rows(kind)
            return src.at[pl.ds(pl.multiple_of(base + (core * line + to) * piece, 16), piece), columns(kind, k)]

        def crossing(kind, k, rows, size):
            ref, base = ((win, 0), (win, d // 2), (wout, 3 * d), (wout, 3 * d + d // 2))[kind]
            return ref.at[pl.ds(pl.multiple_of(base + rows, 16), size), columns(kind, k)]

        def from_left(kind, k, to):
            ref, base = ((wout, 0), (wout, chunks * (line - 1)), (n2, 0), (n2, line - 1), (sl1, 0))[kind]
            rows = (base + k * (line - 1) + to - 1) * piece
            return ref.at[pl.ds(pl.multiple_of(rows, 16), piece), pl.ds(0, widths[kind])]

        def from_right(kind, k, to):
            ref, base = ((xin, 0), (u2, 0), (n2, 2 * (line - 1)), (n2, 3 * (line - 1)), (sl1, shared * (line - 1)))[kind]
            rows = (base + k * (line - 1) + to) * piece
            return ref.at[pl.ds(pl.multiple_of(rows, 16), piece), pl.ds(0, widths[kind])]

        def sem_of(kind, k, to):
            return ((count if kind == 4 else first_of[kind]) + k) * line + to

        def cross_copy(kind, k):
            src, base = own_rows(kind)
            rows = pl.ds(pl.multiple_of(base + (1 - core) * line * piece, 16), line * piece)
            c = first_of[kind] + k
            return pltpu.make_async_remote_copy(
                src_ref=src.at[rows, columns(kind, k)],
                dst_ref=crossing(kind, k, 0, line * piece),
                send_sem=sibs.at[0, c],
                recv_sem=sibs.at[1, c],
                device_id={"dp": sibling},
                device_id_type=MESH,
            )

        def right_copy(kind, k, to):
            return pltpu.make_async_remote_copy(
                src_ref=mine(kind, k, to),
                dst_ref=from_left(kind, k, to),
                send_sem=rights.at[0, sem_of(kind, k, to)],
                recv_sem=rights.at[1, sem_of(kind, k, to)],
                device_id={"dp": rightward},
                device_id_type=MESH,
            )

        def left_copy(kind, k, to):
            return pltpu.make_async_remote_copy(
                src_ref=mine(kind, k, to),
                dst_ref=from_right(kind, k, to),
                send_sem=lefts.at[0, sem_of(kind, k, to)],
                recv_sem=lefts.at[1, sem_of(kind, k, to)],
                device_id={"dp": leftward},
                device_id_type=MESH,
            )

        def chip_sum(kind, k, to):
            if kind == 4:
                return mine(kind, k, to)[...].astype(F32)
            return mine(kind, k, to)[...].astype(F32) + crossing(kind, k, to * piece, piece)[...].astype(F32)

        def flow_right(kind, k):
            def one(j, carry):
                to = line - 1 - j

                @pl.when(z == 0)
                def _():
                    mine(kind, k, to)[...] = chip_sum(kind, k, to).astype(BF16)

                @pl.when(z > 0)
                def _():
                    right_copy(kind, k, to).wait_recv()
                    value = chip_sum(kind, k, to) + from_left(kind, k, to)[...].astype(F32)
                    mine(kind, k, to)[...] = value.astype(BF16)

                right_copy(kind, k, to).start()
                return carry

            lax.fori_loop(0, line - 1 - z, one, 0)

        def flow_left(kind, k):
            def one(to, carry):
                @pl.when(z == line - 1)
                def _():
                    mine(kind, k, to)[...] = chip_sum(kind, k, to).astype(BF16)

                @pl.when(z < line - 1)
                def _():
                    left_copy(kind, k, to).wait_recv()
                    value = chip_sum(kind, k, to) + from_right(kind, k, to)[...].astype(F32)
                    mine(kind, k, to)[...] = value.astype(BF16)

                left_copy(kind, k, to).start()
                return carry

            lax.fori_loop(0, z, one, 0)

        def out_stage(kind, k):
            if kind == 0:
                return mid.at[pl.ds(pl.multiple_of(k * piece, 16), piece)]
            if kind in (1, 4):
                at = k + (chunks if kind == 4 else 0)
                return acc.at[pl.ds(pl.multiple_of(at * piece, 16), piece)]
            return (tl, ts)[kind - 2]

        def out_copies(kind, k):
            c = first_of[kind] + k
            if kind < 2:
                dst = (chan_a, chan_b)[kind].at[:, columns(kind, k)]
            else:
                dst = (tok_l, tok_s)[kind - 2]
            return pltpu.make_async_copy(out_stage(kind, k), dst, outsem.at[c])

        def gather(kind, k):
            width = (d, d, pl_, ps, d)[kind]
            dst = out_stage(kind, k)
            dst[...] = chip_sum(kind, k, z)[:, 0:width]

            @pl.when(z > 0)
            def _():
                right_copy(kind, k, z).wait_recv()
                dst[...] += from_left(kind, k, z)[...].astype(F32)[:, 0:width]

            @pl.when(z < line - 1)
            def _():
                left_copy(kind, k, z).wait_recv()
                dst[...] += from_right(kind, k, z)[...].astype(F32)[:, 0:width]

            if kind == 4:
                give_back(k).start()
            else:
                out_copies(kind, k).start()

        def lend_copy(j, f, to):
            rows = pl.ds(pl.multiple_of(core * line * piece, 16), line * piece)
            return pltpu.make_async_remote_copy(
                src_ref=slope.at[rows, columns(0, j + 1)],
                dst_ref=h1.at[pl.ds(pl.multiple_of(f * line * piece, 16), line * piece)],
                send_sem=lent.at[0, j],
                recv_sem=lent.at[1, f],
                device_id={"section": to},
                device_id_type=MESH,
            )

        def return_copy(f, j, to):
            return pltpu.make_async_remote_copy(
                src_ref=out_stage(4, f),
                dst_ref=out_stage(0, j + 1),
                send_sem=lent.at[2, f],
                recv_sem=lent.at[3, j],
                device_id={"section": to},
                device_id_type=MESH,
            )

        def lend_away(j):
            return lend_copy(j, place * j, (1 - place) * (2 - j) + place * 3)

        def give_back(f):
            return return_copy(f, f + (2 - place) * (1 - last), owner)

        def lend(c):
            @pl.when(giver & (c >= 1) & (c <= shared))
            def _():
                @pl.when(c == 1)
                def _():
                    pl.semaphore_wait(ready.at[3], 1)

                @pl.when((c == 2) & (place == 0))
                def _():
                    pl.semaphore_wait(ready.at[6], 1)

                def one(to, carry):
                    mine(0, c, to)[...] = chip_sum(0, c, to).astype(BF16)
                    return carry

                lax.fori_loop(0, line, one, 0)
                lend_away(c - 1).start()

        def pair_copy(which):
            return pltpu.make_async_copy(paired, (small_made, small_back)[which], pairs.at[which])

        def pair(which):
            if which:
                pair_copy(0).wait()
            src = (raw_a, raw_b)[which]
            for r in range(0, ps, 32):
                rows = slice(r, min(r + 32, ps))
                images = [src[j, rows].astype(F32)[:, None, :] for j in range(n)]
                paired[rows] = jnp.concatenate(images, axis=1).astype(BF16)
            pair_copy(which).start()

        def vec_cross():
            return pltpu.make_async_remote_copy(
                src_ref=vecs.at[own],
                dst_ref=vecs.at[across],
                send_sem=vsem.at[0, 0],
                recv_sem=vsem.at[1, 0],
                device_id={"dp": sibling},
                device_id_type=MESH,
            )

        def vec_copy(k):
            return pltpu.make_async_remote_copy(
                src_ref=vecs.at[z],
                dst_ref=vecs.at[z],
                send_sem=vsem.at[0, k],
                recv_sem=vsem.at[1, k],
                device_id={"dp": (rank + 2 * k) % dp},
                device_id_type=MESH,
            )

        def first(kind, k):
            if kind == 4:

                @pl.when(k == 0)
                def _():
                    @pl.when(z < line - 1)
                    def _():
                        pl.semaphore_wait(ready.at[4], 1)

                    @pl.when(z > 0)
                    def _():
                        pl.semaphore_wait(ready.at[5], 1)

                lend_copy(0, k, owner).wait_recv()
                return
            product(kind, k)
            if kind == 3:

                @pl.when(taker)
                def _():
                    for at, here in ((6, place == 1), (3, place > 1)):

                        @pl.when(here)
                        def _(at=at):
                            pl.semaphore_signal(ready.at[at], inc=1, device_id={"section": owner}, device_id_type=MESH)

                    @pl.when(z > 0)
                    def _():
                        pl.semaphore_signal(ready.at[4], inc=1, device_id={"dp": leftward}, device_id_type=MESH)

                    @pl.when(z < line - 1)
                    def _():
                        pl.semaphore_signal(ready.at[5], inc=1, device_id={"dp": rightward}, device_id_type=MESH)

            if kind == 0:

                @pl.when(k == 0)
                def _():
                    pl.semaphore_wait(ready.at[0], 1)

                    @pl.when(z < line - 1)
                    def _():
                        pl.semaphore_wait(ready.at[1], 1)

                    @pl.when(z > 0)
                    def _():
                        pl.semaphore_wait(ready.at[2], 1)

            cross_copy(kind, k).start()

        def crossed(kind, k):
            if kind < 4:
                cross_copy(kind, k).wait_recv()

        def finish(kind, k):
            if kind == 4:
                give_back(k).wait_send()
            else:
                cross_copy(kind, k).wait_send()
                out_copies(kind, k).wait()

            def right(j, carry):
                right_copy(kind, k, line - 1 - j).wait_send()
                return carry

            def left(to, carry):
                left_copy(kind, k, to).wait_send()
                return carry

            sent = line - 1 - z, z
            if kind == 0:
                away = giver & (k >= 1) & (k <= shared)
                own_line = 1 - away.astype(jnp.int32)
                sent = sent[0] * own_line, sent[1] * own_line
            lax.fori_loop(0, sent[0], right, 0)
            lax.fori_loop(0, sent[1], left, 0)

        pl.semaphore_signal(ready.at[0], inc=1, device_id={"dp": sibling}, device_id_type=MESH)

        @pl.when(z > 0)
        def _():
            pl.semaphore_signal(ready.at[1], inc=1, device_id={"dp": leftward}, device_id_type=MESH)

        @pl.when(z < line - 1)
        def _():
            pl.semaphore_signal(ready.at[2], inc=1, device_id={"dp": rightward}, device_id_type=MESH)

        def run(c, carry):
            ways(crossed)(c - 1)
            lend(c - 1)
            ways(flow_right, True)(c - 1 - z, z < line - 1)
            ways(flow_left, True)(c - line + z, z > 0)
            ways(first)(c)

            @pl.when(c == count)
            def _():
                vec_cross().start()

            @pl.when(c == count + 1)
            def _():
                vec_cross().wait()
                vecs[z] = vecs[own] + vecs[across]
                for k in range(1, line):
                    vec_copy(k).start()

            for which in range(2):

                @pl.when(c == count - 2 + which)
                def _(which=which):
                    pair(which)

            ways(gather, True)(c - line - 1)
            return carry

        steps = count + 1 + shared
        lax.fori_loop(0, steps + line + 1, run, 0)

        @pl.when(giver)
        def _():
            for k in range(shared):
                lend_away(k).wait_send()
                return_copy(0, k, owner).wait_recv()
                out_copies(0, k + 1).start()

        def end(c, carry):
            ways(finish)(c)
            return carry

        lax.fori_loop(0, steps, end, 0)
        pair_copy(1).wait()
        for k in range(1, line):
            vec_copy(k).wait()
        value = vecs[0]
        for k in range(1, line):
            value = value + vecs[k]
        vec_out[...] = value

    for i in range(2 * n):
        unit = Unit(i < n, i % n)
        for b in range(unit.blocks):
            if unit.large or not fused:
                unit.out_copy(1, b).wait()

            @pl.when(place > 0)
            def _(b=b, unit=unit):
                behind_copy(unit.base + b * unit.size, unit.size, unit.slot + b).wait_send()


def finish_kernel(tok_piece, d, chunks, moved, *refs):
    sources, (tok_l, tok_s, vec), rest = refs[:moved], refs[moved : moved + 3], refs[moved + 3 :]
    outs, vias, sem = rest[: -moved - 1], rest[-moved - 1 : -1], rest[-1]
    bring = [pltpu.make_async_copy(a, b, sem.at[0, k]) for k, (a, b) in enumerate(zip(sources, vias))]
    take = [pltpu.make_async_copy(a, b, sem.at[1, k]) for k, (a, b) in enumerate(zip(vias, outs[:moved]))]
    for c in bring:
        c.start()
    outs = outs[moved:]
    for k, src in enumerate((tok_l, tok_s)):
        outs[2 * k][...] = src[0:tok_piece]
        outs[2 * k + 1][...] = src[tok_piece:]
    for k in range(chunks):
        outs[4][:, k * d : (k + 1) * d] = vec[k : k + 1]
    at = chunks
    for out in outs[5:]:
        rows, width = out.shape
        out[...] = vec[at : at + rows, 0:width]
        at += rows
    for a, b in zip(bring, take):
        a.wait()
        b.start()
    for c in take:
        c.wait()


def local(
    small_images,
    large_images,
    small_upstream,
    large_upstream,
    small_keep,
    large_keep,
    small_in,
    small_bias,
    small_out,
    small_shift,
    large_in,
    large_bias,
    large_out,
    large_shift,
    channel_in,
    channel_bias,
    channel_out,
    channel_shift,
    norm_gain,
    norm_shift,
):
    sections = lax.axis_size("section")
    micro, imgs, ps, d = small_images.shape
    pl_ = large_images.shape[2]
    n = micro * imgs
    ds_ = small_in.shape[2]
    dc = channel_in.shape[2]
    pp = up_to(ps, 16)
    rows = n * (pl_ + pp)
    small_width, large_width = up_to(pp, 128), up_to(pl_, 128)
    dp = lax.axis_size("dp")
    piece, tok_piece = d // dp, ds_ // dp
    fused = d % (16 * dp) == 0 and ds_ % (16 * dp) == 0 and dc == 4 * d and d == 2 * ds_ and 2 * dp * piece <= rows
    fused = fused and sections == 4
    shared = 2
    dims = (sections, n, ps, pl_, pp, d, ds_, dc, dp, fused, shared)
    chunks = dc // d
    line = dp // 2 if fused else 1
    count = 2 * chunks + 2
    vec_rows = up_to(chunks + 9, 8)
    any_ = pl.BlockSpec(memory_space=pl.ANY)
    vmem = pl.BlockSpec(memory_space=pltpu.VMEM)
    smem = pl.BlockSpec(memory_space=pltpu.SMEM)
    block = max(pl_, n * pp)
    blocks = 2 * n + n
    scratch = [
        pltpu.VMEM((d, dc), BF16),
        pltpu.VMEM((dc, d), BF16),
        pltpu.VMEM((rows, dc), BF16),
        pltpu.VMEM((rows, dc), BF16),
        pltpu.VMEM((rows, d), BF16),
        pltpu.VMEM((rows, d), BF16),
        pltpu.VMEM((rows, d), BF16),
        pltpu.VMEM((rows, d), BF16),
        pltpu.VMEM((rows, d), BF16),
        pltpu.VMEM((rows, 128), F32),
        pltpu.VMEM((rows, d), BF16),
        pltpu.VMEM((rows, d), BF16),
        pltpu.VMEM((2 * n * ds_, d), BF16),
        pltpu.VMEM((2 * n * ds_, d), BF16),
        pltpu.VMEM((pl_, ds_), BF16),
        pltpu.VMEM((ds_, pl_), BF16),
        pltpu.VMEM((ds_, pl_), BF16),
        pltpu.VMEM((pl_, ds_), BF16),
        pltpu.VMEM((pp, ds_), BF16),
        pltpu.VMEM((ds_, pp), BF16),
        pltpu.VMEM((ds_, pp), BF16),
        pltpu.VMEM((pp, ds_), BF16),
        pltpu.VMEM((d, rows), BF16),
        pltpu.VMEM((ds_, 128), F32),
        pltpu.VMEM((pl_, 128), F32),
        pltpu.VMEM((ds_, 128), F32),
        pltpu.VMEM((pp, 128), F32),
        pltpu.VMEM((block, d), F32),
        pltpu.VMEM((block, d), F32),
        pltpu.VMEM((n, ps, d), BF16),
        pltpu.VMEM((n, ps, d), BF16),
        pltpu.VMEM((32, d), F32),
        pltpu.SemaphoreType.DMA((6,)),
        pltpu.SemaphoreType.DMA((2 * n,)),
        pltpu.SemaphoreType.DMA((2 * n,)),
        pltpu.SemaphoreType.DMA((blocks,)),
        pltpu.SemaphoreType.DMA((blocks,)),
        pltpu.SemaphoreType.DMA((blocks,)),
        pltpu.SemaphoreType.DMA((blocks,)),
        pltpu.SemaphoreType.DMA((blocks,)),
        pltpu.SemaphoreType.DMA((blocks,)),
        pltpu.SemaphoreType.DMA((2, count)),
        pltpu.SemaphoreType.DMA((2, (count + shared) * line)),
        pltpu.SemaphoreType.DMA((2, (count + shared) * line)),
        pltpu.SemaphoreType.DMA((count,)),
        pltpu.SemaphoreType.DMA((2, line)),
        pltpu.SemaphoreType.REGULAR((7,)),
        pltpu.SemaphoreType.DMA((4, shared)),
        pltpu.VMEM((2 * tok_piece, pl_), F32),
        pltpu.VMEM((2 * tok_piece, ps), F32),
        pltpu.VMEM((line + 2, vec_rows, d), F32),
        pltpu.VMEM((ps, n, d) if fused else (8, 128), BF16),
        pltpu.SemaphoreType.DMA((2,)),
    ]
    if fused:
        reduced = (
            jax.ShapeDtypeStruct((piece, dc), F32),
            jax.ShapeDtypeStruct((piece, dc), F32),
            jax.ShapeDtypeStruct((2 * tok_piece, pl_), F32),
            jax.ShapeDtypeStruct((2 * tok_piece, ps), F32),
        )
    else:
        reduced = (
            jax.ShapeDtypeStruct((d, dc), BF16),
            jax.ShapeDtypeStruct((d, dc), BF16),
            jax.ShapeDtypeStruct((d, large_width), BF16),
            jax.ShapeDtypeStruct((d, small_width), BF16),
        )
    small_shape = (ps, n, d) if fused else (n, ps, d)
    outs = (
        jax.ShapeDtypeStruct(small_shape, BF16),
        jax.ShapeDtypeStruct((n, pl_, d), BF16),
        jax.ShapeDtypeStruct(small_shape, BF16),
        jax.ShapeDtypeStruct((n, pl_, d), BF16),
        *reduced,
        jax.ShapeDtypeStruct((vec_rows, d), F32),
    )
    made_s, made_l, back_s, back_l, chan_a, chan_b, tok_l, tok_s, vec = pl.pallas_call(
        functools.partial(kernel, dims),
        out_shape=outs,
        in_specs=[any_] * 4
        + [smem] * 2
        + [any_, vmem, any_, vmem] * 2
        + [any_, vmem, any_, vmem]
        + [vmem, vmem],
        out_specs=(any_,) * 8 + (vmem,),
        scratch_shapes=scratch,
        compiler_params=pltpu.CompilerParams(
            collective_id=0, has_side_effects=True, vmem_limit_bytes=65400 * 1024
        ),
        cost_estimate=pl.CostEstimate(flops=50 * 10**9, bytes_accessed=40 * 10**6, transcendentals=10**7),
    )(
        small_images.reshape(n, ps, d),
        large_images.reshape(n, pl_, d),
        small_upstream.reshape(n, ps, d),
        large_upstream.reshape(n, pl_, d),
        small_keep.reshape(n, 2),
        large_keep.reshape(n, 2),
        small_in[0],
        small_bias,
        small_out[0].T,
        small_shift,
        large_in[0],
        large_bias,
        large_out[0].T,
        large_shift,
        channel_in[0],
        channel_bias,
        channel_out[0],
        channel_shift,
        norm_gain[0],
        norm_shift[0],
    )
    if fused:
        large = (made_l, back_l, chan_a, chan_b, made_s, back_s)
        final = [jax.ShapeDtypeStruct(x.shape, x.dtype) for x in large]
        final += [jax.ShapeDtypeStruct((tok_piece, width), F32) for width in (pl_, pl_, ps, ps)]
        final += [
            jax.ShapeDtypeStruct(shape, F32)
            for shape in ((1, dc), (1, d), (2, d), (2, d), (1, ds_), (1, pl_), (1, ds_), (1, ps))
        ]
        made_l, back_l, chan_a, chan_b, made_s, back_s, lin, lout, sin, sout, *vecs = pl.pallas_call(
            functools.partial(finish_kernel, tok_piece, d, chunks, len(large)),
            out_shape=final,
            in_specs=[any_] * len(large) + [vmem] * 3,
            out_specs=[any_] * len(large) + [vmem] * 12,
            scratch_shapes=[pltpu.VMEM(x.shape, x.dtype) for x in large] + [pltpu.SemaphoreType.DMA((2, len(large)))],
            compiler_params=pltpu.CompilerParams(vmem_limit_bytes=65400 * 1024),
        )(*large, tok_l, tok_s, vec)
        cbias, cshift, gain, shift, lbias, lshift, sbias, sshift = vecs
        made_s, back_s = (x.transpose(1, 0, 2) for x in (made_s, back_s))
    else:
        chan_a, chan_b = (lax.psum_scatter(x, "dp", scatter_dimension=0, tiled=True).astype(F32) for x in (chan_a, chan_b))
        tok = jnp.concatenate([tok_l, tok_s], axis=1).reshape(2, ds_, large_width + small_width)
        tok = lax.psum_scatter(tok, "dp", scatter_dimension=1, tiled=True).astype(F32)
        lin, lout, sin, sout = tok[0, :, 0:pl_], tok[1, :, 0:pl_], tok[0, :, large_width:], tok[1, :, large_width:]
        sin, sout = sin[:, 0:ps], sout[:, 0:ps]
        vec = lax.psum(vec, "dp")
        at = chunks
        cbias, cshift = vec[0:at].reshape(1, dc), vec[at : at + 1]
        gain, shift = vec[at + 1 : at + 3], vec[at + 3 : at + 5]
        lbias, lshift = vec[at + 5 : at + 6, 0:ds_], vec[at + 6 : at + 7, 0:pl_]
        sbias, sshift = vec[at + 7 : at + 8, 0:ds_], vec[at + 8 : at + 9, 0:ps]
    return (
        made_s.reshape(1, micro, imgs, ps, d),
        made_l.reshape(1, micro, imgs, pl_, d),
        back_s.reshape(1, micro, imgs, ps, d),
        back_l.reshape(1, micro, imgs, pl_, d),
        sin.T[None],
        sbias,
        sout[None],
        sshift,
        lin.T[None],
        lbias,
        lout[None],
        lshift,
        chan_a[None],
        cbias,
        chan_b.T[None],
        cshift,
        gain[None],
        shift[None],
    )


def solution(mesh):
    placed = (
        (P(None, "dp", None, None),) * 4
        + (P("section", None, "dp", None),) * 2
        + (P("section", None, None), P("section", None)) * 6
        + (P("section", None, None),) * 2
    )
    outs = (
        (P("section", None, "dp", None, None),) * 4
        + (P("section", None, "dp"), P("section", None), P("section", "dp", None), P("section", None)) * 2
        + (P("section", "dp", None), P("section", None), P("section", None, "dp"), P("section", None))
        + (P("section", None, None),) * 2
    )
    return jax.shard_map(local, mesh=mesh, in_specs=placed, out_specs=outs, check_vma=False)
```

```python
import functools

import jax
import jax.numpy as jnp
from jax import lax
from jax.experimental import pallas as pl
from jax.experimental.pallas import tpu as pltpu
from jax.sharding import PartitionSpec as P

MESH = pl.DeviceIdType.MESH
F32 = jnp.float32
BF16 = jnp.bfloat16
EPSILON = 1e-06
DENSITY = 0.3989422804014327
ROWS = 144
COLS = 256
WIDE = 1024


def up_to(value, step):
    return -(-value // step) * step


def mm(a, b, ca, cb):
    return lax.dot_general(a, b, (((ca,), (cb,)), ((), ())), preferred_element_type=F32)


def gelu_pair(v):
    cdf = 0.5 + 0.5 * lax.erf(v * 0.7071067811865476)
    bell = jnp.exp2((v * v) * (-0.5 * 1.4426950408889634))
    return v * cdf, cdf + (v * DENSITY) * bell


def groups(x):
    return x.reshape(x.shape[0] // 8, 8, x.shape[1]).sum(0)


def kernel(
    dims,
    small_images,
    large_images,
    small_upstream,
    large_upstream,
    small_keep,
    large_keep,
    small_in,
    small_bias,
    small_out,
    small_shift,
    large_in,
    large_bias,
    large_out,
    large_shift,
    channel_in,
    channel_bias,
    channel_out,
    channel_shift,
    norm_gain,
    norm_shift,
    small_made,
    large_made,
    small_back,
    large_back,
    chan_a,
    chan_b,
    tok_l,
    tok_s,
    vec_out,
    win,
    wout,
    hid,
    slope,
    xin,
    up,
    n1,
    n2,
    u2,
    r2,
    gb1,
    stage,
    h1,
    sl1,
    lgin,
    lgin_t,
    lgout,
    lgout_t,
    sgin,
    sgin_t,
    sgout,
    sgout_t,
    turned,
    lbcol,
    lscol,
    sbcol,
    sscol,
    mid,
    acc,
    raw_a,
    raw_b,
    sums,
    wsem,
    isem,
    usem,
    ysem,
    gsem,
    fs,
    fr,
    bs,
    br,
    sibs,
    rights,
    lefts,
    outsem,
    vsem,
    ready,
    lent,
    tl,
    ts,
    vecs,
    paired,
    pairs,
):
    sections, n, ps, pl_, pp, d, ds_, dc, dp, fused, shared = dims
    place = lax.axis_index("section")
    ahead = lax.rem(place + 1, sections)
    behind = lax.rem(place + sections - 1, sections)
    last = place // (sections - 1)
    first_rows = n * pl_
    half = pl_ // 2
    line = dp // 2 if fused else 1
    rank = lax.axis_index("dp")
    z = rank // 2
    core = rank % 2
    sibling = rank + 1 - 2 * core
    partner = (place + sections // 2) % sections
    giver = place < sections // 2
    taker = place > 0
    owner = (place + sections - 1) // 2 % 2
    foreign = 1 + last

    def weight_copies():
        pairs = (
            (large_in, lgin),
            (large_out, lgout_t),
            (small_in, raw_a.at[0, :, pl.ds(0, ds_)]),
            (small_out, raw_a.at[0, :, pl.ds(ds_, ds_)]),
            (channel_in, win),
            (channel_out, wout),
        )
        return [pltpu.make_async_copy(a, b, wsem.at[k]) for k, (a, b) in enumerate(pairs)]

    def large_copy(src, dst, sem, i):
        return pltpu.make_async_copy(src.at[i], dst.at[pl.ds(pl.multiple_of(i * pl_, 64), pl_)], sem.at[i])

    def small_copy(src, dst, sem, j):
        return pltpu.make_async_copy(src.at[j], dst.at[j], sem.at[n + j])

    copies = weight_copies()

    @pl.when(place == 0)
    def _():
        for i in range(n):
            large_copy(large_images, xin, isem, i).start()

    for c in copies:
        c.start()

    @pl.when(last == 1)
    def _():
        for i in range(n):
            large_copy(large_upstream, up, usem, i).start()
        if fused:
            pltpu.make_async_copy(small_upstream, paired, usem.at[n]).start()
        else:
            for j in range(n):
                small_copy(small_upstream, raw_b, usem, j).start()

    barrier = pltpu.get_barrier_semaphore()

    @pl.when(place > 0)
    def _():
        pl.semaphore_signal(barrier, inc=1, device_id={"section": behind}, device_id_type=MESH)

    @pl.when(place < sections - 1)
    def _():
        pl.semaphore_signal(barrier, inc=1, device_id={"section": ahead}, device_id_type=MESH)

    peers = (place + sections - 2) // (sections - 1) + 1 - last
    if fused:
        pl.semaphore_signal(barrier, inc=1, device_id={"dp": sibling}, device_id_type=MESH)
        for k in range(1, line):
            pl.semaphore_signal(barrier, inc=1, device_id={"dp": (rank + 2 * k) % dp}, device_id_type=MESH)
        pl.semaphore_signal(barrier, inc=1, device_id={"section": partner}, device_id_type=MESH)
        peers = peers + line + 1

    def column(row, dst):
        width = up_to(dst.shape[0], 128)
        sums[0:1, 0:width] = jnp.zeros((1, width), F32)
        sums[0:1, 0 : row.shape[1]] = row
        dst[...] = jnp.transpose(jnp.broadcast_to(sums[0:1, 0:width], (128, width)))[0 : dst.shape[0]]

    column(large_bias[...], lbcol)
    column(large_shift[...], lscol)
    column(small_bias[...], sbcol)
    column(small_shift[...], sscol)
    sums[...] = jnp.zeros(sums.shape, F32)
    for c in copies[:4]:
        c.wait()
    for k, padded in enumerate((sgin, sgout_t)):
        padded[...] = jnp.zeros(padded.shape, BF16)
        padded[0:ps, :] = raw_a[0, :, k * ds_ : (k + 1) * ds_]

    @pl.when(place == 0)
    def _():
        for j in range(n):
            small_copy(small_images, raw_a, isem, j).start()

    lgin_t[...] = jnp.transpose(lgin[...])
    sgin_t[...] = jnp.transpose(sgin[...])

    def prepare_backward():
        lgout[...] = jnp.transpose(lgout_t[...])
        sgout[...] = jnp.transpose(sgout_t[...])

    @pl.when(last == 1)
    def _():
        prepare_backward()
        if fused:
            pltpu.make_async_copy(small_upstream, paired, usem.at[n]).wait()
            for j in range(n):
                base = first_rows + j * pp
                up[base : base + pp] = jnp.zeros((pp, d), BF16)
                for r in range(0, ps, 32):
                    size = min(32, ps - r)
                    up[base + r : base + r + size] = paired[r : r + size].astype(F32)[:, j, :].astype(BF16)


    gains = norm_gain[...]
    shifts = norm_shift[...]

    def ahead_copy(rows, size, k):
        return pltpu.make_async_remote_copy(
            src_ref=stage.at[pl.ds(rows, size)],
            dst_ref=xin.at[pl.ds(rows, size)],
            send_sem=fs.at[k],
            recv_sem=fr.at[k],
            device_id={"section": ahead},
            device_id_type=MESH,
        )

    def behind_copy(rows, size, k):
        return pltpu.make_async_remote_copy(
            src_ref=stage.at[pl.ds(rows, size)],
            dst_ref=up.at[pl.ds(rows, size)],
            send_sem=bs.at[k],
            recv_sem=br.at[k],
            device_id={"section": behind},
            device_id_type=MESH,
        )

    class Unit:
        def __init__(self, large, i):
            self.large = large
            self.i = i
            self.rows = pl_ if large else pp
            self.blocks = 2 if large else 1
            self.size = self.rows // self.blocks
            self.some = ROWS if large else pp
            self.base = pl.multiple_of(i * pl_, 64) if large else pl.multiple_of(first_rows + i * pp, 16)
            self.head = pl.multiple_of((i if large else n + i) * ds_, 128)
            self.heads = pl.ds(self.head, ds_)
            self.slot = i * 2 if large else 2 * n + i
            self.gin, self.gin_t = (lgin, lgin_t) if large else (sgin, sgin_t)
            self.gout, self.gout_t = (lgout, lgout_t) if large else (sgout, sgout_t)
            self.bcol, self.scol = (lbcol, lscol) if large else (sbcol, sscol)
            self.mask = large_keep if large else small_keep

        def at(self, offset, size):
            return pl.ds(pl.multiple_of(self.base + offset, 16), size)

        def keep(self, which):
            return self.mask[self.i, which].astype(F32)

        def out_copy(self, which, b):
            sem = (ysem, gsem)[which].at[self.slot + b]
            if self.large:
                dst = (large_made, large_back)[which]
                return pltpu.make_async_copy(
                    stage.at[self.at(b * half, half)], dst.at[self.i, pl.ds(b * half, half)], sem
                )
            src = (raw_a, raw_b)[which]
            dst = (small_made, small_back)[which]
            return pltpu.make_async_copy(src.at[self.i], dst.at[self.i], sem)

    units = 2 * n

    def unit_at(which):
        return (which + core) % 2, which // 2

    def forward(unit, step):
        @pl.when(place == 0)
        def _():
            if unit.large:
                large_copy(large_images, xin, isem, unit.i).wait()
            else:
                small_copy(small_images, raw_a, isem, unit.i).wait()
                xin[unit.at(0, pp)] = jnp.zeros((pp, d), BF16)
                xin[unit.at(0, ps)] = raw_a[unit.i]

        def norm_one(r):
            rows = unit.at(r * unit.some, unit.some)
            x = xin[rows].astype(F32)
            x = x - jnp.mean(x, axis=1, keepdims=True)
            s = lax.rsqrt(jnp.mean(x * x, axis=1, keepdims=True) + EPSILON)
            n1[rows] = (x * s * gains[0:1] + shifts[0:1]).astype(BF16)

        steps = unit.size // unit.some
        for b in range(unit.blocks):

            @pl.when(place > 0)
            def _(b=b):
                ahead_copy(unit.base + b * unit.size, unit.size, unit.slot + b).wait_recv()

            for r in range(b * steps, (b + 1) * steps):
                norm_one(r)
        rows = unit.at(0, unit.rows)
        keep_one = unit.keep(0)
        keep_two = unit.keep(1)
        for c in range(0, d, COLS):
            pre = mm(unit.gin_t[...], n1[rows, c : c + COLS], 1, 0) + unit.bcol[:, 0:1]
            act, slp = gelu_pair(pre)
            h1[unit.heads, c : c + COLS] = act.astype(BF16)
            sl1[unit.heads, c : c + COLS] = slp.astype(BF16)
        for c in range(0, d, COLS):
            branch = mm(unit.gout_t[...], h1[unit.heads, c : c + COLS], 1, 0) + unit.scol[:, 0:1]
            mid[0 : unit.rows, c : c + COLS] = xin[rows, c : c + COLS].astype(F32) + keep_one * branch

        def norm_two(r):
            rows = unit.at(r * unit.some, unit.some)
            x = mid[r * unit.some : (r + 1) * unit.some]
            x = x - jnp.mean(x, axis=1, keepdims=True)
            s = lax.rsqrt(jnp.mean(x * x, axis=1, keepdims=True) + EPSILON)
            x = x * s
            u2[rows] = x.astype(BF16)
            r2[rows] = jnp.broadcast_to(s, (unit.some, 128))
            n2[rows] = (x * gains[1:2] + shifts[1:2]).astype(BF16)

        for r in range(unit.rows // unit.some):
            norm_two(r)

        @pl.when(step == 0)
        def _():
            for c in copies[4:]:
                c.wait()

        for b in range(unit.blocks):
            size = unit.size
            rows = unit.at(b * size, size)
            here = slice(b * size, (b + 1) * size)
            total = channel_shift[...]
            parts = [slice(c, c + COLS) for c in range(0, dc, COLS)]
            ahead_of = mm(n2[rows], win[:, parts[0]], 1, 0)
            acts = []
            for c, cols in enumerate(parts):
                pre = ahead_of + channel_bias[:, cols]
                if c + 1 < len(parts):
                    ahead_of = mm(n2[rows], win[:, parts[c + 1]], 1, 0)
                act, slp = gelu_pair(pre)
                acts.append(act.astype(BF16))
                hid[rows, cols] = acts[-1]
                slope[rows, cols] = slp.astype(BF16)
                if cols.stop % WIDE == 0:
                    total = total + mm(jnp.concatenate(acts, axis=1), wout[cols.stop - WIDE : cols.stop, :], 1, 0)
                    acts = []
            y = (mid[here] + keep_two * total).astype(BF16)
            stage[rows] = y
            if not unit.large:
                raw_a[unit.i] = y[0:ps]

            if b == 0:

                @pl.when(step == 0)
                def _():
                    pl.semaphore_wait(barrier, peers)

            @pl.when(place < sections - 1)
            def _(b=b, size=size):
                ahead_copy(unit.base + b * size, size, unit.slot + b).start()

            if unit.large or not fused:
                unit.out_copy(0, b).start()

    def backward(unit):
        @pl.when(last == 1)
        def _():
            if unit.large:
                large_copy(large_upstream, up, usem, unit.i).wait()
            elif not fused:
                small_copy(small_upstream, raw_b, usem, unit.i).wait()
                up[unit.at(0, pp)] = jnp.zeros((pp, d), BF16)
                up[unit.at(0, ps)] = raw_b[unit.i]

        keep_one = unit.keep(0)
        keep_two = unit.keep(1)
        size = unit.size
        for b in range(unit.blocks):
            rows = unit.at(b * size, size)
            here = slice(b * size, (b + 1) * size)

            @pl.when(place < sections - 1)
            def _(b=b):
                ahead_copy(unit.base + b * size, size, unit.slot + b).wait_send()

            if unit.large or not fused:
                unit.out_copy(0, b).wait()

            @pl.when(last == 0)
            def _(b=b):
                behind_copy(unit.base + b * size, size, unit.slot + b).wait_recv()

            stage[rows] = up[rows] * keep_two.astype(BF16)

            parts = [slice(c, c + COLS) for c in range(0, dc, COLS)]
            total = None
            ahead_of = mm(stage[rows], wout[parts[0], :], 1, 1)
            grads = []
            for c, cols in enumerate(parts):
                grad = ahead_of
                if c + 1 < len(parts):
                    ahead_of = mm(stage[rows], wout[parts[c + 1], :], 1, 1)
                grads.append((grad * slope[rows, cols].astype(F32)).astype(BF16))
                slope[rows, cols] = grads[-1]
                if cols.stop % WIDE == 0:
                    term = mm(jnp.concatenate(grads, axis=1), win[:, cols.stop - WIDE : cols.stop], 1, 1)
                    total = term if total is None else total + term
                    grads = []
            acc[here] = total

        def norm_two(r):
            offset = r * unit.some
            rows = unit.at(offset, unit.some)
            local = slice(offset, offset + unit.some)
            h = acc[local]
            u = u2[rows].astype(F32)
            s = r2[rows][:, 0:1]
            g = up[rows].astype(F32)
            q = h * gains[1:2]
            first = jnp.mean(q, axis=1, keepdims=True)
            second = jnp.mean(q * u, axis=1, keepdims=True)
            g_mid = g + s * (q - first - u * second)
            mid[local] = g_mid
            gb1[rows] = (keep_one * g_mid).astype(BF16)
            up[rows] = (keep_two * g).astype(BF16)
            return groups(h * u), groups(h)

        parts = [norm_two(r) for r in range(unit.rows // unit.some)]
        sums[8:16, 0:d] += sum(p[0] for p in parts)
        sums[24:32, 0:d] += sum(p[1] for p in parts)
        rows = unit.at(0, unit.rows)
        for c in range(0, d, COLS):
            grad = mm(unit.gout[...], gb1[rows, c : c + COLS], 1, 0)
            grad = (grad * sl1[unit.heads, c : c + COLS].astype(F32)).astype(BF16)
            sl1[unit.heads, c : c + COLS] = grad
        for c in range(0, d, COLS):
            acc[0 : unit.rows, c : c + COLS] = mm(unit.gin[...], sl1[unit.heads, c : c + COLS], 1, 0)

        def norm_one(r):
            offset = r * unit.some
            rows = unit.at(offset, unit.some)
            local = slice(offset, offset + unit.some)
            x = xin[rows].astype(F32)
            x = x - jnp.mean(x, axis=1, keepdims=True)
            s = lax.rsqrt(jnp.mean(x * x, axis=1, keepdims=True) + EPSILON)
            u = x * s
            h = acc[local]
            q = h * gains[0:1]
            first = jnp.mean(q, axis=1, keepdims=True)
            second = jnp.mean(q * u, axis=1, keepdims=True)
            stage[rows] = (mid[local] + s * (q - first - u * second)).astype(BF16)
            return groups(h * u), groups(h)

        steps = size // unit.some
        for b in range(unit.blocks):
            parts = [norm_one(r) for r in range(b * steps, (b + 1) * steps)]
            sums[0:8, 0:d] += sum(p[0] for p in parts)
            sums[16:24, 0:d] += sum(p[1] for p in parts)
            if not unit.large:
                raw_b[unit.i] = stage[unit.at(0, ps)]

            @pl.when(place > 0)
            def _(b=b):
                behind_copy(unit.base + b * size, size, unit.slot + b).start()

            if unit.large or not fused:
                unit.out_copy(1, b).start()

    piece = d // dp
    tok_piece = ds_ // dp

    def turn(src):
        def some(rows, size):
            value = jnp.transpose(src[pl.ds(rows, size)])
            if not fused:
                turned[:, pl.ds(rows, size)] = value
                return
            for b in range(dp):
                at = ((b % 2) * line + b // 2) * piece
                turned[at : at + piece, pl.ds(rows, size)] = value[b * piece : (b + 1) * piece]

        def full(r, carry):
            some(pl.multiple_of(r * 128, 128), 128)
            return carry

        whole = src.shape[0] // 128
        lax.fori_loop(0, whole, full, 0)
        if src.shape[0] % 128:
            some(whole * 128, src.shape[0] % 128)


    def step(t, carry):
        back = (1 - last) * (t // units) + last * (t % 2)
        which = (1 - last) * (t % units) + last * (t // 2)
        small, i = unit_at(which)

        @pl.when((t == units) & (last == 0))
        def _():
            prepare_backward()

        @pl.when(t == 2 * units - 1)
        def _():
            turn(n2)

        @pl.when((back == 0) & (small == 0))
        def _():
            forward(Unit(True, i), t)

        @pl.when((back == 0) & (small == 1))
        def _():
            forward(Unit(False, i), t)

        @pl.when((back == 1) & (small == 0))
        def _():
            backward(Unit(True, i))

        @pl.when((back == 1) & (small == 1))
        def _():
            backward(Unit(False, i))

        return carry

    lax.fori_loop(0, 2 * units, step, 0)

    total = hid.shape[0]
    chunks = dc // d
    count = 2 * chunks + 2
    kinds = (chunks, chunks, 1, 1, shared)
    first_of = (0, chunks + 2, chunks, chunks + 1, count + 1)
    large_width, small_width = up_to(pl_, 128), up_to(pp, 128)
    widths = (d, d, large_width, small_width, d)
    own = line
    across = line + 1

    def columns(kind, k):
        if kind < 2:
            return pl.ds(pl.multiple_of(k * d, 128), d)
        return pl.ds(0, widths[kind])

    def own_rows(kind):
        return ((slope, 0), (hid, 0), (up, 0), (up, d))[kind]

    def weight_product(kind, k):
        src = (slope, hid)[kind]

        def part(j, carry):
            cols = pl.ds(pl.multiple_of(k * d + j * COLS, COLS), COLS)
            if kind == 0:
                bias = mm(jnp.ones((8, total), BF16), src[:, cols], 1, 0)[0:1]
                vecs[own, pl.ds(k, 1), pl.ds(pl.multiple_of(j * COLS, COLS), COLS)] = bias
            src[0:d, cols] = mm(turned[...], src[:, cols], 1, 0).astype(BF16)
            return carry

        lax.fori_loop(0, d // COLS, part, 0)

    def token_product(large):
        unit_rows = pl_ if large else pp
        ones_d = jnp.ones((8, d), BF16)
        out_grad = in_grad = bias = shift = None
        for k in range(n):
            base = k * pl_ if large else first_rows + k * pp
            head = k * ds_ if large else (n + k) * ds_
            g = gb1[base : base + unit_rows]
            x = n1[base : base + unit_rows]
            h = h1[head : head + ds_]
            p = sl1[head : head + ds_]
            terms = (mm(p, x, 1, 1), mm(h, g, 1, 1), mm(ones_d, p, 1, 1), mm(ones_d, g, 1, 1))
            if k == 0:
                in_grad, out_grad, bias, shift = terms
            else:
                in_grad, out_grad, bias, shift = in_grad + terms[0], out_grad + terms[1], bias + terms[2], shift + terms[3]
        src, base = own_rows(2 if large else 3)
        for at, value in ((0, in_grad), (1, out_grad)):
            value = value.astype(BF16)
            if not fused:
                src[base + at * ds_ : base + (at + 1) * ds_, 0:unit_rows] = value
                continue
            for b in range(dp):
                to = base + ((b % 2) * line + b // 2) * piece + at * tok_piece
                src[to : to + tok_piece, 0:unit_rows] = value[b * tok_piece : (b + 1) * tok_piece]
        row = chunks + 5 + (0 if large else 2)
        vecs[own, row : row + 1, 0:ds_] = bias[0:1]
        vecs[own, row + 1 : row + 2, 0:unit_rows] = shift[0:1]

    def product(kind, k):
        if kind == 2:
            turn(up)
            vecs[own, chunks : chunks + 1] = mm(jnp.ones((8, total), BF16), up[...], 1, 0)[0:1]
            for j in range(4):
                vecs[own, chunks + 1 + j : chunks + 2 + j] = jnp.sum(sums[8 * j : 8 * j + 8], axis=0, keepdims=True)
        if kind < 2:
            weight_product(kind, k)
        else:
            token_product(kind == 2)

    def ways(step_of, kept=False):
        def at(c, valid=True):
            for kind in range(5 if fused else 4):
                low, high = first_of[kind], first_of[kind] + kinds[kind]
                here = (c >= low) & (c < high) & valid
                if kind == 4:
                    here = here & taker & (c < low + foreign)
                if kind == 0 and kept:
                    here = here & ((place >= sections // 2) | (c < 1) | (c > shared))

                @pl.when(here)
                def _(kind=kind, low=low):
                    step_of(kind, c - low)

        return at

    vecs[own] = jnp.zeros(vecs.shape[1:], F32)
    if not fused:

        def whole_copies(kind, k):
            src, base = own_rows(kind)
            if kind < 2:
                cols = columns(kind, k)
                dst = (chan_a, chan_b)[kind]
                return [pltpu.make_async_copy(src.at[pl.ds(0, d), cols], dst.at[:, cols], outsem.at[first_of[kind] + k])]
            cols = pl.ds(0, widths[kind])
            dst = (tok_l, tok_s)[kind - 2]
            return [pltpu.make_async_copy(src.at[pl.ds(base, d), cols], dst, outsem.at[first_of[kind]])]

        def one(kind, k):
            product(kind, k)
            for c in whole_copies(kind, k):
                c.start()

        def finish(kind, k):
            for c in whole_copies(kind, k):
                c.wait()

        def run(c, carry):
            ways(one)(c)
            return carry

        def end(c, carry):
            ways(finish)(c)
            return carry

        lax.fori_loop(0, count, run, 0)
        lax.fori_loop(0, count, end, 0)
        vec_out[...] = vecs[own]
    else:
        rightward, leftward = (rank + 2) % dp, (rank + dp - 2) % dp

        def mine(kind, k, to):
            if kind == 4:
                return h1.at[pl.ds(pl.multiple_of((k * line + to) * piece, 16), piece)]
            src, base = own_rows(kind)
            return src.at[pl.ds(pl.multiple_of(base + (core * line + to) * piece, 16), piece), columns(kind, k)]

        def crossing(kind, k, rows, size):
            ref, base = ((win, 0), (win, d // 2), (wout, 3 * d), (wout, 3 * d + d // 2))[kind]
            return ref.at[pl.ds(pl.multiple_of(base + rows, 16), size), columns(kind, k)]

        def from_left(kind, k, to):
            ref, base = ((wout, 0), (wout, chunks * (line - 1)), (n2, 0), (n2, line - 1), (sl1, 0))[kind]
            rows = (base + k * (line - 1) + to - 1) * piece
            return ref.at[pl.ds(pl.multiple_of(rows, 16), piece), pl.ds(0, widths[kind])]

        def from_right(kind, k, to):
            ref, base = ((xin, 0), (u2, 0), (n2, 2 * (line - 1)), (n2, 3 * (line - 1)), (sl1, shared * (line - 1)))[kind]
            rows = (base + k * (line - 1) + to) * piece
            return ref.at[pl.ds(pl.multiple_of(rows, 16), piece), pl.ds(0, widths[kind])]

        def sem_of(kind, k, to):
            return ((count if kind == 4 else first_of[kind]) + k) * line + to

        def cross_copy(kind, k):
            src, base = own_rows(kind)
            rows = pl.ds(pl.multiple_of(base + (1 - core) * line * piece, 16), line * piece)
            c = first_of[kind] + k
            return pltpu.make_async_remote_copy(
                src_ref=src.at[rows, columns(kind, k)],
                dst_ref=crossing(kind, k, 0, line * piece),
                send_sem=sibs.at[0, c],
                recv_sem=sibs.at[1, c],
                device_id={"dp": sibling},
                device_id_type=MESH,
            )

        def right_copy(kind, k, to):
            return pltpu.make_async_remote_copy(
                src_ref=mine(kind, k, to),
                dst_ref=from_left(kind, k, to),
                send_sem=rights.at[0, sem_of(kind, k, to)],
                recv_sem=rights.at[1, sem_of(kind, k, to)],
                device_id={"dp": rightward},
                device_id_type=MESH,
            )

        def left_copy(kind, k, to):
            return pltpu.make_async_remote_copy(
                src_ref=mine(kind, k, to),
                dst_ref=from_right(kind, k, to),
                send_sem=lefts.at[0, sem_of(kind, k, to)],
                recv_sem=lefts.at[1, sem_of(kind, k, to)],
                device_id={"dp": leftward},
                device_id_type=MESH,
            )

        def chip_sum(kind, k, to):
            if kind == 4:
                return mine(kind, k, to)[...].astype(F32)
            return mine(kind, k, to)[...].astype(F32) + crossing(kind, k, to * piece, piece)[...].astype(F32)

        def flow_right(kind, k):
            def one(j, carry):
                to = line - 1 - j

                @pl.when(z == 0)
                def _():
                    mine(kind, k, to)[...] = chip_sum(kind, k, to).astype(BF16)

                @pl.when(z > 0)
                def _():
                    right_copy(kind, k, to).wait_recv()
                    value = chip_sum(kind, k, to) + from_left(kind, k, to)[...].astype(F32)
                    mine(kind, k, to)[...] = value.astype(BF16)

                right_copy(kind, k, to).start()
                return carry

            lax.fori_loop(0, line - 1 - z, one, 0)

        def flow_left(kind, k):
            def one(to, carry):
                @pl.when(z == line - 1)
                def _():
                    mine(kind, k, to)[...] = chip_sum(kind, k, to).astype(BF16)

                @pl.when(z < line - 1)
                def _():
                    left_copy(kind, k, to).wait_recv()
                    value = chip_sum(kind, k, to) + from_right(kind, k, to)[...].astype(F32)
                    mine(kind, k, to)[...] = value.astype(BF16)

                left_copy(kind, k, to).start()
                return carry

            lax.fori_loop(0, z, one, 0)

        def out_stage(kind, k):
            if kind == 0:
                return mid.at[pl.ds(pl.multiple_of(k * piece, 16), piece)]
            if kind in (1, 4):
                at = k + (chunks if kind == 4 else 0)
                return acc.at[pl.ds(pl.multiple_of(at * piece, 16), piece)]
            return (tl, ts)[kind - 2]

        def out_copies(kind, k):
            c = first_of[kind] + k
            if kind < 2:
                dst = (chan_a, chan_b)[kind].at[:, columns(kind, k)]
            else:
                dst = (tok_l, tok_s)[kind - 2]
            return pltpu.make_async_copy(out_stage(kind, k), dst, outsem.at[c])

        def gather(kind, k):
            width = (d, d, pl_, ps, d)[kind]
            dst = out_stage(kind, k)
            dst[...] = chip_sum(kind, k, z)[:, 0:width]

            @pl.when(z > 0)
            def _():
                right_copy(kind, k, z).wait_recv()
                dst[...] += from_left(kind, k, z)[...].astype(F32)[:, 0:width]

            @pl.when(z < line - 1)
            def _():
                left_copy(kind, k, z).wait_recv()
                dst[...] += from_right(kind, k, z)[...].astype(F32)[:, 0:width]

            if kind == 4:
                give_back(k).start()
            else:
                out_copies(kind, k).start()

        def lend_copy(j, f, to):
            rows = pl.ds(pl.multiple_of(core * line * piece, 16), line * piece)
            return pltpu.make_async_remote_copy(
                src_ref=slope.at[rows, columns(0, j + 1)],
                dst_ref=h1.at[pl.ds(pl.multiple_of(f * line * piece, 16), line * piece)],
                send_sem=lent.at[0, j],
                recv_sem=lent.at[1, f],
                device_id={"section": to},
                device_id_type=MESH,
            )

        def return_copy(f, j, to):
            return pltpu.make_async_remote_copy(
                src_ref=out_stage(4, f),
                dst_ref=out_stage(0, j + 1),
                send_sem=lent.at[2, f],
                recv_sem=lent.at[3, j],
                device_id={"section": to},
                device_id_type=MESH,
            )

        def lend_away(j):
            return lend_copy(j, place * j, (1 - place) * (2 - j) + place * 3)

        def give_back(f):
            return return_copy(f, f + (2 - place) * (1 - last), owner)

        def lend(c):
            @pl.when(giver & (c >= 1) & (c <= shared))
            def _():
                @pl.when(c == 1)
                def _():
                    pl.semaphore_wait(ready.at[3], 1)

                @pl.when((c == 2) & (place == 0))
                def _():
                    pl.semaphore_wait(ready.at[6], 1)

                def one(to, carry):
                    mine(0, c, to)[...] = chip_sum(0, c, to).astype(BF16)
                    return carry

                lax.fori_loop(0, line, one, 0)
                lend_away(c - 1).start()

        def pair_copy(which):
            return pltpu.make_async_copy(paired, (small_made, small_back)[which], pairs.at[which])

        def pair(which):
            if which:
                pair_copy(0).wait()
            src = (raw_a, raw_b)[which]
            for r in range(0, ps, 32):
                rows = slice(r, min(r + 32, ps))
                images = [src[j, rows].astype(F32)[:, None, :] for j in range(n)]
                paired[rows] = jnp.concatenate(images, axis=1).astype(BF16)
            pair_copy(which).start()

        def vec_cross():
            return pltpu.make_async_remote_copy(
                src_ref=vecs.at[own],
                dst_ref=vecs.at[across],
                send_sem=vsem.at[0, 0],
                recv_sem=vsem.at[1, 0],
                device_id={"dp": sibling},
                device_id_type=MESH,
            )

        def vec_copy(k):
            return pltpu.make_async_remote_copy(
                src_ref=vecs.at[z],
                dst_ref=vecs.at[z],
                send_sem=vsem.at[0, k],
                recv_sem=vsem.at[1, k],
                device_id={"dp": (rank + 2 * k) % dp},
                device_id_type=MESH,
            )

        def first(kind, k):
            if kind == 4:

                @pl.when(k == 0)
                def _():
                    @pl.when(z < line - 1)
                    def _():
                        pl.semaphore_wait(ready.at[4], 1)

                    @pl.when(z > 0)
                    def _():
                        pl.semaphore_wait(ready.at[5], 1)

                lend_copy(0, k, owner).wait_recv()
                return
            product(kind, k)
            if kind == 3:

                @pl.when(taker)
                def _():
                    for at, here in ((6, place == 1), (3, place > 1)):

                        @pl.when(here)
                        def _(at=at):
                            pl.semaphore_signal(ready.at[at], inc=1, device_id={"section": owner}, device_id_type=MESH)

                    @pl.when(z > 0)
                    def _():
                        pl.semaphore_signal(ready.at[4], inc=1, device_id={"dp": leftward}, device_id_type=MESH)

                    @pl.when(z < line - 1)
                    def _():
                        pl.semaphore_signal(ready.at[5], inc=1, device_id={"dp": rightward}, device_id_type=MESH)

            if kind == 0:

                @pl.when(k == 0)
                def _():
                    pl.semaphore_wait(ready.at[0], 1)

                    @pl.when(z < line - 1)
                    def _():
                        pl.semaphore_wait(ready.at[1], 1)

                    @pl.when(z > 0)
                    def _():
                        pl.semaphore_wait(ready.at[2], 1)

            cross_copy(kind, k).start()

        def crossed(kind, k):
            if kind < 4:
                cross_copy(kind, k).wait_recv()

        def finish(kind, k):
            if kind == 4:
                give_back(k).wait_send()
            else:
                cross_copy(kind, k).wait_send()
                out_copies(kind, k).wait()

            def right(j, carry):
                right_copy(kind, k, line - 1 - j).wait_send()
                return carry

            def left(to, carry):
                left_copy(kind, k, to).wait_send()
                return carry

            sent = line - 1 - z, z
            if kind == 0:
                away = giver & (k >= 1) & (k <= shared)
                own_line = 1 - away.astype(jnp.int32)
                sent = sent[0] * own_line, sent[1] * own_line
            lax.fori_loop(0, sent[0], right, 0)
            lax.fori_loop(0, sent[1], left, 0)

        pl.semaphore_signal(ready.at[0], inc=1, device_id={"dp": sibling}, device_id_type=MESH)

        @pl.when(z > 0)
        def _():
            pl.semaphore_signal(ready.at[1], inc=1, device_id={"dp": leftward}, device_id_type=MESH)

        @pl.when(z < line - 1)
        def _():
            pl.semaphore_signal(ready.at[2], inc=1, device_id={"dp": rightward}, device_id_type=MESH)

        def run(c, carry):
            ways(crossed)(c - 1)
            lend(c - 1)
            ways(flow_right, True)(c - 1 - z, z < line - 1)
            ways(flow_left, True)(c - line + z, z > 0)
            ways(first)(c)

            @pl.when(c == count)
            def _():
                vec_cross().start()

            @pl.when(c == count + 1)
            def _():
                vec_cross().wait()
                vecs[z] = vecs[own] + vecs[across]
                for k in range(1, line):
                    vec_copy(k).start()

            for which in range(2):

                @pl.when(c == count - 2 + which)
                def _(which=which):
                    pair(which)

            ways(gather, True)(c - line - 1)
            return carry

        steps = count + 1 + shared
        lax.fori_loop(0, steps + line + 1, run, 0)

        @pl.when(giver)
        def _():
            for k in range(shared):
                lend_away(k).wait_send()
                return_copy(0, k, owner).wait_recv()
                out_copies(0, k + 1).start()

        def end(c, carry):
            ways(finish)(c)
            return carry

        lax.fori_loop(0, steps, end, 0)
        pair_copy(1).wait()
        for k in range(1, line):
            vec_copy(k).wait()
        value = vecs[0]
        for k in range(1, line):
            value = value + vecs[k]
        vec_out[...] = value

    for i in range(2 * n):
        unit = Unit(i < n, i % n)
        for b in range(unit.blocks):
            if unit.large or not fused:
                unit.out_copy(1, b).wait()

            @pl.when(place > 0)
            def _(b=b, unit=unit):
                behind_copy(unit.base + b * unit.size, unit.size, unit.slot + b).wait_send()


def finish_kernel(tok_piece, d, chunks, moved, *refs):
    sources, (tok_l, tok_s, vec), rest = refs[:moved], refs[moved : moved + 3], refs[moved + 3 :]
    outs, vias, sem = rest[: -moved - 1], rest[-moved - 1 : -1], rest[-1]
    bring = [pltpu.make_async_copy(a, b, sem.at[0, k]) for k, (a, b) in enumerate(zip(sources, vias))]
    take = [pltpu.make_async_copy(a, b, sem.at[1, k]) for k, (a, b) in enumerate(zip(vias, outs[:moved]))]
    for c in bring:
        c.start()
    outs = outs[moved:]
    for k, src in enumerate((tok_l, tok_s)):
        outs[2 * k][...] = src[0:tok_piece]
        outs[2 * k + 1][...] = src[tok_piece:]
    for k in range(chunks):
        outs[4][:, k * d : (k + 1) * d] = vec[k : k + 1]
    at = chunks
    for out in outs[5:]:
        rows, width = out.shape
        out[...] = vec[at : at + rows, 0:width]
        at += rows
    for a, b in zip(bring, take):
        a.wait()
        b.start()
    for c in take:
        c.wait()


def local(
    small_images,
    large_images,
    small_upstream,
    large_upstream,
    small_keep,
    large_keep,
    small_in,
    small_bias,
    small_out,
    small_shift,
    large_in,
    large_bias,
    large_out,
    large_shift,
    channel_in,
    channel_bias,
    channel_out,
    channel_shift,
    norm_gain,
    norm_shift,
):
    sections = lax.axis_size("section")
    micro, imgs, ps, d = small_images.shape
    pl_ = large_images.shape[2]
    n = micro * imgs
    ds_ = small_in.shape[2]
    dc = channel_in.shape[2]
    pp = up_to(ps, 16)
    rows = n * (pl_ + pp)
    small_width, large_width = up_to(pp, 128), up_to(pl_, 128)
    dp = lax.axis_size("dp")
    piece, tok_piece = d // dp, ds_ // dp
    fused = d % (16 * dp) == 0 and ds_ % (16 * dp) == 0 and dc == 4 * d and d == 2 * ds_ and 2 * dp * piece <= rows
    fused = fused and sections == 4
    shared = 2
    dims = (sections, n, ps, pl_, pp, d, ds_, dc, dp, fused, shared)
    chunks = dc // d
    line = dp // 2 if fused else 1
    count = 2 * chunks + 2
    vec_rows = up_to(chunks + 9, 8)
    any_ = pl.BlockSpec(memory_space=pl.ANY)
    vmem = pl.BlockSpec(memory_space=pltpu.VMEM)
    smem = pl.BlockSpec(memory_space=pltpu.SMEM)
    block = max(pl_, n * pp)
    blocks = 2 * n + n
    scratch = [
        pltpu.VMEM((d, dc), BF16),
        pltpu.VMEM((dc, d), BF16),
        pltpu.VMEM((rows, dc), BF16),
        pltpu.VMEM((rows, dc), BF16),
        pltpu.VMEM((rows, d), BF16),
        pltpu.VMEM((rows, d), BF16),
        pltpu.VMEM((rows, d), BF16),
        pltpu.VMEM((rows, d), BF16),
        pltpu.VMEM((rows, d), BF16),
        pltpu.VMEM((rows, 128), F32),
        pltpu.VMEM((rows, d), BF16),
        pltpu.VMEM((rows, d), BF16),
        pltpu.VMEM((2 * n * ds_, d), BF16),
        pltpu.VMEM((2 * n * ds_, d), BF16),
        pltpu.VMEM((pl_, ds_), BF16),
        pltpu.VMEM((ds_, pl_), BF16),
        pltpu.VMEM((ds_, pl_), BF16),
        pltpu.VMEM((pl_, ds_), BF16),
        pltpu.VMEM((pp, ds_), BF16),
        pltpu.VMEM((ds_, pp), BF16),
        pltpu.VMEM((ds_, pp), BF16),
        pltpu.VMEM((pp, ds_), BF16),
        pltpu.VMEM((d, rows), BF16),
        pltpu.VMEM((ds_, 128), F32),
        pltpu.VMEM((pl_, 128), F32),
        pltpu.VMEM((ds_, 128), F32),
        pltpu.VMEM((pp, 128), F32),
        pltpu.VMEM((block, d), F32),
        pltpu.VMEM((block, d), F32),
        pltpu.VMEM((n, ps, d), BF16),
        pltpu.VMEM((n, ps, d), BF16),
        pltpu.VMEM((32, d), F32),
        pltpu.SemaphoreType.DMA((6,)),
        pltpu.SemaphoreType.DMA((2 * n,)),
        pltpu.SemaphoreType.DMA((2 * n,)),
        pltpu.SemaphoreType.DMA((blocks,)),
        pltpu.SemaphoreType.DMA((blocks,)),
        pltpu.SemaphoreType.DMA((blocks,)),
        pltpu.SemaphoreType.DMA((blocks,)),
        pltpu.SemaphoreType.DMA((blocks,)),
        pltpu.SemaphoreType.DMA((blocks,)),
        pltpu.SemaphoreType.DMA((2, count)),
        pltpu.SemaphoreType.DMA((2, (count + shared) * line)),
        pltpu.SemaphoreType.DMA((2, (count + shared) * line)),
        pltpu.SemaphoreType.DMA((count,)),
        pltpu.SemaphoreType.DMA((2, line)),
        pltpu.SemaphoreType.REGULAR((7,)),
        pltpu.SemaphoreType.DMA((4, shared)),
        pltpu.VMEM((2 * tok_piece, pl_), F32),
        pltpu.VMEM((2 * tok_piece, ps), F32),
        pltpu.VMEM((line + 2, vec_rows, d), F32),
        pltpu.VMEM((ps, n, d) if fused else (8, 128), BF16),
        pltpu.SemaphoreType.DMA((2,)),
    ]
    if fused:
        reduced = (
            jax.ShapeDtypeStruct((piece, dc), F32),
            jax.ShapeDtypeStruct((piece, dc), F32),
            jax.ShapeDtypeStruct((2 * tok_piece, pl_), F32),
            jax.ShapeDtypeStruct((2 * tok_piece, ps), F32),
        )
    else:
        reduced = (
            jax.ShapeDtypeStruct((d, dc), BF16),
            jax.ShapeDtypeStruct((d, dc), BF16),
            jax.ShapeDtypeStruct((d, large_width), BF16),
            jax.ShapeDtypeStruct((d, small_width), BF16),
        )
    small_shape = (ps, n, d) if fused else (n, ps, d)
    outs = (
        jax.ShapeDtypeStruct(small_shape, BF16),
        jax.ShapeDtypeStruct((n, pl_, d), BF16),
        jax.ShapeDtypeStruct(small_shape, BF16),
        jax.ShapeDtypeStruct((n, pl_, d), BF16),
        *reduced,
        jax.ShapeDtypeStruct((vec_rows, d), F32),
    )
    made_s, made_l, back_s, back_l, chan_a, chan_b, tok_l, tok_s, vec = pl.pallas_call(
        functools.partial(kernel, dims),
        out_shape=outs,
        in_specs=[any_] * 4
        + [smem] * 2
        + [any_, vmem, any_, vmem] * 2
        + [any_, vmem, any_, vmem]
        + [vmem, vmem],
        out_specs=(any_,) * 8 + (vmem,),
        scratch_shapes=scratch,
        compiler_params=pltpu.CompilerParams(
            collective_id=0, has_side_effects=True, vmem_limit_bytes=65400 * 1024
        ),
        cost_estimate=pl.CostEstimate(flops=50 * 10**9, bytes_accessed=40 * 10**6, transcendentals=10**7),
    )(
        small_images.reshape(n, ps, d),
        large_images.reshape(n, pl_, d),
        small_upstream.reshape(n, ps, d).transpose(1, 0, 2) if fused else small_upstream.reshape(n, ps, d),
        large_upstream.reshape(n, pl_, d),
        small_keep.reshape(n, 2),
        large_keep.reshape(n, 2),
        small_in[0],
        small_bias,
        small_out[0].T,
        small_shift,
        large_in[0],
        large_bias,
        large_out[0].T,
        large_shift,
        channel_in[0],
        channel_bias,
        channel_out[0],
        channel_shift,
        norm_gain[0],
        norm_shift[0],
    )
    if fused:
        large = (made_l, back_l, chan_a, chan_b, made_s, back_s)
        final = [jax.ShapeDtypeStruct(x.shape, x.dtype) for x in large]
        final += [jax.ShapeDtypeStruct((tok_piece, width), F32) for width in (pl_, pl_, ps, ps)]
        final += [
            jax.ShapeDtypeStruct(shape, F32)
            for shape in ((1, dc), (1, d), (2, d), (2, d), (1, ds_), (1, pl_), (1, ds_), (1, ps))
        ]
        made_l, back_l, chan_a, chan_b, made_s, back_s, lin, lout, sin, sout, *vecs = pl.pallas_call(
            functools.partial(finish_kernel, tok_piece, d, chunks, len(large)),
            out_shape=final,
            in_specs=[any_] * len(large) + [vmem] * 3,
            out_specs=[any_] * len(large) + [vmem] * 12,
            scratch_shapes=[pltpu.VMEM(x.shape, x.dtype) for x in large] + [pltpu.SemaphoreType.DMA((2, len(large)))],
            compiler_params=pltpu.CompilerParams(vmem_limit_bytes=65400 * 1024),
        )(*large, tok_l, tok_s, vec)
        cbias, cshift, gain, shift, lbias, lshift, sbias, sshift = vecs
        made_s, back_s = (x.transpose(1, 0, 2) for x in (made_s, back_s))
    else:
        chan_a, chan_b = (lax.psum_scatter(x, "dp", scatter_dimension=0, tiled=True).astype(F32) for x in (chan_a, chan_b))
        tok = jnp.concatenate([tok_l, tok_s], axis=1).reshape(2, ds_, large_width + small_width)
        tok = lax.psum_scatter(tok, "dp", scatter_dimension=1, tiled=True).astype(F32)
        lin, lout, sin, sout = tok[0, :, 0:pl_], tok[1, :, 0:pl_], tok[0, :, large_width:], tok[1, :, large_width:]
        sin, sout = sin[:, 0:ps], sout[:, 0:ps]
        vec = lax.psum(vec, "dp")
        at = chunks
        cbias, cshift = vec[0:at].reshape(1, dc), vec[at : at + 1]
        gain, shift = vec[at + 1 : at + 3], vec[at + 3 : at + 5]
        lbias, lshift = vec[at + 5 : at + 6, 0:ds_], vec[at + 6 : at + 7, 0:pl_]
        sbias, sshift = vec[at + 7 : at + 8, 0:ds_], vec[at + 8 : at + 9, 0:ps]
    return (
        made_s.reshape(1, micro, imgs, ps, d),
        made_l.reshape(1, micro, imgs, pl_, d),
        back_s.reshape(1, micro, imgs, ps, d),
        back_l.reshape(1, micro, imgs, pl_, d),
        sin.T[None],
        sbias,
        sout[None],
        sshift,
        lin.T[None],
        lbias,
        lout[None],
        lshift,
        chan_a[None],
        cbias,
        chan_b.T[None],
        cshift,
        gain[None],
        shift[None],
    )


def solution(mesh):
    placed = (
        (P(None, "dp", None, None),) * 4
        + (P("section", None, "dp", None),) * 2
        + (P("section", None, None), P("section", None)) * 6
        + (P("section", None, None),) * 2
    )
    outs = (
        (P("section", None, "dp", None, None),) * 4
        + (P("section", None, "dp"), P("section", None), P("section", "dp", None), P("section", None)) * 2
        + (P("section", "dp", None), P("section", None), P("section", None, "dp"), P("section", None))
        + (P("section", None, None),) * 2
    )
    return jax.shard_map(local, mesh=mesh, in_specs=placed, out_specs=outs, check_vma=False)
```

```python
import functools

import jax
import jax.numpy as jnp
from jax import lax
from jax.experimental import pallas as pl
from jax.experimental.pallas import tpu as pltpu
from jax.sharding import PartitionSpec as P

MESH = pl.DeviceIdType.MESH
F32 = jnp.float32
BF16 = jnp.bfloat16
EPSILON = 1e-06
DENSITY = 0.3989422804014327
ROWS = 144
COLS = 256
WIDE = 1024


def up_to(value, step):
    return -(-value // step) * step


def mm(a, b, ca, cb):
    return lax.dot_general(a, b, (((ca,), (cb,)), ((), ())), preferred_element_type=F32)


def gelu_pair(v):
    cdf = 0.5 + 0.5 * lax.erf(v * 0.7071067811865476)
    bell = jnp.exp2((v * v) * (-0.5 * 1.4426950408889634))
    return v * cdf, cdf + (v * DENSITY) * bell


def groups(x):
    return x.reshape(x.shape[0] // 8, 8, x.shape[1]).sum(0)


def kernel(
    dims,
    small_images,
    large_images,
    small_upstream,
    large_upstream,
    small_keep,
    large_keep,
    small_in,
    small_bias,
    small_out,
    small_shift,
    large_in,
    large_bias,
    large_out,
    large_shift,
    channel_in,
    channel_bias,
    channel_out,
    channel_shift,
    norm_gain,
    norm_shift,
    small_made,
    large_made,
    small_back,
    large_back,
    chan_a,
    chan_b,
    tok_l,
    tok_s,
    vec_out,
    win,
    wout,
    hid,
    slope,
    xin,
    up,
    n1,
    n2,
    u2,
    r2,
    gb1,
    stage,
    h1,
    sl1,
    lgin,
    lgin_t,
    lgout,
    lgout_t,
    sgin,
    sgin_t,
    sgout,
    sgout_t,
    turned,
    lbcol,
    lscol,
    sbcol,
    sscol,
    mid,
    acc,
    raw_a,
    raw_b,
    sums,
    wsem,
    isem,
    usem,
    ysem,
    gsem,
    fs,
    fr,
    bs,
    br,
    sibs,
    rights,
    lefts,
    outsem,
    vsem,
    ready,
    lent,
    tl,
    ts,
    vecs,
    paired,
    pairs,
):
    sections, n, ps, pl_, pp, d, ds_, dc, dp, fused, shared = dims
    place = lax.axis_index("section")
    ahead = lax.rem(place + 1, sections)
    behind = lax.rem(place + sections - 1, sections)
    last = place // (sections - 1)
    first_rows = n * pl_
    half = pl_ // 2
    line = dp // 2 if fused else 1
    rank = lax.axis_index("dp")
    z = rank // 2
    core = rank % 2
    sibling = rank + 1 - 2 * core
    partner = (place + sections // 2) % sections
    giver = place < sections // 2
    taker = place > 0
    owner = (place + sections - 1) // 2 % 2
    foreign = 1 + last

    def weight_copies():
        pairs = (
            (large_in, lgin),
            (large_out, lgout_t),
            (small_in, raw_a.at[0, :, pl.ds(0, ds_)]),
            (small_out, raw_a.at[0, :, pl.ds(ds_, ds_)]),
            (channel_in, win),
            (channel_out, wout),
        )
        return [pltpu.make_async_copy(a, b, wsem.at[k]) for k, (a, b) in enumerate(pairs)]

    def large_copy(src, dst, sem, i):
        return pltpu.make_async_copy(src.at[i], dst.at[pl.ds(pl.multiple_of(i * pl_, 64), pl_)], sem.at[i])

    def small_copy(src, dst, sem, j):
        return pltpu.make_async_copy(src.at[j], dst.at[j], sem.at[n + j])

    copies = weight_copies()

    @pl.when(place == 0)
    def _():
        for i in range(n):
            large_copy(large_images, xin, isem, i).start()

    for c in copies:
        c.start()

    @pl.when(last == 1)
    def _():
        for i in range(n):
            large_copy(large_upstream, up, usem, i).start()
        if fused:
            pltpu.make_async_copy(small_upstream, paired, usem.at[n]).start()
        else:
            for j in range(n):
                small_copy(small_upstream, raw_b, usem, j).start()

    barrier = pltpu.get_barrier_semaphore()

    @pl.when(place > 0)
    def _():
        pl.semaphore_signal(barrier, inc=1, device_id={"section": behind}, device_id_type=MESH)

    @pl.when(place < sections - 1)
    def _():
        pl.semaphore_signal(barrier, inc=1, device_id={"section": ahead}, device_id_type=MESH)

    peers = (place + sections - 2) // (sections - 1) + 1 - last
    if fused:
        pl.semaphore_signal(barrier, inc=1, device_id={"dp": sibling}, device_id_type=MESH)
        for k in range(1, line):
            pl.semaphore_signal(barrier, inc=1, device_id={"dp": (rank + 2 * k) % dp}, device_id_type=MESH)
        pl.semaphore_signal(barrier, inc=1, device_id={"section": partner}, device_id_type=MESH)
        peers = peers + line + 1

    def column(row, dst):
        width = up_to(dst.shape[0], 128)
        sums[0:1, 0:width] = jnp.zeros((1, width), F32)
        sums[0:1, 0 : row.shape[1]] = row
        dst[...] = jnp.transpose(jnp.broadcast_to(sums[0:1, 0:width], (128, width)))[0 : dst.shape[0]]

    column(large_bias[...], lbcol)
    column(large_shift[...], lscol)
    column(small_bias[...], sbcol)
    column(small_shift[...], sscol)
    sums[...] = jnp.zeros(sums.shape, F32)
    for c in copies[:4]:
        c.wait()
    for k, padded in enumerate((sgin, sgout_t)):
        padded[...] = jnp.zeros(padded.shape, BF16)
        padded[0:ps, :] = raw_a[0, :, k * ds_ : (k + 1) * ds_]

    @pl.when(place == 0)
    def _():
        for j in range(n):
            small_copy(small_images, raw_a, isem, j).start()

    lgin_t[...] = jnp.transpose(lgin[...])
    sgin_t[...] = jnp.transpose(sgin[...])

    def prepare_backward():
        lgout[...] = jnp.transpose(lgout_t[...])
        sgout[...] = jnp.transpose(sgout_t[...])

    @pl.when(last == 1)
    def _():
        prepare_backward()
        if fused:
            pltpu.make_async_copy(small_upstream, paired, usem.at[n]).wait()
            for j in range(n):
                base = first_rows + j * pp
                up[base : base + pp] = jnp.zeros((pp, d), BF16)
                for r in range(0, ps, 32):
                    size = min(32, ps - r)
                    up[base + r : base + r + size] = paired[r : r + size].astype(F32)[:, j, :].astype(BF16)


    gains = norm_gain[...]
    shifts = norm_shift[...]

    def ahead_copy(rows, size, k):
        return pltpu.make_async_remote_copy(
            src_ref=stage.at[pl.ds(rows, size)],
            dst_ref=xin.at[pl.ds(rows, size)],
            send_sem=fs.at[k],
            recv_sem=fr.at[k],
            device_id={"section": ahead},
            device_id_type=MESH,
        )

    def behind_copy(rows, size, k):
        return pltpu.make_async_remote_copy(
            src_ref=stage.at[pl.ds(rows, size)],
            dst_ref=up.at[pl.ds(rows, size)],
            send_sem=bs.at[k],
            recv_sem=br.at[k],
            device_id={"section": behind},
            device_id_type=MESH,
        )

    class Unit:
        def __init__(self, large, i):
            self.large = large
            self.i = i
            self.rows = pl_ if large else pp
            self.blocks = 2 if large else 1
            self.size = self.rows // self.blocks
            self.some = ROWS if large else pp
            self.base = pl.multiple_of(i * pl_, 64) if large else pl.multiple_of(first_rows + i * pp, 16)
            self.head = pl.multiple_of((i if large else n + i) * ds_, 128)
            self.heads = pl.ds(self.head, ds_)
            self.slot = i * 2 if large else 2 * n + i
            self.gin, self.gin_t = (lgin, lgin_t) if large else (sgin, sgin_t)
            self.gout, self.gout_t = (lgout, lgout_t) if large else (sgout, sgout_t)
            self.bcol, self.scol = (lbcol, lscol) if large else (sbcol, sscol)
            self.mask = large_keep if large else small_keep

        def at(self, offset, size):
            return pl.ds(pl.multiple_of(self.base + offset, 16), size)

        def keep(self, which):
            return self.mask[self.i, which].astype(F32)

        def out_copy(self, which, b):
            sem = (ysem, gsem)[which].at[self.slot + b]
            if self.large:
                dst = (large_made, large_back)[which]
                return pltpu.make_async_copy(
                    stage.at[self.at(b * half, half)], dst.at[self.i, pl.ds(b * half, half)], sem
                )
            src = (raw_a, raw_b)[which]
            dst = (small_made, small_back)[which]
            return pltpu.make_async_copy(src.at[self.i], dst.at[self.i], sem)

    units = 2 * n

    def unit_at(which):
        return (which + core) % 2, which // 2

    def forward(unit, step):
        @pl.when(place == 0)
        def _():
            if unit.large:
                large_copy(large_images, xin, isem, unit.i).wait()
            else:
                small_copy(small_images, raw_a, isem, unit.i).wait()
                xin[unit.at(0, pp)] = jnp.zeros((pp, d), BF16)
                xin[unit.at(0, ps)] = raw_a[unit.i]

        def norm_one(r):
            rows = unit.at(r * unit.some, unit.some)
            x = xin[rows].astype(F32)
            x = x - jnp.mean(x, axis=1, keepdims=True)
            s = lax.rsqrt(jnp.mean(x * x, axis=1, keepdims=True) + EPSILON)
            n1[rows] = (x * s * gains[0:1] + shifts[0:1]).astype(BF16)

        steps = unit.size // unit.some
        for b in range(unit.blocks):

            @pl.when(place > 0)
            def _(b=b):
                ahead_copy(unit.base + b * unit.size, unit.size, unit.slot + b).wait_recv()

            for r in range(b * steps, (b + 1) * steps):
                norm_one(r)
        rows = unit.at(0, unit.rows)
        keep_one = unit.keep(0)
        keep_two = unit.keep(1)
        for c in range(0, d, COLS):
            pre = mm(unit.gin_t[...], n1[rows, c : c + COLS], 1, 0) + unit.bcol[:, 0:1]
            act, slp = gelu_pair(pre)
            h1[unit.heads, c : c + COLS] = act.astype(BF16)
            sl1[unit.heads, c : c + COLS] = slp.astype(BF16)
        for c in range(0, d, COLS):
            branch = mm(unit.gout_t[...], h1[unit.heads, c : c + COLS], 1, 0) + unit.scol[:, 0:1]
            mid[0 : unit.rows, c : c + COLS] = xin[rows, c : c + COLS].astype(F32) + keep_one * branch

        def norm_two(r):
            rows = unit.at(r * unit.some, unit.some)
            x = mid[r * unit.some : (r + 1) * unit.some]
            x = x - jnp.mean(x, axis=1, keepdims=True)
            s = lax.rsqrt(jnp.mean(x * x, axis=1, keepdims=True) + EPSILON)
            x = x * s
            u2[rows] = x.astype(BF16)
            r2[rows] = jnp.broadcast_to(s, (unit.some, 128))
            n2[rows] = (x * gains[1:2] + shifts[1:2]).astype(BF16)

        for r in range(unit.rows // unit.some):
            norm_two(r)

        @pl.when(step == 0)
        def _():
            for c in copies[4:]:
                c.wait()

        for b in range(unit.blocks):
            size = unit.size
            rows = unit.at(b * size, size)
            here = slice(b * size, (b + 1) * size)
            total = channel_shift[...]
            parts = [slice(c, c + COLS) for c in range(0, dc, COLS)]
            ahead_of = mm(n2[rows], win[:, parts[0]], 1, 0)
            acts = []
            for c, cols in enumerate(parts):
                pre = ahead_of + channel_bias[:, cols]
                if c + 1 < len(parts):
                    ahead_of = mm(n2[rows], win[:, parts[c + 1]], 1, 0)
                act, slp = gelu_pair(pre)
                acts.append(act.astype(BF16))
                hid[rows, cols] = acts[-1]
                slope[rows, cols] = slp.astype(BF16)
                if cols.stop % WIDE == 0:
                    total = total + mm(jnp.concatenate(acts, axis=1), wout[cols.stop - WIDE : cols.stop, :], 1, 0)
                    acts = []
            y = (mid[here] + keep_two * total).astype(BF16)
            stage[rows] = y
            if not unit.large:
                raw_a[unit.i] = y[0:ps]

            if b == 0:

                @pl.when(step == 0)
                def _():
                    pl.semaphore_wait(barrier, peers)

            @pl.when(place < sections - 1)
            def _(b=b, size=size):
                ahead_copy(unit.base + b * size, size, unit.slot + b).start()

            if unit.large or not fused:
                unit.out_copy(0, b).start()

    def backward(unit):
        @pl.when(last == 1)
        def _():
            if unit.large:
                large_copy(large_upstream, up, usem, unit.i).wait()
            elif not fused:
                small_copy(small_upstream, raw_b, usem, unit.i).wait()
                up[unit.at(0, pp)] = jnp.zeros((pp, d), BF16)
                up[unit.at(0, ps)] = raw_b[unit.i]

        keep_one = unit.keep(0)
        keep_two = unit.keep(1)
        size = unit.size
        for b in range(unit.blocks):
            rows = unit.at(b * size, size)
            here = slice(b * size, (b + 1) * size)

            @pl.when(place < sections - 1)
            def _(b=b):
                ahead_copy(unit.base + b * size, size, unit.slot + b).wait_send()

            if unit.large or not fused:
                unit.out_copy(0, b).wait()

            @pl.when(last == 0)
            def _(b=b):
                behind_copy(unit.base + b * size, size, unit.slot + b).wait_recv()

            stage[rows] = up[rows] * keep_two.astype(BF16)

            parts = [slice(c, c + COLS) for c in range(0, dc, COLS)]
            total = None
            ahead_of = mm(stage[rows], wout[parts[0], :], 1, 1)
            grads = []
            for c, cols in enumerate(parts):
                grad = ahead_of
                if c + 1 < len(parts):
                    ahead_of = mm(stage[rows], wout[parts[c + 1], :], 1, 1)
                grads.append((grad * slope[rows, cols].astype(F32)).astype(BF16))
                slope[rows, cols] = grads[-1]
                if cols.stop % WIDE == 0:
                    term = mm(jnp.concatenate(grads, axis=1), win[:, cols.stop - WIDE : cols.stop], 1, 1)
                    total = term if total is None else total + term
                    grads = []
            acc[here] = total

        def norm_two(r):
            offset = r * unit.some
            rows = unit.at(offset, unit.some)
            local = slice(offset, offset + unit.some)
            h = acc[local]
            u = u2[rows].astype(F32)
            s = r2[rows][:, 0:1]
            g = up[rows].astype(F32)
            q = h * gains[1:2]
            first = jnp.mean(q, axis=1, keepdims=True)
            second = jnp.mean(q * u, axis=1, keepdims=True)
            g_mid = g + s * (q - first - u * second)
            mid[local] = g_mid
            gb1[rows] = (keep_one * g_mid).astype(BF16)
            up[rows] = (keep_two * g).astype(BF16)
            return groups(h * u), groups(h)

        parts = [norm_two(r) for r in range(unit.rows // unit.some)]
        sums[8:16, 0:d] += sum(p[0] for p in parts)
        sums[24:32, 0:d] += sum(p[1] for p in parts)
        rows = unit.at(0, unit.rows)
        for c in range(0, d, COLS):
            grad = mm(unit.gout[...], gb1[rows, c : c + COLS], 1, 0)
            grad = (grad * sl1[unit.heads, c : c + COLS].astype(F32)).astype(BF16)
            sl1[unit.heads, c : c + COLS] = grad
        for c in range(0, d, COLS):
            acc[0 : unit.rows, c : c + COLS] = mm(unit.gin[...], sl1[unit.heads, c : c + COLS], 1, 0)

        def norm_one(r):
            offset = r * unit.some
            rows = unit.at(offset, unit.some)
            local = slice(offset, offset + unit.some)
            x = xin[rows].astype(F32)
            x = x - jnp.mean(x, axis=1, keepdims=True)
            s = lax.rsqrt(jnp.mean(x * x, axis=1, keepdims=True) + EPSILON)
            u = x * s
            h = acc[local]
            q = h * gains[0:1]
            first = jnp.mean(q, axis=1, keepdims=True)
            second = jnp.mean(q * u, axis=1, keepdims=True)
            stage[rows] = (mid[local] + s * (q - first - u * second)).astype(BF16)
            return groups(h * u), groups(h)

        steps = size // unit.some
        for b in range(unit.blocks):
            parts = [norm_one(r) for r in range(b * steps, (b + 1) * steps)]
            sums[0:8, 0:d] += sum(p[0] for p in parts)
            sums[16:24, 0:d] += sum(p[1] for p in parts)
            if not unit.large:
                raw_b[unit.i] = stage[unit.at(0, ps)]

            @pl.when(place > 0)
            def _(b=b):
                behind_copy(unit.base + b * size, size, unit.slot + b).start()

            if unit.large or not fused:
                unit.out_copy(1, b).start()

    piece = d // dp
    tok_piece = ds_ // dp

    def turn(src):
        def some(rows, size):
            value = jnp.transpose(src[pl.ds(rows, size)])
            if not fused:
                turned[:, pl.ds(rows, size)] = value
                return
            for b in range(dp):
                at = ((b % 2) * line + b // 2) * piece
                turned[at : at + piece, pl.ds(rows, size)] = value[b * piece : (b + 1) * piece]

        def full(r, carry):
            some(pl.multiple_of(r * 128, 128), 128)
            return carry

        whole = src.shape[0] // 128
        lax.fori_loop(0, whole, full, 0)
        if src.shape[0] % 128:
            some(whole * 128, src.shape[0] % 128)


    def step(t, carry):
        back = (1 - last) * (t // units) + last * (t % 2)
        which = (1 - last) * (t % units) + last * (t // 2)
        small, i = unit_at(which)

        @pl.when((t == units) & (last == 0))
        def _():
            prepare_backward()

        @pl.when(t == 2 * units - 1)
        def _():
            turn(n2)

        @pl.when((back == 0) & (small == 0))
        def _():
            forward(Unit(True, i), t)

        @pl.when((back == 0) & (small == 1))
        def _():
            forward(Unit(False, i), t)

        @pl.when((back == 1) & (small == 0))
        def _():
            backward(Unit(True, i))

        @pl.when((back == 1) & (small == 1))
        def _():
            backward(Unit(False, i))

        return carry

    lax.fori_loop(0, 2 * units, step, 0)

    total = hid.shape[0]
    chunks = dc // d
    count = 2 * chunks + 2
    kinds = (chunks, chunks, 1, 1, shared)
    first_of = (0, chunks + 2, chunks, chunks + 1, count + 1)
    large_width, small_width = up_to(pl_, 128), up_to(pp, 128)
    widths = (d, d, large_width, small_width, d)
    own = line
    across = line + 1

    def columns(kind, k):
        if kind < 2:
            return pl.ds(pl.multiple_of(k * d, 128), d)
        return pl.ds(0, widths[kind])

    def own_rows(kind):
        return ((slope, 0), (hid, 0), (up, 0), (up, d))[kind]

    def weight_product(kind, k):
        src = (slope, hid)[kind]

        def part(j, carry):
            cols = pl.ds(pl.multiple_of(k * d + j * COLS, COLS), COLS)
            if kind == 0:
                bias = mm(jnp.ones((8, total), BF16), src[:, cols], 1, 0)[0:1]
                vecs[own, pl.ds(k, 1), pl.ds(pl.multiple_of(j * COLS, COLS), COLS)] = bias
            src[0:d, cols] = mm(turned[...], src[:, cols], 1, 0).astype(BF16)
            return carry

        lax.fori_loop(0, d // COLS, part, 0)

    def token_product(large):
        unit_rows = pl_ if large else pp
        ones_d = jnp.ones((8, d), BF16)
        out_grad = in_grad = bias = shift = None
        for k in range(n):
            base = k * pl_ if large else first_rows + k * pp
            head = k * ds_ if large else (n + k) * ds_
            g = gb1[base : base + unit_rows]
            x = n1[base : base + unit_rows]
            h = h1[head : head + ds_]
            p = sl1[head : head + ds_]
            terms = (mm(p, x, 1, 1), mm(h, g, 1, 1), mm(ones_d, p, 1, 1), mm(ones_d, g, 1, 1))
            if k == 0:
                in_grad, out_grad, bias, shift = terms
            else:
                in_grad, out_grad, bias, shift = in_grad + terms[0], out_grad + terms[1], bias + terms[2], shift + terms[3]
        src, base = own_rows(2 if large else 3)
        for at, value in ((0, in_grad), (1, out_grad)):
            value = value.astype(BF16)
            if not fused:
                src[base + at * ds_ : base + (at + 1) * ds_, 0:unit_rows] = value
                continue
            for b in range(dp):
                to = base + ((b % 2) * line + b // 2) * piece + at * tok_piece
                src[to : to + tok_piece, 0:unit_rows] = value[b * tok_piece : (b + 1) * tok_piece]
        row = chunks + 5 + (0 if large else 2)
        vecs[own, row : row + 1, 0:ds_] = bias[0:1]
        vecs[own, row + 1 : row + 2, 0:unit_rows] = shift[0:1]

    def product(kind, k):
        if kind == 2:
            turn(up)
            vecs[own, chunks : chunks + 1] = mm(jnp.ones((8, total), BF16), up[...], 1, 0)[0:1]
            for j in range(4):
                vecs[own, chunks + 1 + j : chunks + 2 + j] = jnp.sum(sums[8 * j : 8 * j + 8], axis=0, keepdims=True)
        if kind < 2:
            weight_product(kind, k)
        else:
            token_product(kind == 2)

    def ways(step_of, kept=False):
        def at(c, valid=True):
            for kind in range(5 if fused else 4):
                low, high = first_of[kind], first_of[kind] + kinds[kind]
                here = (c >= low) & (c < high) & valid
                if kind == 4:
                    here = here & taker & (c < low + foreign)
                if kind == 0 and kept:
                    here = here & ((place >= sections // 2) | (c % 2 == 0))

                @pl.when(here)
                def _(kind=kind, low=low):
                    step_of(kind, c - low)

        return at

    vecs[own] = jnp.zeros(vecs.shape[1:], F32)
    if not fused:

        def whole_copies(kind, k):
            src, base = own_rows(kind)
            if kind < 2:
                cols = columns(kind, k)
                dst = (chan_a, chan_b)[kind]
                return [pltpu.make_async_copy(src.at[pl.ds(0, d), cols], dst.at[:, cols], outsem.at[first_of[kind] + k])]
            cols = pl.ds(0, widths[kind])
            dst = (tok_l, tok_s)[kind - 2]
            return [pltpu.make_async_copy(src.at[pl.ds(base, d), cols], dst, outsem.at[first_of[kind]])]

        def one(kind, k):
            product(kind, k)
            for c in whole_copies(kind, k):
                c.start()

        def finish(kind, k):
            for c in whole_copies(kind, k):
                c.wait()

        def run(c, carry):
            ways(one)(c)
            return carry

        def end(c, carry):
            ways(finish)(c)
            return carry

        lax.fori_loop(0, count, run, 0)
        lax.fori_loop(0, count, end, 0)
        vec_out[...] = vecs[own]
    else:
        rightward, leftward = (rank + 2) % dp, (rank + dp - 2) % dp

        def mine(kind, k, to):
            if kind == 4:
                return h1.at[pl.ds(pl.multiple_of((k * line + to) * piece, 16), piece)]
            src, base = own_rows(kind)
            return src.at[pl.ds(pl.multiple_of(base + (core * line + to) * piece, 16), piece), columns(kind, k)]

        def crossing(kind, k, rows, size):
            ref, base = ((win, 0), (win, d // 2), (wout, 3 * d), (wout, 3 * d + d // 2))[kind]
            return ref.at[pl.ds(pl.multiple_of(base + rows, 16), size), columns(kind, k)]

        def from_left(kind, k, to):
            ref, base = ((wout, 0), (wout, chunks * (line - 1)), (n2, 0), (n2, line - 1), (sl1, 0))[kind]
            rows = (base + k * (line - 1) + to - 1) * piece
            return ref.at[pl.ds(pl.multiple_of(rows, 16), piece), pl.ds(0, widths[kind])]

        def from_right(kind, k, to):
            ref, base = ((xin, 0), (u2, 0), (n2, 2 * (line - 1)), (n2, 3 * (line - 1)), (sl1, shared * (line - 1)))[kind]
            rows = (base + k * (line - 1) + to) * piece
            return ref.at[pl.ds(pl.multiple_of(rows, 16), piece), pl.ds(0, widths[kind])]

        def sem_of(kind, k, to):
            return ((count if kind == 4 else first_of[kind]) + k) * line + to

        def cross_copy(kind, k):
            src, base = own_rows(kind)
            rows = pl.ds(pl.multiple_of(base + (1 - core) * line * piece, 16), line * piece)
            c = first_of[kind] + k
            return pltpu.make_async_remote_copy(
                src_ref=src.at[rows, columns(kind, k)],
                dst_ref=crossing(kind, k, 0, line * piece),
                send_sem=sibs.at[0, c],
                recv_sem=sibs.at[1, c],
                device_id={"dp": sibling},
                device_id_type=MESH,
            )

        def right_copy(kind, k, to):
            return pltpu.make_async_remote_copy(
                src_ref=mine(kind, k, to),
                dst_ref=from_left(kind, k, to),
                send_sem=rights.at[0, sem_of(kind, k, to)],
                recv_sem=rights.at[1, sem_of(kind, k, to)],
                device_id={"dp": rightward},
                device_id_type=MESH,
            )

        def left_copy(kind, k, to):
            return pltpu.make_async_remote_copy(
                src_ref=mine(kind, k, to),
                dst_ref=from_right(kind, k, to),
                send_sem=lefts.at[0, sem_of(kind, k, to)],
                recv_sem=lefts.at[1, sem_of(kind, k, to)],
                device_id={"dp": leftward},
                device_id_type=MESH,
            )

        def chip_sum(kind, k, to):
            if kind == 4:
                return mine(kind, k, to)[...].astype(F32)
            return mine(kind, k, to)[...].astype(F32) + crossing(kind, k, to * piece, piece)[...].astype(F32)

        def flow_right(kind, k):
            def one(j, carry):
                to = line - 1 - j

                @pl.when(z == 0)
                def _():
                    mine(kind, k, to)[...] = chip_sum(kind, k, to).astype(BF16)

                @pl.when(z > 0)
                def _():
                    right_copy(kind, k, to).wait_recv()
                    value = chip_sum(kind, k, to) + from_left(kind, k, to)[...].astype(F32)
                    mine(kind, k, to)[...] = value.astype(BF16)

                right_copy(kind, k, to).start()
                return carry

            lax.fori_loop(0, line - 1 - z, one, 0)

        def flow_left(kind, k):
            def one(to, carry):
                @pl.when(z == line - 1)
                def _():
                    mine(kind, k, to)[...] = chip_sum(kind, k, to).astype(BF16)

                @pl.when(z < line - 1)
                def _():
                    left_copy(kind, k, to).wait_recv()
                    value = chip_sum(kind, k, to) + from_right(kind, k, to)[...].astype(F32)
                    mine(kind, k, to)[...] = value.astype(BF16)

                left_copy(kind, k, to).start()
                return carry

            lax.fori_loop(0, z, one, 0)

        def out_stage(kind, k):
            if kind == 0:
                return mid.at[pl.ds(pl.multiple_of(k * piece, 16), piece)]
            if kind in (1, 4):
                at = k + (chunks if kind == 4 else 0)
                return acc.at[pl.ds(pl.multiple_of(at * piece, 16), piece)]
            return (tl, ts)[kind - 2]

        def out_copies(kind, k):
            c = first_of[kind] + k
            if kind < 2:
                dst = (chan_a, chan_b)[kind].at[:, columns(kind, k)]
            else:
                dst = (tok_l, tok_s)[kind - 2]
            return pltpu.make_async_copy(out_stage(kind, k), dst, outsem.at[c])

        def gather(kind, k):
            width = (d, d, pl_, ps, d)[kind]
            dst = out_stage(kind, k)
            dst[...] = chip_sum(kind, k, z)[:, 0:width]

            @pl.when(z > 0)
            def _():
                right_copy(kind, k, z).wait_recv()
                dst[...] += from_left(kind, k, z)[...].astype(F32)[:, 0:width]

            @pl.when(z < line - 1)
            def _():
                left_copy(kind, k, z).wait_recv()
                dst[...] += from_right(kind, k, z)[...].astype(F32)[:, 0:width]

            if kind == 4:
                give_back(k).start()
            else:
                out_copies(kind, k).start()

        def lend_copy(j, f, to):
            rows = pl.ds(pl.multiple_of(core * line * piece, 16), line * piece)
            return pltpu.make_async_remote_copy(
                src_ref=slope.at[rows, columns(0, 2 * j + 1)],
                dst_ref=h1.at[pl.ds(pl.multiple_of(f * line * piece, 16), line * piece)],
                send_sem=lent.at[0, j],
                recv_sem=lent.at[1, f],
                device_id={"section": to},
                device_id_type=MESH,
            )

        def return_copy(f, j, to):
            return pltpu.make_async_remote_copy(
                src_ref=out_stage(4, f),
                dst_ref=out_stage(0, 2 * j + 1),
                send_sem=lent.at[2, f],
                recv_sem=lent.at[3, j],
                device_id={"section": to},
                device_id_type=MESH,
            )

        def lend_away(j):
            return lend_copy(j, place * j, (1 - place) * (2 - j) + place * 3)

        def give_back(f):
            return return_copy(f, f + (2 - place) * (1 - last), owner)

        def lend(c):
            @pl.when(giver & (c % 2 == 1) & (c >= 1) & (c < 2 * shared))
            def _():
                @pl.when(c == 1)
                def _():
                    pl.semaphore_wait(ready.at[3], 1)

                @pl.when((c == 3) & (place == 0))
                def _():
                    pl.semaphore_wait(ready.at[6], 1)

                def one(to, carry):
                    mine(0, c, to)[...] = chip_sum(0, c, to).astype(BF16)
                    return carry

                lax.fori_loop(0, line, one, 0)
                lend_away(c // 2).start()

        def pair_copy(which):
            return pltpu.make_async_copy(paired, (small_made, small_back)[which], pairs.at[which])

        def pair(which):
            if which:
                pair_copy(0).wait()
            src = (raw_a, raw_b)[which]
            for r in range(0, ps, 32):
                rows = slice(r, min(r + 32, ps))
                images = [src[j, rows].astype(F32)[:, None, :] for j in range(n)]
                paired[rows] = jnp.concatenate(images, axis=1).astype(BF16)
            pair_copy(which).start()

        def vec_cross():
            return pltpu.make_async_remote_copy(
                src_ref=vecs.at[own],
                dst_ref=vecs.at[across],
                send_sem=vsem.at[0, 0],
                recv_sem=vsem.at[1, 0],
                device_id={"dp": sibling},
                device_id_type=MESH,
            )

        def vec_copy(k):
            return pltpu.make_async_remote_copy(
                src_ref=vecs.at[z],
                dst_ref=vecs.at[z],
                send_sem=vsem.at[0, k],
                recv_sem=vsem.at[1, k],
                device_id={"dp": (rank + 2 * k) % dp},
                device_id_type=MESH,
            )

        def first(kind, k):
            if kind == 4:

                @pl.when(k == 0)
                def _():
                    @pl.when(z < line - 1)
                    def _():
                        pl.semaphore_wait(ready.at[4], 1)

                    @pl.when(z > 0)
                    def _():
                        pl.semaphore_wait(ready.at[5], 1)

                lend_copy(0, k, owner).wait_recv()
                return
            product(kind, k)
            if kind == 3:

                @pl.when(taker)
                def _():
                    for at, here in ((6, place == 1), (3, place > 1)):

                        @pl.when(here)
                        def _(at=at):
                            pl.semaphore_signal(ready.at[at], inc=1, device_id={"section": owner}, device_id_type=MESH)

                    @pl.when(z > 0)
                    def _():
                        pl.semaphore_signal(ready.at[4], inc=1, device_id={"dp": leftward}, device_id_type=MESH)

                    @pl.when(z < line - 1)
                    def _():
                        pl.semaphore_signal(ready.at[5], inc=1, device_id={"dp": rightward}, device_id_type=MESH)

            if kind == 0:

                @pl.when(k == 0)
                def _():
                    pl.semaphore_wait(ready.at[0], 1)

                    @pl.when(z < line - 1)
                    def _():
                        pl.semaphore_wait(ready.at[1], 1)

                    @pl.when(z > 0)
                    def _():
                        pl.semaphore_wait(ready.at[2], 1)

            cross_copy(kind, k).start()

        def crossed(kind, k):
            if kind < 4:
                cross_copy(kind, k).wait_recv()

        def finish(kind, k):
            if kind == 4:
                give_back(k).wait_send()
            else:
                cross_copy(kind, k).wait_send()
                out_copies(kind, k).wait()

            def right(j, carry):
                right_copy(kind, k, line - 1 - j).wait_send()
                return carry

            def left(to, carry):
                left_copy(kind, k, to).wait_send()
                return carry

            sent = line - 1 - z, z
            if kind == 0:
                away = giver & (k % 2 == 1)
                own_line = 1 - away.astype(jnp.int32)
                sent = sent[0] * own_line, sent[1] * own_line
            lax.fori_loop(0, sent[0], right, 0)
            lax.fori_loop(0, sent[1], left, 0)

        pl.semaphore_signal(ready.at[0], inc=1, device_id={"dp": sibling}, device_id_type=MESH)

        @pl.when(z > 0)
        def _():
            pl.semaphore_signal(ready.at[1], inc=1, device_id={"dp": leftward}, device_id_type=MESH)

        @pl.when(z < line - 1)
        def _():
            pl.semaphore_signal(ready.at[2], inc=1, device_id={"dp": rightward}, device_id_type=MESH)

        def run(c, carry):
            ways(crossed)(c - 1)
            lend(c - 1)
            ways(flow_right, True)(c - 1 - z, z < line - 1)
            ways(flow_left, True)(c - line + z, z > 0)
            ways(first)(c)

            @pl.when(c == count)
            def _():
                vec_cross().start()

            @pl.when(c == count + 1)
            def _():
                vec_cross().wait()
                vecs[z] = vecs[own] + vecs[across]
                for k in range(1, line):
                    vec_copy(k).start()

            for which in range(2):

                @pl.when(c == count - 2 + which)
                def _(which=which):
                    pair(which)

            ways(gather, True)(c - line - 1)
            return carry

        steps = count + 1 + shared
        lax.fori_loop(0, steps + line + 1, run, 0)

        @pl.when(giver)
        def _():
            for k in range(shared):
                lend_away(k).wait_send()
                return_copy(0, k, owner).wait_recv()
                out_copies(0, 2 * k + 1).start()

        def end(c, carry):
            ways(finish)(c)
            return carry

        lax.fori_loop(0, steps, end, 0)
        pair_copy(1).wait()
        for k in range(1, line):
            vec_copy(k).wait()
        value = vecs[0]
        for k in range(1, line):
            value = value + vecs[k]
        vec_out[...] = value

    for i in range(2 * n):
        unit = Unit(i < n, i % n)
        for b in range(unit.blocks):
            if unit.large or not fused:
                unit.out_copy(1, b).wait()

            @pl.when(place > 0)
            def _(b=b, unit=unit):
                behind_copy(unit.base + b * unit.size, unit.size, unit.slot + b).wait_send()


def finish_kernel(tok_piece, d, chunks, moved, *refs):
    sources, (tok_l, tok_s, vec), rest = refs[:moved], refs[moved : moved + 3], refs[moved + 3 :]
    outs, vias, sem = rest[: -moved - 1], rest[-moved - 1 : -1], rest[-1]
    bring = [pltpu.make_async_copy(a, b, sem.at[0, k]) for k, (a, b) in enumerate(zip(sources, vias))]
    take = [pltpu.make_async_copy(a, b, sem.at[1, k]) for k, (a, b) in enumerate(zip(vias, outs[:moved]))]
    for c in bring:
        c.start()
    outs = outs[moved:]
    for k, src in enumerate((tok_l, tok_s)):
        outs[2 * k][...] = src[0:tok_piece]
        outs[2 * k + 1][...] = src[tok_piece:]
    for k in range(chunks):
        outs[4][:, k * d : (k + 1) * d] = vec[k : k + 1]
    at = chunks
    for out in outs[5:]:
        rows, width = out.shape
        out[...] = vec[at : at + rows, 0:width]
        at += rows
    for a, b in zip(bring, take):
        a.wait()
        b.start()
    for c in take:
        c.wait()


def local(
    small_images,
    large_images,
    small_upstream,
    large_upstream,
    small_keep,
    large_keep,
    small_in,
    small_bias,
    small_out,
    small_shift,
    large_in,
    large_bias,
    large_out,
    large_shift,
    channel_in,
    channel_bias,
    channel_out,
    channel_shift,
    norm_gain,
    norm_shift,
):
    sections = lax.axis_size("section")
    micro, imgs, ps, d = small_images.shape
    pl_ = large_images.shape[2]
    n = micro * imgs
    ds_ = small_in.shape[2]
    dc = channel_in.shape[2]
    pp = up_to(ps, 16)
    rows = n * (pl_ + pp)
    small_width, large_width = up_to(pp, 128), up_to(pl_, 128)
    dp = lax.axis_size("dp")
    piece, tok_piece = d // dp, ds_ // dp
    fused = d % (16 * dp) == 0 and ds_ % (16 * dp) == 0 and dc == 4 * d and d == 2 * ds_ and 2 * dp * piece <= rows
    fused = fused and sections == 4
    shared = 2
    dims = (sections, n, ps, pl_, pp, d, ds_, dc, dp, fused, shared)
    chunks = dc // d
    line = dp // 2 if fused else 1
    count = 2 * chunks + 2
    vec_rows = up_to(chunks + 9, 8)
    any_ = pl.BlockSpec(memory_space=pl.ANY)
    vmem = pl.BlockSpec(memory_space=pltpu.VMEM)
    smem = pl.BlockSpec(memory_space=pltpu.SMEM)
    block = max(pl_, n * pp)
    blocks = 2 * n + n
    scratch = [
        pltpu.VMEM((d, dc), BF16),
        pltpu.VMEM((dc, d), BF16),
        pltpu.VMEM((rows, dc), BF16),
        pltpu.VMEM((rows, dc), BF16),
        pltpu.VMEM((rows, d), BF16),
        pltpu.VMEM((rows, d), BF16),
        pltpu.VMEM((rows, d), BF16),
        pltpu.VMEM((rows, d), BF16),
        pltpu.VMEM((rows, d), BF16),
        pltpu.VMEM((rows, 128), F32),
        pltpu.VMEM((rows, d), BF16),
        pltpu.VMEM((rows, d), BF16),
        pltpu.VMEM((2 * n * ds_, d), BF16),
        pltpu.VMEM((2 * n * ds_, d), BF16),
        pltpu.VMEM((pl_, ds_), BF16),
        pltpu.VMEM((ds_, pl_), BF16),
        pltpu.VMEM((ds_, pl_), BF16),
        pltpu.VMEM((pl_, ds_), BF16),
        pltpu.VMEM((pp, ds_), BF16),
        pltpu.VMEM((ds_, pp), BF16),
        pltpu.VMEM((ds_, pp), BF16),
        pltpu.VMEM((pp, ds_), BF16),
        pltpu.VMEM((d, rows), BF16),
        pltpu.VMEM((ds_, 128), F32),
        pltpu.VMEM((pl_, 128), F32),
        pltpu.VMEM((ds_, 128), F32),
        pltpu.VMEM((pp, 128), F32),
        pltpu.VMEM((block, d), F32),
        pltpu.VMEM((block, d), F32),
        pltpu.VMEM((n, ps, d), BF16),
        pltpu.VMEM((n, ps, d), BF16),
        pltpu.VMEM((32, d), F32),
        pltpu.SemaphoreType.DMA((6,)),
        pltpu.SemaphoreType.DMA((2 * n,)),
        pltpu.SemaphoreType.DMA((2 * n,)),
        pltpu.SemaphoreType.DMA((blocks,)),
        pltpu.SemaphoreType.DMA((blocks,)),
        pltpu.SemaphoreType.DMA((blocks,)),
        pltpu.SemaphoreType.DMA((blocks,)),
        pltpu.SemaphoreType.DMA((blocks,)),
        pltpu.SemaphoreType.DMA((blocks,)),
        pltpu.SemaphoreType.DMA((2, count)),
        pltpu.SemaphoreType.DMA((2, (count + shared) * line)),
        pltpu.SemaphoreType.DMA((2, (count + shared) * line)),
        pltpu.SemaphoreType.DMA((count,)),
        pltpu.SemaphoreType.DMA((2, line)),
        pltpu.SemaphoreType.REGULAR((7,)),
        pltpu.SemaphoreType.DMA((4, shared)),
        pltpu.VMEM((2 * tok_piece, pl_), F32),
        pltpu.VMEM((2 * tok_piece, ps), F32),
        pltpu.VMEM((line + 2, vec_rows, d), F32),
        pltpu.VMEM((ps, n, d) if fused else (8, 128), BF16),
        pltpu.SemaphoreType.DMA((2,)),
    ]
    if fused:
        reduced = (
            jax.ShapeDtypeStruct((piece, dc), F32),
            jax.ShapeDtypeStruct((piece, dc), F32),
            jax.ShapeDtypeStruct((2 * tok_piece, pl_), F32),
            jax.ShapeDtypeStruct((2 * tok_piece, ps), F32),
        )
    else:
        reduced = (
            jax.ShapeDtypeStruct((d, dc), BF16),
            jax.ShapeDtypeStruct((d, dc), BF16),
            jax.ShapeDtypeStruct((d, large_width), BF16),
            jax.ShapeDtypeStruct((d, small_width), BF16),
        )
    small_shape = (ps, n, d) if fused else (n, ps, d)
    outs = (
        jax.ShapeDtypeStruct(small_shape, BF16),
        jax.ShapeDtypeStruct((n, pl_, d), BF16),
        jax.ShapeDtypeStruct(small_shape, BF16),
        jax.ShapeDtypeStruct((n, pl_, d), BF16),
        *reduced,
        jax.ShapeDtypeStruct((vec_rows, d), F32),
    )
    made_s, made_l, back_s, back_l, chan_a, chan_b, tok_l, tok_s, vec = pl.pallas_call(
        functools.partial(kernel, dims),
        out_shape=outs,
        in_specs=[any_] * 4
        + [smem] * 2
        + [any_, vmem, any_, vmem] * 2
        + [any_, vmem, any_, vmem]
        + [vmem, vmem],
        out_specs=(any_,) * 8 + (vmem,),
        scratch_shapes=scratch,
        compiler_params=pltpu.CompilerParams(
            collective_id=0, has_side_effects=True, vmem_limit_bytes=65400 * 1024
        ),
        cost_estimate=pl.CostEstimate(flops=50 * 10**9, bytes_accessed=40 * 10**6, transcendentals=10**7),
    )(
        small_images.reshape(n, ps, d),
        large_images.reshape(n, pl_, d),
        small_upstream.reshape(n, ps, d).transpose(1, 0, 2) if fused else small_upstream.reshape(n, ps, d),
        large_upstream.reshape(n, pl_, d),
        small_keep.reshape(n, 2),
        large_keep.reshape(n, 2),
        small_in[0],
        small_bias,
        small_out[0].T,
        small_shift,
        large_in[0],
        large_bias,
        large_out[0].T,
        large_shift,
        channel_in[0],
        channel_bias,
        channel_out[0],
        channel_shift,
        norm_gain[0],
        norm_shift[0],
    )
    if fused:
        large = (made_l, back_l, chan_a, chan_b, made_s, back_s)
        final = [jax.ShapeDtypeStruct(x.shape, x.dtype) for x in large]
        final += [jax.ShapeDtypeStruct((tok_piece, width), F32) for width in (pl_, pl_, ps, ps)]
        final += [
            jax.ShapeDtypeStruct(shape, F32)
            for shape in ((1, dc), (1, d), (2, d), (2, d), (1, ds_), (1, pl_), (1, ds_), (1, ps))
        ]
        made_l, back_l, chan_a, chan_b, made_s, back_s, lin, lout, sin, sout, *vecs = pl.pallas_call(
            functools.partial(finish_kernel, tok_piece, d, chunks, len(large)),
            out_shape=final,
            in_specs=[any_] * len(large) + [vmem] * 3,
            out_specs=[any_] * len(large) + [vmem] * 12,
            scratch_shapes=[pltpu.VMEM(x.shape, x.dtype) for x in large] + [pltpu.SemaphoreType.DMA((2, len(large)))],
            compiler_params=pltpu.CompilerParams(vmem_limit_bytes=65400 * 1024),
        )(*large, tok_l, tok_s, vec)
        cbias, cshift, gain, shift, lbias, lshift, sbias, sshift = vecs
        made_s, back_s = (x.transpose(1, 0, 2) for x in (made_s, back_s))
    else:
        chan_a, chan_b = (lax.psum_scatter(x, "dp", scatter_dimension=0, tiled=True).astype(F32) for x in (chan_a, chan_b))
        tok = jnp.concatenate([tok_l, tok_s], axis=1).reshape(2, ds_, large_width + small_width)
        tok = lax.psum_scatter(tok, "dp", scatter_dimension=1, tiled=True).astype(F32)
        lin, lout, sin, sout = tok[0, :, 0:pl_], tok[1, :, 0:pl_], tok[0, :, large_width:], tok[1, :, large_width:]
        sin, sout = sin[:, 0:ps], sout[:, 0:ps]
        vec = lax.psum(vec, "dp")
        at = chunks
        cbias, cshift = vec[0:at].reshape(1, dc), vec[at : at + 1]
        gain, shift = vec[at + 1 : at + 3], vec[at + 3 : at + 5]
        lbias, lshift = vec[at + 5 : at + 6, 0:ds_], vec[at + 6 : at + 7, 0:pl_]
        sbias, sshift = vec[at + 7 : at + 8, 0:ds_], vec[at + 8 : at + 9, 0:ps]
    return (
        made_s.reshape(1, micro, imgs, ps, d),
        made_l.reshape(1, micro, imgs, pl_, d),
        back_s.reshape(1, micro, imgs, ps, d),
        back_l.reshape(1, micro, imgs, pl_, d),
        sin.T[None],
        sbias,
        sout[None],
        sshift,
        lin.T[None],
        lbias,
        lout[None],
        lshift,
        chan_a[None],
        cbias,
        chan_b.T[None],
        cshift,
        gain[None],
        shift[None],
    )


def solution(mesh):
    placed = (
        (P(None, "dp", None, None),) * 4
        + (P("section", None, "dp", None),) * 2
        + (P("section", None, None), P("section", None)) * 6
        + (P("section", None, None),) * 2
    )
    outs = (
        (P("section", None, "dp", None, None),) * 4
        + (P("section", None, "dp"), P("section", None), P("section", "dp", None), P("section", None)) * 2
        + (P("section", "dp", None), P("section", None), P("section", None, "dp"), P("section", None))
        + (P("section", None, None),) * 2
    )
    return jax.shard_map(local, mesh=mesh, in_specs=placed, out_specs=outs, check_vma=False)
```
